32 devices in a mesh: parts: 2 (over y), gx: 4 (over z), gy: 4 (over x, core).
Axes of the slice: x: 2, y: 2, z: 4, core: 2. Of those that a mesh axis runs over, the one named last changes fastest.
Arguments:
- cell_x: int32 [131072], P(('parts', 'gx', 'gy')), parts along dimension 0, may hold values from 0 to 63
- cell_y: int32 [131072], P(('parts', 'gx', 'gy')), parts along dimension 0, may hold values from 0 to 63
- cell_z: int32 [131072], P(('parts', 'gx', 'gy')), parts along dimension 0, may hold values from 0 to 255
- fraction: float32 [3, 131072], P(None, ('parts', 'gx', 'gy')), parts along dimension 1, may hold values from 0 to 1
- charge: float32 [131072], P(('parts', 'gx', 'gy')), parts along dimension 0, may hold values from -6 to 6
Outputs:
- charge_potential: float32 [131072], P(('parts', 'gx', 'gy')), parts along dimension 0
- forces: float32 [3, 131072], P(None, ('parts', 'gx', 'gy')), parts along dimension 1
The draws below stay inside these ranges and needn't reach their ends.
There are 2 independent parts, one for each index of `parts`. The reference program is written for one: setup_inputs(seed, part) draws one part's arguments, and reference() takes and returns one part's arrays. A program takes and returns all parts, laid end to end along the dimension named above; each array names one. Nothing has to cross between parts.
Inputs may be any that keep to these rules, and one draw needn't show every extreme that they name: `cell_x`: a charge's cell along the first dimension, local to its device. `cell_y`: a charge's cell along the second dimension, local to its device.
All inputs are finite; a program needn't handle non-finite values.
Results may differ from the reference program's by a relative error of at most 0.0003.
Values sent between devices are 32-bit elements; how exact they have to be, the bound alone decides.
No kernel may reach another device: no remote copies, remote signals or barrier semaphores. Data moves between devices by JAX's collectives and lax.ppermute only.
A program may use at most 384 MiB of HBM per device.

```python
import jax
import jax.numpy as jnp
from jax import lax

N = 256
NCH_DEV = 4096
XLOC = 64
YLOC = 64
CHARGES = 65536
N_GY = 4


def plant(result, own_key, smallest, largest):
    spot = [jax.random.randint(jax.random.fold_in(own_key, axis), (), 0, length) for axis, length in enumerate(result.shape)]
    main_axis = result.shape.index(max(result.shape))
    neighbour = spot[:main_axis] + [(spot[main_axis] + 1) % result.shape[main_axis]] + spot[main_axis + 1:]
    return result.at[tuple(spot)].set(smallest).at[tuple(neighbour)].set(largest)


def block_scale(own_key, extent, pieces, least, top_value):
    def one(position, shards_of):
        draws = jax.random.uniform(jax.random.fold_in(jax.random.fold_in(own_key, 6), position), (shards_of,), jnp.float32, least / len(pieces), top_value / len(pieces))
        return jnp.repeat(jnp.exp(draws), extent[position] // shards_of).reshape((-1,) + (1,) * (len(extent) - position - 1))

    factor_of = one(*pieces[0])
    for cut in pieces[1:]:
        factor_of = factor_of * one(*cut)
    return factor_of


def bell_draw(stream_key, dims, scale, most, split=(), kind=jnp.bfloat16):
    entries = scale * jax.random.normal(stream_key, dims, jnp.float32)
    if split:
        entries = entries * block_scale(stream_key, dims, split, -0.22, 0.18)
    return jnp.clip(entries, -most, most).astype(kind)


def setup_inputs(seed: int = 0, part: int = 0) -> dict:
    streams_of = jax.random.split(jax.random.key(seed), 6)
    part_keys = jax.random.split(jax.random.fold_in(streams_of[5], part), 6)
    cell_x = plant(jax.random.randint(part_keys[0], (CHARGES,), 0, XLOC), jax.random.fold_in(part_keys[0], 1), 0, XLOC - 1).astype(jnp.int32)
    cell_y = plant(jax.random.randint(part_keys[1], (CHARGES,), 0, YLOC), jax.random.fold_in(part_keys[1], 1), 0, YLOC - 1).astype(jnp.int32)
    cell_z = plant(jax.random.randint(part_keys[2], (CHARGES,), 0, N), jax.random.fold_in(part_keys[2], 1), 0, N - 1).astype(jnp.int32)
    fraction = jnp.clip(1.0 * jax.random.uniform(part_keys[3], (3, CHARGES), jnp.float32) ** block_scale(part_keys[3], (3, CHARGES), ((1, 16),), -0.2, 0.2), 0.0, 1.0)
    charge = bell_draw(part_keys[4], (CHARGES,), 1.0, 6.0, ((0, 16),), jnp.float32)
    return {"cell_x": cell_x, "cell_y": cell_y, "cell_z": cell_z, "fraction": fraction, "charge": charge}


def transform_table(size):
    index = jnp.arange(size, dtype=jnp.int32)
    product = (index[:, None] * index[None, :]) % size
    angle = product.astype(jnp.float32) * (2.0 * jnp.pi / size)
    return jnp.cos(angle) + jnp.sin(angle)


def spline(param):
    rest = 1.0 - param
    square = param * param
    cube = square * param
    weights = jnp.stack([rest * rest * rest / 6.0, (3.0 * cube - 6.0 * square + 4.0) / 6.0,
                         (-3.0 * cube + 3.0 * square + 3.0 * param + 1.0) / 6.0, cube / 6.0], axis=1)
    slopes = jnp.stack([-rest * rest / 2.0, 1.5 * square - 2.0 * param,
                        -1.5 * square + param + 0.5, square / 2.0], axis=1)
    return weights, slopes


def symbol(size):
    index = jnp.arange(size, dtype=jnp.int32).astype(jnp.float32)
    sines = 2.0 * jnp.sin(jnp.pi * index / size)
    return sines * sines


def apply_all(field, table):
    high = lax.Precision.HIGHEST
    field = jnp.einsum('ax,xyz->ayz', table, field, precision=high)
    field = jnp.einsum('by,xyz->xbz', table, field, precision=high)
    field = jnp.einsum('cz,xyz->xyc', table, field, precision=high)
    return field


def reference(cell_x, cell_y, cell_z, fraction, charge):
    count = charge.shape[0]
    device = jnp.arange(count, dtype=jnp.int32) // NCH_DEV
    along_x = device // N_GY
    along_y = device % N_GY
    offsets = jnp.arange(4, dtype=jnp.int32)
    index_x = (along_x * XLOC + cell_x - 1)[:, None] + offsets[None, :]
    index_y = (along_y * YLOC + cell_y - 1)[:, None] + offsets[None, :]
    index_z = (cell_z - 1)[:, None] + offsets[None, :]
    index_x = index_x % N
    index_y = index_y % N
    index_z = index_z % N
    flat = (index_x[:, :, None, None] * N + index_y[:, None, :, None]) * N + index_z[:, None, None, :]
    flat = flat.reshape(count, 64)
    weight_x, slope_x = spline(fraction[0])
    weight_y, slope_y = spline(fraction[1])
    weight_z, slope_z = spline(fraction[2])
    values = charge[:, None, None, None] * weight_x[:, :, None, None] * weight_y[:, None, :, None] * weight_z[:, None, None, :]
    density = jax.ops.segment_sum(values.reshape(-1), flat.reshape(-1), N * N * N).reshape(N, N, N)
    table = transform_table(N)
    spectrum = apply_all(density, table)
    scale = symbol(N)
    total = scale[:, None, None] + scale[None, :, None] + scale[None, None, :]
    safe = jnp.where(total > 0, total, jnp.float32(1.0))
    green = jnp.where(total > 0, jnp.exp(-0.5 * total) / safe, jnp.float32(0.0)) / float(N * N * N)
    potential = apply_all(spectrum * green, table)
    sampled = potential.reshape(-1)[flat].reshape(count, 4, 4, 4)

    def contract(first, second, third):
        return jnp.sum(sampled * first[:, :, None, None] * second[:, None, :, None] * third[:, None, None, :], axis=(1, 2, 3))

    value = contract(weight_x, weight_y, weight_z)
    grad_x = contract(slope_x, weight_y, weight_z)
    grad_y = contract(weight_x, slope_y, weight_z)
    grad_z = contract(weight_x, weight_y, slope_z)
    forces = -charge[None, :] * jnp.stack([grad_x, grad_y, grad_z], axis=0)
    return charge * value, forces
```

```python
import functools

import jax
import jax.numpy as jnp
import numpy as np
from jax import lax
from jax.experimental import pallas as pl
from jax.experimental.pallas import tpu as pltpu
from jax.sharding import PartitionSpec as P

N = 256
LANES = 128
ROWS = 16
PLANES = 8
PAD = 16
F32 = jnp.float32
BF16 = jnp.bfloat16

SIN_PI = (3.141592640130707, -5.167710083507877, 2.550077523214437, -0.5982912856197345, 0.07765766030450941)
COS_PI = (
    0.9999999997799038,
    -4.934802137078749,
    4.058709159554242,
    -1.335212003029471,
    0.23493731372678894,
    -0.024396324214549327,
)


def poly(coefficients, x):
    result = coefficients[-1]
    for value in coefficients[-2::-1]:
        result = result * x + F32(value)
    return result


def spline(param):
    rest = 1.0 - param
    square = param * param
    cube = square * param
    return [
        rest * rest * rest * F32(1 / 6),
        (3.0 * cube - 6.0 * square + 4.0) * F32(1 / 6),
        (-3.0 * cube + 3.0 * square + 3.0 * param + 1.0) * F32(1 / 6),
        cube * F32(1 / 6),
    ]


def slopes(param):
    rest = 1.0 - param
    square = param * param
    return [
        rest * rest * F32(-0.5),
        1.5 * square - 2.0 * param,
        -1.5 * square + param + 0.5,
        square * F32(0.5),
    ]


def split(value):
    high = value.astype(BF16)
    return high, (value - high.astype(F32)).astype(BF16)


def wide(row, rows):
    return jnp.broadcast_to(row, (rows, row.shape[1]))


def pick(offset, options):
    result = jnp.zeros(offset.shape, F32)
    for i in (3, 2, 1, 0):
        result = jnp.where(offset == F32(i), wide(options[i], offset.shape[0]), result)
    return result


def iota(rows):
    return lax.broadcasted_iota(jnp.int32, (rows, LANES), 0).astype(F32)


def rotation(tab, row_y):
    turn = tab[0] * wide(row_y, ROWS)
    turn = turn - jnp.round(turn)
    square = turn * turn
    sine = turn * poly(SIN_PI, square)
    cosine = poly(COS_PI, square)
    full_cos = 1.0 - 2.0 * sine * sine
    full_sin = 2.0 * sine * cosine
    return full_cos + full_sin, full_cos - full_sin


def along_y(tab, plus, minus, options):
    w = [wide(o, ROWS) for o in options]
    even = w[0] + tab[1] * w[1] + tab[2] * w[2] + tab[3] * w[3]
    odd = tab[4] * w[1] + tab[5] * w[2] + tab[6] * w[3]
    return even * plus + odd * minus


def z_tiles(row_z, options_list):
    tile = jnp.floor(row_z * F32(1 / 16))
    first = iota(16) - wide(row_z - 16.0 * tile, 16)
    here = wide(tile, 16)
    after = jnp.where(here == F32(N // 16 - 1), F32(0.0), here + 1.0)
    here = here.astype(BF16)
    after = after.astype(BF16)
    results = [[] for _ in range(2 * len(options_list))]
    pieces = []
    for options in options_list:
        pieces.append((*split(pick(first, options)), *split(pick(first + 16.0, options))))
    zero = jnp.zeros((16, LANES), BF16)
    for t in range(N // 16):
        at_here = here == BF16(t)
        at_after = after == BF16(t)
        for i, (h0, l0, h1, l1) in enumerate(pieces):
            results[2 * i].append(jnp.where(at_here, h0, jnp.where(at_after, h1, zero)))
            results[2 * i + 1].append(jnp.where(at_here, l0, jnp.where(at_after, l1, zero)))
    return [jnp.concatenate(r, axis=0) for r in results]


def lanes(parts):
    return parts[0] if len(parts) == 1 else jnp.concatenate(parts, axis=1)


def row(values, i):
    return [v[i : i + 1] for v in values]


NT = (((1,), (1,)), ((), ()))


def spread_kernel(group, unroll, steps, base_ref, pass_ref, tab_ref, in_ref, out_ref):
    a = pl.program_id(0)
    i = pl.program_id(1)

    @pl.when((a == 0) & (i == 0))
    def _():
        out_ref[...] = jnp.zeros_like(out_ref)

    tab = [tab_ref[m] for m in range(7)]
    for u in range(unroll):
        index = (a * steps + i) * unroll + u
        base = base_ref[index]
        sets = []
        z_high, z_low = [], []
        for j in range(group):
            rows = in_ref[0, j, :, u * LANES : (u + 1) * LANES]
            w = spline(rows)
            plus, minus = rotation(tab, rows[1:2])
            y = along_y(tab, plus, minus, row(w, 4)) * wide(rows[6:7], ROWS)
            high, low = z_tiles(rows[2:3], [row(w, 5)])
            z_high.append(high)
            z_low.append(low)
            sets.append((rows[0:1], row(w, 3), y))
        z_high, z_low = lanes(z_high), lanes(z_low)

        def one_pass(start):
            highs, lows = [], []
            for row_x, w, y in sets:
                x = pick(iota(PLANES) + (start.astype(F32) - wide(row_x, PLANES)), w)
                pieces = [split(wide(x[m : m + 1], ROWS) * y) for m in range(PLANES)]
                highs.append(jnp.concatenate([p[0] for p in pieces], axis=0))
                lows.append(jnp.concatenate([p[1] for p in pieces], axis=0))
            high, low = lanes(highs), lanes(lows)
            both = lax.dot_general(
                jnp.concatenate([high, low], axis=0), z_high, NT, preferred_element_type=F32
            )
            rows_in = PLANES * ROWS
            total = both[:rows_in] + both[rows_in:]
            total += lax.dot_general(high, z_low, NT, preferred_element_type=F32)
            total = total.reshape(PLANES, ROWS, N)
            for h in range(N // LANES):
                out_ref[h, pl.ds(start, PLANES)] += total[:, :, h * LANES : (h + 1) * LANES]

        one_pass(base)

        def more(p, carry):
            one_pass(base + p * PLANES)
            return carry

        lax.fori_loop(1, pass_ref[index], more, 0)

    @pl.when((a == pl.num_programs(0) - 1) & (i == pl.num_programs(1) - 1))
    def _():
        for h in range(N // LANES):
            out_ref[h, N] += out_ref[h, 0]
            out_ref[h, 1:3] += out_ref[h, N + 1 : N + 3]


def sample_kernel(group, unroll, steps, base_ref, pass_ref, tab_ref, in_ref, high_ref, low_ref, out_ref):
    a = pl.program_id(0)
    i = pl.program_id(1)
    tab = [tab_ref[m] for m in range(7)]
    for u in range(unroll):
        index = (a * steps + i) * unroll + u
        base = base_ref[index]
        sets = []
        tiles = [[] for _ in range(4)]
        for j in range(group):
            rows = in_ref[0, j, :, u * LANES : (u + 1) * LANES]
            w = spline(rows)
            s = slopes(rows)
            plus, minus = rotation(tab, rows[1:2])
            y = along_y(tab, plus, minus, row(w, 4))
            y_slope = along_y(tab, plus, minus, row(s, 4))
            for k, t in enumerate(z_tiles(rows[2:3], [row(w, 5), row(s, 5)])):
                tiles[k].append(t)
            sets.append((rows[0:1], row(w, 3), row(s, 3), y, y_slope))
        z_high, z_low, s_high, s_low = [lanes(t) for t in tiles]
        z_all = jnp.concatenate([z_high, z_high, z_low], axis=0)
        s_all = jnp.concatenate([s_high, s_high, s_low], axis=0)

        def one_pass(start):
            high = high_ref[pl.ds(start, PLANES)].reshape(PLANES * ROWS, N)
            low = low_ref[pl.ds(start, PLANES)].reshape(PLANES * ROWS, N)
            field = jnp.concatenate([high, low, high], axis=1)
            value = jnp.dot(field, z_all, preferred_element_type=F32)
            slope = jnp.dot(field, s_all, preferred_element_type=F32)
            results = []
            for j, (row_x, w, s, y, y_slope) in enumerate(sets):
                offset = iota(PLANES) + (start.astype(F32) - wide(row_x, PLANES))
                x = pick(offset, w)
                x_slope = pick(offset, s)
                sums = [jnp.zeros((ROWS, LANES), F32) for _ in range(4)]
                for m in range(PLANES):
                    v = value[m * ROWS : (m + 1) * ROWS, j * LANES : (j + 1) * LANES]
                    g = slope[m * ROWS : (m + 1) * ROWS, j * LANES : (j + 1) * LANES]
                    wx = wide(x[m : m + 1], ROWS)
                    sx = wide(x_slope[m : m + 1], ROWS)
                    sums[0] += v * wx
                    sums[1] += v * sx
                    sums[3] += g * wx
                results.append(
                    jnp.concatenate(
                        [
                            jnp.sum(sums[0] * y, axis=0, keepdims=True),
                            jnp.sum(sums[1] * y, axis=0, keepdims=True),
                            jnp.sum(sums[0] * y_slope, axis=0, keepdims=True),
                            jnp.sum(sums[3] * y, axis=0, keepdims=True),
                        ],
                        axis=0,
                    )
                )
            return results

        for j, r in enumerate(one_pass(base)):
            out_ref[0, j, :, u * LANES : (u + 1) * LANES] = r

        def more(p, carry):
            for j, r in enumerate(one_pass(base + p * PLANES)):
                out_ref[0, j, :, u * LANES : (u + 1) * LANES] += r
            return carry

        lax.fori_loop(1, pass_ref[index], more, 0)


def filter_kernel(table_ref, green_ref, in_ref, high_ref, low_ref, field):
    k = pl.program_id(0)
    t_high, t_low = split(table_ref[...])

    def right(value):
        high, low = split(value)
        both = jnp.dot(jnp.concatenate([high, low], axis=0), t_high, preferred_element_type=F32)
        return both[:N] + both[N:] + jnp.dot(high, t_low, preferred_element_type=F32)

    def left(value):
        high, low = split(value)
        both = jnp.dot(jnp.concatenate([t_high, t_low], axis=0), high, preferred_element_type=F32)
        return both[:N] + both[N:] + jnp.dot(t_high, low, preferred_element_type=F32)

    halves = range(N // LANES)
    value = lanes([in_ref.at[h][pl.ds(ROWS + k, N, ROWS), :] for h in halves])
    value = left(right(value)) * green_ref[0]
    value = right(left(value))
    for h in halves:
        field.at[h][pl.ds(ROWS + k, N, ROWS), :] = value[:, h * LANES : (h + 1) * LANES]

    @pl.when(k == pl.num_programs(0) - 1)
    def _():
        for h in halves:
            field[h, 0:ROWS, :] = field[h, N * ROWS : (N + 1) * ROWS, :]
            field[h, (N + 1) * ROWS : (N + PAD) * ROWS, :] = field[h, ROWS : PAD * ROWS, :]

        def part(x, carry):
            where = pl.ds(pl.multiple_of(x * (PLANES * ROWS), PLANES * ROWS), PLANES * ROWS)
            high, low = split(lanes([field[h, where, :] for h in halves]))
            high_ref[where, :] = high
            low_ref[where, :] = low
            return carry

        lax.fori_loop(0, (N + PAD) // PLANES, part, 0)


def table_part(rows, columns, size):
    product = rows[:, None] * columns[None, :] % size
    angle = product.astype(F32) * (2.0 * jnp.pi / size)
    return jnp.cos(angle) + jnp.sin(angle)


def symbol(index, size):
    sines = 2.0 * jnp.sin(jnp.pi * index.astype(F32) / size)
    return sines * sines


def green_of(freq_a, freq_b, freq_c, grid_size):
    total = (
        symbol(freq_a, grid_size)[:, None, None]
        + symbol(freq_b, grid_size)[None, :, None]
        + symbol(freq_c, grid_size)[None, None, :]
    )
    safe = jnp.where(total > 0, total, F32(1.0))
    return jnp.where(total > 0, jnp.exp(-0.5 * total) / safe, F32(0.0)) / float(
        grid_size * grid_size * grid_size
    )


def shards(cell_x, cell_y, cell_z, fraction, charge):
    count = charge.shape[0]
    n_x, n_y = lax.axis_size("gx"), lax.axis_size("gy")
    at_x, at_y = lax.axis_index("gx"), lax.axis_index("gy")
    planes_x, planes_y = N // n_x, N // n_y
    own = N // (n_x * n_y)
    chunks = count // LANES
    place = jnp.arange(count, dtype=jnp.int32)

    key, cy, cz, fx, fy, fz, q, order = lax.sort(
        (cell_x, cell_y, cell_z, fraction[0], fraction[1], fraction[2], charge, place),
        num_keys=1,
        is_stable=False,
    )
    plane = (key + at_x * planes_x).astype(F32)
    line = ((cy + (at_y * planes_y + N - 1)) % N).astype(F32)
    depth = ((cz + (N - 1)) % N).astype(F32)
    ends = plane.reshape(chunks, LANES)
    ends = jnp.concatenate([ends[:, 0], ends[:, -1], jnp.zeros((count - 2 * chunks,), F32)])
    packed = jnp.stack([plane, line, depth, fx, fy, fz, q, ends])
    everyone = lax.all_gather(packed, ("gx", "gy")).reshape(n_x, n_y, 8, count)

    ends = everyone[:, :, 7, : 2 * chunks]
    first = jnp.min(ends[:, :, :chunks], axis=1).astype(jnp.int32)
    last = jnp.max(ends[:, :, chunks:], axis=1).astype(jnp.int32)
    passes = ((last - first + (3 + PLANES)) // PLANES).reshape(-1)
    first = first.reshape(-1)

    freq = (at_x * n_y + at_y) * own + jnp.arange(ROWS, dtype=jnp.int32)
    angle = freq.astype(F32) * F32(2.0 * np.pi / N)
    offsets = jnp.arange(1, 4, dtype=F32)[:, None] * angle[None, :]
    tab = jnp.concatenate(
        [(freq.astype(F32) * F32(1.0 / N))[None], jnp.cos(offsets), jnp.sin(offsets)], axis=0
    )
    tab = jnp.broadcast_to(tab[:, :, None], (7, ROWS, LANES))
    full = jnp.arange(N, dtype=jnp.int32)
    table = table_part(full, full, N)
    green = green_of(freq[:own], full, full, N)

    unroll = 2 if chunks % 2 == 0 else 1
    steps = chunks // unroll
    size = N + PAD
    params = pltpu.CompilerParams(vmem_limit_bytes=50 * 1024 * 1024)
    in_spec = pl.BlockSpec((1, n_y, 8, unroll * LANES), lambda a, i, *_: (a, 0, 0, i))
    tab_spec = pl.BlockSpec((7, ROWS, LANES), lambda a, i, *_: (0, 0, 0))
    whole = pl.BlockSpec((size, ROWS, N), lambda a, i, *_: (0, 0, 0))
    mesh_part = pl.pallas_call(
        functools.partial(spread_kernel, n_y, unroll, steps),
        grid_spec=pltpu.PrefetchScalarGridSpec(
            num_scalar_prefetch=2,
            grid=(n_x, steps),
            in_specs=[tab_spec, in_spec],
            out_specs=pl.BlockSpec((N // LANES, size, ROWS, LANES), lambda a, i, *_: (0, 0, 0, 0)),
        ),
        out_shape=jax.ShapeDtypeStruct((N // LANES, size, ROWS, LANES), F32),
        compiler_params=params,
        name="spread",
    )(first, passes, tab, everyone)

    flat = jax.ShapeDtypeStruct((size * ROWS, N), BF16)
    flat_spec = pl.BlockSpec((size * ROWS, N), lambda k: (0, 0))
    high, low = pl.pallas_call(
        filter_kernel,
        grid=(own,),
        in_specs=[
            pl.BlockSpec((N, N), lambda k: (0, 0)),
            pl.BlockSpec((1, N, N), lambda k: (k, 0, 0)),
            pl.BlockSpec((N // LANES, size * ROWS, LANES), lambda k: (0, 0, 0)),
        ],
        out_specs=[flat_spec, flat_spec],
        out_shape=[flat, flat],
        scratch_shapes=[pltpu.VMEM((N // LANES, size * ROWS, LANES), F32)],
        compiler_params=params,
        name="filter",
    )(table, green, mesh_part.reshape(N // LANES, size * ROWS, LANES))

    partial = pl.pallas_call(
        functools.partial(sample_kernel, n_y, unroll, steps),
        grid_spec=pltpu.PrefetchScalarGridSpec(
            num_scalar_prefetch=2,
            grid=(n_x, steps),
            in_specs=[tab_spec, in_spec, whole, whole],
            out_specs=pl.BlockSpec((1, n_y, 4, unroll * LANES), lambda a, i, *_: (a, 0, 0, i)),
        ),
        out_shape=jax.ShapeDtypeStruct((n_x, n_y, 4, count), F32),
        compiler_params=params,
        name="sample",
    )(first, passes, tab, everyone, high.reshape(size, ROWS, N), low.reshape(size, ROWS, N))

    back = lax.all_to_all(
        partial.reshape(n_x * n_y, 4, count), ("gx", "gy"), split_axis=0, concat_axis=0, tiled=True
    )
    total = jnp.sum(back, axis=0)
    _, value, grad_x, grad_y, grad_z = lax.sort(
        (order, total[0], total[1], total[2], total[3]), num_keys=1, is_stable=False
    )
    forces = -charge[None, :] * jnp.stack([grad_x, grad_y, grad_z], axis=0)
    return (charge * value, forces)


def solution(mesh):
    placed = P(("parts", "gx", "gy"))
    return jax.shard_map(
        shards,
        mesh=mesh,
        in_specs=(placed, placed, placed, P(None, ("parts", "gx", "gy")), placed),
        out_specs=(placed, P(None, ("parts", "gx", "gy"))),
        check_vma=False,
    )
```

```python
import functools

import jax
import jax.numpy as jnp
import numpy as np
from jax import lax
from jax.experimental import pallas as pl
from jax.experimental.pallas import tpu as pltpu
from jax.sharding import PartitionSpec as P

N = 256
LANES = 128
ROWS = 16
PLANES = 7
PAD = 16
LINES = 80
F32 = jnp.float32
BF16 = jnp.bfloat16
NT = (((1,), (1,)), ((), ()))

SIN_PI = (3.141592640130707, -5.167710083507877, 2.550077523214437, -0.5982912856197345, 0.07765766030450941)
COS_PI = (
    0.9999999997799038,
    -4.934802137078749,
    4.058709159554242,
    -1.335212003029471,
    0.23493731372678894,
    -0.024396324214549327,
)


def poly(coefficients, x):
    result = coefficients[-1]
    for value in coefficients[-2::-1]:
        result = result * x + F32(value)
    return result


def spline(param):
    rest = 1.0 - param
    square = param * param
    cube = square * param
    return [
        rest * rest * rest * F32(1 / 6),
        (3.0 * cube - 6.0 * square + 4.0) * F32(1 / 6),
        (-3.0 * cube + 3.0 * square + 3.0 * param + 1.0) * F32(1 / 6),
        cube * F32(1 / 6),
    ]


def slopes(param):
    rest = 1.0 - param
    square = param * param
    return [
        rest * rest * F32(-0.5),
        1.5 * square - 2.0 * param,
        -1.5 * square + param + 0.5,
        square * F32(0.5),
    ]


def split(value):
    high = value.astype(BF16)
    return high, (value - high.astype(F32)).astype(BF16)


def wide(row, rows):
    return jnp.broadcast_to(row, (rows, row.shape[1]))


def at(values, i):
    return [v[i : i + 1] for v in values]


def pick(offset, options):
    result = jnp.zeros(offset.shape, F32)
    for i in (3, 2, 1, 0):
        result = jnp.where(offset == F32(i), wide(options[i], offset.shape[0]), result)
    return result


def iota(rows):
    return lax.broadcasted_iota(jnp.int32, (rows, LANES), 0).astype(F32)


def along_x(start, row_x, options):
    return pick(iota(8) + (start.astype(F32) - wide(row_x, 8)), options)


def rotation(tab, row_z):
    turn = tab[0] * wide(row_z + 0.5, ROWS)
    turn = turn - jnp.round(turn)
    square = turn * turn
    sine = turn * poly(SIN_PI, square)
    cosine = poly(COS_PI, square)
    twice = sine + sine
    full_cos = 1.0 - twice * sine
    full_sin = twice * cosine
    return full_cos + full_sin, full_cos - full_sin


def along_z(tab, plus, minus, options):
    w = at(options, 5)
    even = tab[1] * wide(w[0] + w[3], ROWS) + tab[2] * wide(w[1] + w[2], ROWS)
    odd = tab[3] * wide(w[3] - w[0], ROWS) + tab[4] * wide(w[2] - w[1], ROWS)
    return even * plus + odd * minus


def along_y(row_y, options_list):
    tile = wide(jnp.floor(row_y * F32(1 / 16)), 16)
    offset = iota(16) - (wide(row_y, 16) - 16.0 * tile)
    before = offset < 0.0
    offset = jnp.where(before, offset + 16.0, offset)
    tile = jnp.where(before, tile + 1.0, tile).astype(BF16)
    pieces = []
    for options in options_list:
        pieces += split(pick(offset, options))
    zero = jnp.zeros((16, LANES), BF16)
    results = [[] for _ in pieces]
    for t in range(LINES // 16):
        here = tile == BF16(t)
        for result, piece in zip(results, pieces):
            result.append(jnp.where(here, piece, zero))
    return [jnp.concatenate(r, axis=0) for r in results]


def lanes(parts):
    return parts[0] if len(parts) == 1 else jnp.concatenate(parts, axis=1)


def place_of(u):
    return pl.ds(pl.multiple_of(u * LANES, LANES), LANES)


def loader(refs, step, n_x):
    def load(place):
        rows = refs[0][0, :, place]
        for g in range(1, len(refs)):
            rows = jnp.where(step >= g * n_x, refs[g][0, :, place], rows)
        return rows

    return load


def rounds(unroll, chunks, begin, base_ref, pass_ref, one_pass):
    def some(i, most):
        for u in range(unroll):
            index = begin + i * unroll + u
            most = jnp.maximum(most, pass_ref[index])
            one_pass(place_of(i * unroll + u), base_ref[index], False)
        return most

    most = lax.fori_loop(0, chunks // unroll, some, jnp.int32(1))

    @pl.when(most > 1)
    def _():
        def one(u, carry):
            def more(p, carry):
                one_pass(place_of(u), base_ref[begin + u] + p * PLANES, True)
                return carry

            return lax.fori_loop(1, pass_ref[begin + u], more, carry)

        lax.fori_loop(0, chunks, one, 0)


def spread(unroll, chunks, step, base_ref, pass_ref, tab_ref, load, out_ref):
    tab = [tab_ref[m] for m in range(5)]
    empty = jnp.zeros((LANES - LINES, 2 * LANES), BF16)

    def one_pass(place, start, again):
        rows = load(place)
        w = spline(rows)
        plus, minus = rotation(tab, rows[2:3])
        z = along_z(tab, plus, minus, w) * wide(rows[6:7], ROWS)
        high, low = along_y(rows[1:2], [at(w, 4)])
        lines = jnp.concatenate(
            [lanes([high, high]), empty, lanes([low, jnp.zeros_like(low)]), empty], axis=0
        )
        x = along_x(start, rows[0:1], at(w, 3))
        pieces = [split(wide(x[m : m + 1], ROWS) * z) for m in range(PLANES)]
        left = lanes([jnp.concatenate([p[k] for p in pieces], axis=0) for k in range(2)])
        both = lax.dot_general(left, lines, NT, preferred_element_type=F32)
        total = both[:, :LANES] + both[:, LANES:]
        out_ref[pl.ds(start, PLANES)] += total.reshape(PLANES, ROWS, LANES)

    rounds(unroll, chunks, step * chunks, base_ref, pass_ref, one_pass)


def add_rows(terms):
    a, c, b, d = terms
    place = lax.broadcasted_iota(jnp.int32, (8, LANES), 0)
    low, even = place < 4, place & 2 == 0
    p = jnp.where(low, a, b) + pltpu.roll(jnp.where(low, b, a), 4, 0)
    q = jnp.where(low, c, d) + pltpu.roll(jnp.where(low, d, c), 4, 0)
    r = jnp.where(even, p, q) + jnp.where(even, pltpu.roll(p, 6, 0), pltpu.roll(q, 2, 0))
    r = r + pltpu.roll(r, 7, 0)
    return jnp.concatenate([r[i : i + 1] for i in (0, 2, 4, 6)], axis=0)


def sample(unroll, chunks, step, base_ref, pass_ref, tab_ref, load, field_ref, out_ref):
    tab = [tab_ref[m] for m in range(5)]

    def one_pass(place, start, again):
        rows = load(place)
        w, s = spline(rows), slopes(rows)
        plus, minus = rotation(tab, rows[2:3])
        charge = wide(rows[6:7], ROWS)
        z = along_z(tab, plus, minus, w) * charge
        z_slope = along_z(tab, plus, minus, s) * charge
        high, low, s_high, s_low = along_y(rows[1:2], [at(w, 4), at(s, 4)])
        lines = lanes([stack_lines(high, low), stack_lines(s_high, s_low)])
        field = field_ref[pl.ds(start, PLANES)].reshape(PLANES * ROWS, N)
        sampled = jnp.dot(field, lines, preferred_element_type=F32)
        x = along_x(start, rows[0:1], at(w, 3))
        x_slope = along_x(start, rows[0:1], at(s, 3))
        both, by_x, by_y = [jnp.zeros((ROWS, LANES), F32) for _ in range(3)]
        for m in range(PLANES):
            v = sampled[m * ROWS : (m + 1) * ROWS, :LANES]
            g = sampled[m * ROWS : (m + 1) * ROWS, LANES:]
            wx = wide(x[m : m + 1], ROWS)
            both += v * wx
            by_x += v * wide(x_slope[m : m + 1], ROWS)
            by_y += g * wx
        terms = [both * z, by_x * z, by_y * z, both * z_slope]
        total = add_rows([t[:8] + t[8:] for t in terms])
        if again:
            total += out_ref[:, place]
        out_ref[:, place] = total

    rounds(unroll, chunks, step * chunks, base_ref, pass_ref, one_pass)


MORE = LANES - LINES


def stack_lines(high, low):
    zero = jnp.zeros((2 * LANES - 3 * LINES, LANES), BF16)
    return jnp.concatenate([high, low[MORE:], zero, high, low[:MORE]], axis=0)


def pack(field, out_ref):
    field[0:ROWS, :] = field[N * ROWS : (N + 1) * ROWS, :]
    field[(N + 1) * ROWS : (N + PAD) * ROWS, :] = field[ROWS : PAD * ROWS, :]
    size = (N + PAD) * ROWS // 4
    lane = lax.broadcasted_iota(jnp.int32, (size, LANES), 1)

    def part(i, carry):
        where = pl.ds(pl.multiple_of(i * size, size), size)
        value = field[where, :]
        high = value.astype(BF16).astype(F32)
        first = jnp.where(lane < LINES, high, pltpu.roll(high, LANES - MORE + LINES - LANES, 1))
        second = jnp.where(lane < LINES, value - high, pltpu.roll(high, LINES, 1))
        out_ref[where, :LANES] = first.astype(BF16)
        out_ref[where, LANES:] = second.astype(BF16)
        return carry

    lax.fori_loop(0, (N + PAD) * ROWS // size, part, 0)


def wrap(mesh_ref):
    mesh_ref[N] += mesh_ref[0]
    mesh_ref[1:3] += mesh_ref[N + 1 : N + 3]


def near_kernel(unroll, chunks, n_x, base_ref, pass_ref, tab_ref, *refs):
    in_refs, out_ref = refs[:-1], refs[-1]
    step = pl.program_id(0)

    @pl.when(step == 0)
    def _():
        out_ref[...] = jnp.zeros_like(out_ref)

    load = loader(in_refs, step, n_x)
    spread(unroll, chunks, step, base_ref, pass_ref, tab_ref, load, out_ref.at[step // n_x])

    @pl.when(step == pl.num_programs(0) - 1)
    def _():
        for g in range(len(in_refs)):
            wrap(out_ref.at[g])


def far_kernel(longer, unroll, chunks, n_x, turns, base_ref, pass_ref, tab_ref, *refs):
    groups = len(refs) - 10
    in_refs = refs[:groups]
    near_ref, table_ref, lines_ref, back_ref, green_ref = refs[groups : groups + 5]
    field_ref, out_ref, mesh, far_field, arrived = refs[groups + 5 :]
    step = pl.program_id(0)
    spreads = groups * n_x
    packs = spreads + turns
    samples = packs + 2 * groups
    copy = pltpu.make_async_copy(near_ref, mesh.at[pl.ds(0, groups)], arrived)

    @pl.when(step == 0)
    def _():
        copy.start()
        mesh[groups:] = jnp.zeros_like(mesh[groups:])

    @pl.when(step < spreads)
    def _():
        load = loader(in_refs, step, n_x)
        to = mesh.at[groups + step // n_x]
        spread(longer, chunks, step, base_ref, pass_ref, tab_ref, load, to)

    @pl.when(step == spreads)
    def _():
        copy.wait()
        for g in range(groups):
            wrap(mesh.at[groups + g])

    flat = mesh.reshape(2 * groups, (N + PAD) * ROWS, LANES)

    @pl.when((step >= spreads) & (step < packs))
    def _():
        def right(value, matrix_ref):
            high, low = split(value)
            return jnp.dot(lanes([high, low, high]), matrix_ref[...], preferred_element_type=F32)

        def left(value):
            high, low = split(value)
            both = jnp.concatenate([high, high, low], axis=0)
            return jnp.dot(table_ref[...], both, preferred_element_type=F32)

        at_once = green_ref.shape[0]
        begin = ROWS + (step - spreads) * at_once
        owns = [pl.ds(begin + u, N, ROWS) for u in range(at_once)]
        values = [lanes([flat.at[s][own, :] for s in range(2 * groups)]) for own in owns]
        values = [right(v, lines_ref) for v in values]
        values = [left(v) * green_ref[u] for u, v in enumerate(values)]
        values = [left(v) for v in values]
        values = [right(v, back_ref) for v in values]
        for own, value in zip(owns, values):
            for s in range(2 * groups):
                flat.at[s][own, :] = value[:, s * LANES : (s + 1) * LANES]

    far_flat = far_field.reshape(groups, (N + PAD) * ROWS, N)

    @pl.when((step >= packs) & (step < packs + groups))
    def _():
        pack(flat.at[groups + step - packs], far_flat.at[step - packs])

    @pl.when((step >= packs + groups) & (step < samples))
    def _():
        pack(flat.at[step - packs - groups], field_ref.at[0])

    @pl.when(step >= samples)
    def _():
        now = step - samples
        load = loader(in_refs, now, n_x)
        at_field = far_field.at[now // n_x]
        sample(unroll, chunks, now, base_ref, pass_ref, tab_ref, load, at_field, out_ref.at[0, 0])


def last_kernel(unroll, chunks, n_x, base_ref, pass_ref, tab_ref, *refs):
    in_refs, (field_ref, out_ref) = refs[:-2], refs[-2:]
    step = pl.program_id(0)
    load = loader(in_refs, step, n_x)
    sample(unroll, chunks, step, base_ref, pass_ref, tab_ref, load, field_ref.at[0], out_ref.at[0, 0])


def table_part(rows, columns, size):
    product = rows[:, None] * columns[None, :] % size
    angle = product.astype(F32) * (2.0 * jnp.pi / size)
    return jnp.cos(angle) + jnp.sin(angle)


def symbol(index, size):
    sines = 2.0 * jnp.sin(jnp.pi * index.astype(F32) / size)
    return sines * sines


def green_of(freq_a, freq_b, freq_c, grid_size):
    total = (
        symbol(freq_a, grid_size)[:, None, None]
        + symbol(freq_b, grid_size)[None, :, None]
        + symbol(freq_c, grid_size)[None, None, :]
    )
    safe = jnp.where(total > 0, total, F32(1.0))
    return jnp.where(total > 0, jnp.exp(-0.5 * total) / safe, F32(0.0)) / float(
        grid_size * grid_size * grid_size
    )


def halves(value):
    high = lax.reduce_precision(value, exponent_bits=8, mantissa_bits=7)
    return high.astype(BF16), (value - high).astype(BF16)


def exchange(value, axis, distance, flip):
    size = lax.axis_size(axis)
    pairs = [(i, i ^ distance if flip else (i + distance) % size) for i in range(size)]
    return lax.ppermute(value, axis, pairs)


def gather_x(value):
    size = lax.axis_size("gx")
    if size > 8:
        return lax.all_gather(value, "gx")
    me = lax.axis_index("gx")
    parts = jnp.stack([value] + [exchange(value, "gx", s, False) for s in range(1, size)])
    return parts[(me - jnp.arange(size)) % size] if size > 1 else parts


def scatter_x(value):
    size = lax.axis_size("gx")
    if size > 8:
        return jnp.sum(lax.all_to_all(value, "gx", split_axis=0, concat_axis=0, tiled=True), axis=0)
    me = lax.axis_index("gx")
    total = lax.dynamic_index_in_dim(value, me, 0, keepdims=False)
    for s in range(1, size):
        part = lax.dynamic_index_in_dim(value, (me + s) % size, 0, keepdims=False)
        total = total + exchange(part, "gx", s, False)
    return total


def shards(cell_x, cell_y, cell_z, fraction, charge):
    count = charge.shape[0]
    n_x, n_y = lax.axis_size("gx"), lax.axis_size("gy")
    at_x, at_y = lax.axis_index("gx"), lax.axis_index("gy")
    planes_x, planes_y = N // n_x, N // n_y
    own = N // (n_x * n_y)
    chunks = count // LANES
    place = jnp.arange(count, dtype=jnp.int32)

    key, cy, cz, fx, fy, fz, q, order = lax.sort(
        (cell_x, cell_y, cell_z, fraction[0], fraction[1], fraction[2], charge, place),
        num_keys=1,
        is_stable=False,
    )
    plane = (key + at_x * planes_x).astype(F32)
    ends = plane.reshape(chunks, LANES)
    ends = jnp.concatenate([ends[:, 0], ends[:, -1], jnp.zeros((count - 2 * chunks,), F32)])
    packed = jnp.stack([plane, cy.astype(F32), cz.astype(F32), fx, fy, fz, q, ends])

    half = n_y // 2
    groups = [gather_x(packed)]
    for s in range(1, half + 1):
        step = s & -s
        groups.append(exchange(groups[s ^ step], "gy", step, True))
    partners = [at_y ^ s for s in range(n_y)]

    freq = (at_x * n_y + at_y) * own + jnp.arange(ROWS, dtype=jnp.int32)
    angle = freq.astype(F32) * F32(np.pi / N)
    tab = jnp.stack(
        [freq.astype(F32) * F32(1 / N), jnp.cos(3 * angle), jnp.cos(angle), jnp.sin(3 * angle), jnp.sin(angle)]
    )
    tab = jnp.where((jnp.arange(ROWS) < own)[None], tab, F32(0.0))
    tab = jnp.broadcast_to(tab[:, :, None], (5, ROWS, LANES))
    full = jnp.arange(N, dtype=jnp.int32)
    table = table_part(full, full, N)
    green = green_of(freq[:own], full, full, N)
    reach = jnp.arange(LANES, dtype=jnp.int32)
    line = jnp.concatenate([p * planes_y + reach - 1 for p in partners]) % N
    used = jnp.tile(reach < planes_y + 3, n_y)
    lines = jnp.where(used[:, None], table_part(line, full, N), F32(0.0))
    back = jnp.where(used[None, :], table_part(full, line, N), F32(0.0))

    unroll = 8 if chunks % 8 == 0 else 1
    longer = 32 if chunks % 32 == 0 else unroll
    size = N + PAD
    steps = half * n_x
    at_once = 4 if own % 4 == 0 else 1
    turns = own // at_once
    params = pltpu.CompilerParams(vmem_limit_bytes=56 * 1024 * 1024)

    def bounds(some):
        ends = jnp.concatenate([g[:, 7, : 2 * chunks] for g in some]).astype(jnp.int32)
        first, last = ends[:, :chunks].reshape(-1), ends[:, chunks:].reshape(-1)
        return first, (last - first + (3 + PLANES)) // PLANES

    def clamp(step, top):
        return jnp.minimum(jnp.maximum(step, 0), top)

    def charges(begins):
        def spec(g):
            def place(t, *_):
                at = 0
                for begin in begins:
                    at = jnp.where(t >= begin, clamp(t - begin - g * n_x, n_x - 1), at)
                return (at, 0, 0)

            return pl.BlockSpec((1, 8, count), place)

        return [spec(g) for g in range(half)]

    def whole(*shape):
        return pl.BlockSpec(shape, lambda *_: (0,) * len(shape))

    def results(begin):
        def place(t, *_):
            at = clamp(t - begin, steps - 1)
            return (at // n_x, at % n_x, 0, 0)

        return pl.BlockSpec((1, 1, 4, count), place)

    def estimate(passes):
        return pl.CostEstimate(
            flops=passes * steps * count * 600000,
            bytes_accessed=passes * steps * count * 160,
            transcendentals=0,
        )

    tab_spec = whole(5, ROWS, LANES)
    mesh_shape = (half, size, ROWS, LANES)
    sums_shape = jax.ShapeDtypeStruct((half, n_x, 4, count), F32)
    near = groups[:half]
    near_bounds = bounds(near)

    near_mesh = pl.pallas_call(
        functools.partial(near_kernel, longer, chunks, n_x),
        grid_spec=pltpu.PrefetchScalarGridSpec(
            num_scalar_prefetch=2,
            grid=(steps,),
            in_specs=[tab_spec] + charges([0]),
            out_specs=whole(*mesh_shape),
        ),
        out_shape=jax.ShapeDtypeStruct(mesh_shape, F32),
        compiler_params=params,
        cost_estimate=estimate(1),
        name="near_spread",
    )(*near_bounds, tab, *near)

    near_mesh, arrived = lax.optimization_barrier((near_mesh, groups[half]))
    far = [arrived]
    for s in range(1, half):
        step = s & -s
        far.append(exchange(far[s ^ step], "gy", step, True))
    far_bounds = bounds(far)

    packs = steps + turns
    samples = packs + 2 * half
    t_high, t_low = halves(table)
    l_high, l_low = halves(lines)
    b_high, b_low = halves(back)
    near_field, far_sums = pl.pallas_call(
        functools.partial(far_kernel, longer, unroll, chunks, n_x, turns),
        grid_spec=pltpu.PrefetchScalarGridSpec(
            num_scalar_prefetch=2,
            grid=(samples + steps,),
            in_specs=[tab_spec]
            + charges([0, samples])
            + [
                pl.BlockSpec(memory_space=pl.ANY),
                whole(N, 3 * N),
                whole(3 * n_y * LANES, N),
                whole(3 * N, n_y * LANES),
                pl.BlockSpec((at_once, N, N), lambda t, *_: (clamp(t - steps, turns - 1), 0, 0)),
            ],
            out_specs=[
                pl.BlockSpec(
                    (1, size * ROWS, N), lambda t, *_: (clamp(t - packs - half, half - 1), 0, 0)
                ),
                results(samples),
            ],
            scratch_shapes=[
                pltpu.VMEM((n_y, size, ROWS, LANES), F32),
                pltpu.VMEM((half, size, ROWS, N), BF16),
                pltpu.SemaphoreType.DMA,
            ],
        ),
        out_shape=[jax.ShapeDtypeStruct((half, size * ROWS, N), BF16), sums_shape],
        compiler_params=params,
        cost_estimate=estimate(3),
        name="far_spread_filter_sample",
    )(
        *far_bounds,
        tab,
        *far,
        near_mesh,
        jnp.concatenate([t_high, t_low, t_high], axis=1),
        jnp.concatenate([l_high, l_high, l_low], axis=0),
        jnp.concatenate([b_high, b_high, b_low], axis=0),
        green,
    )

    def fold(sums):
        for s in range(len(sums) - 1, 0, -1):
            step = s & -s
            sums[s ^ step] = sums[s ^ step] + exchange(sums[s], "gy", step, True)
        return sums[0]

    far_total = fold([far_sums[s] for s in range(half)])
    far_total, near_field = lax.optimization_barrier((far_total, near_field))
    far_total = exchange(far_total, "gy", half, True)
    near_sums = pl.pallas_call(
        functools.partial(last_kernel, unroll, chunks, n_x),
        grid_spec=pltpu.PrefetchScalarGridSpec(
            num_scalar_prefetch=2,
            grid=(steps,),
            in_specs=[tab_spec]
            + charges([0])
            + [pl.BlockSpec((1, size, ROWS, N), lambda t, *_: (t // n_x, 0, 0, 0))],
            out_specs=results(0),
        ),
        out_shape=sums_shape,
        compiler_params=params,
        cost_estimate=estimate(1),
        name="near_sample",
    )(*near_bounds, tab, *near, near_field.reshape(half, size, ROWS, N))

    near_total = fold([near_sums[s] for s in range(half)])
    total = scatter_x(near_total + far_total)
    _, value, grad_x, grad_y, grad_z = lax.sort(
        (order, total[0], total[1], total[2], total[3]), num_keys=1, is_stable=False
    )
    return (value, -jnp.stack([grad_x, grad_y, grad_z], axis=0))


def solution(mesh):
    placed = P(("parts", "gx", "gy"))
    return jax.shard_map(
        shards,
        mesh=mesh,
        in_specs=(placed, placed, placed, P(None, ("parts", "gx", "gy")), placed),
        out_specs=(placed, P(None, ("parts", "gx", "gy"))),
        check_vma=False,
    )
```

```python
import functools

import jax
import jax.numpy as jnp
import numpy as np
from jax import lax
from jax.experimental import pallas as pl
from jax.experimental.pallas import tpu as pltpu
from jax.sharding import PartitionSpec as P

N = 256
LANES = 128
ROWS = 16
PLANES = 7
TABLES = 7
PAD = 16
LINES = 80
F32 = jnp.float32
BF16 = jnp.bfloat16
NT = (((1,), (1,)), ((), ()))

SIN_PI = (3.141592640130707, -5.167710083507877, 2.550077523214437, -0.5982912856197345, 0.07765766030450941)
COS_PI = (
    0.9999999997799038,
    -4.934802137078749,
    4.058709159554242,
    -1.335212003029471,
    0.23493731372678894,
    -0.024396324214549327,
)


def poly(coefficients, x):
    result = coefficients[-1]
    for value in coefficients[-2::-1]:
        result = result * x + value
    return result


SPLINE = (
    (1 / 6, 4 / 6, 1 / 6, 0.0),
    (-1 / 2, 0.0, 1 / 2, 0.0),
    (1 / 2, -1.0, 1 / 2, 0.0),
    (-1 / 6, 1 / 2, -1 / 2, 1 / 6),
)
SLOPES = ((-1 / 2, 0.0, 1 / 2, 0.0), (1.0, -2.0, 1.0, 0.0), (-1 / 2, 3 / 2, -3 / 2, 1 / 2))


def coefficients(table):
    place = iota(8)
    results = []
    for values in table:
        result = jnp.zeros((8, LANES), F32)
        for i, value in enumerate(values):
            result = jnp.where(place == i, F32(value), result)
        results.append(result)
    return results


def split(value):
    high = value.astype(BF16)
    return high, (value - high.astype(F32)).astype(BF16)


def wide(row, rows):
    return jnp.broadcast_to(row, (rows, row.shape[1]))


def iota(rows):
    return lax.broadcasted_iota(jnp.int32, (rows, LANES), 0)


def pick(options, index):
    return jnp.take_along_axis(options, index, axis=0)


def x_index(start, row_x):
    offset = iota(8) + (start - wide(row_x, 8).astype(jnp.int32))
    return jnp.minimum(offset & 0x7FFFFFFF, 7)


def rotation(tab, row_z):
    turn = tab[0] * wide(row_z + 0.5, ROWS)
    turn = turn - jnp.round(turn)
    square = turn * turn
    sine = turn * poly(SIN_PI, square)
    cosine = poly(COS_PI, square)
    twice = sine + sine
    full_cos = 1.0 - twice * sine
    full_sin = twice * cosine
    return full_cos + full_sin, full_cos - full_sin


def along_z(tab, plus, minus, middle, square):
    return (tab[1] + tab[2] * square) * plus + middle * (tab[3] + tab[4] * square) * minus


def slope_along_z(tab, plus, minus, middle, square):
    return (tab[5] * middle) * plus + (tab[3] + tab[6] * square) * minus


def along_y(row_y, options_list):
    cell = wide(row_y, 8).astype(jnp.int32)
    places = [iota(8), iota(8) + 8]
    index = [jnp.minimum((p - cell) & 15, 7) for p in places]
    tile = jnp.concatenate([(cell + (15 - p)) >> 4 for p in places], axis=0)
    tile = tile.astype(F32).astype(BF16)
    pieces = []
    for options in options_list:
        pieces += split(jnp.concatenate([pick(options, i) for i in index], axis=0))
    zero = jnp.zeros((16, LANES), BF16)
    results = [[] for _ in pieces]
    for t in range(LINES // 16):
        here = tile == BF16(t)
        for result, piece in zip(results, pieces):
            result.append(jnp.where(here, piece, zero))
    return [jnp.concatenate(r, axis=0) for r in results]


def lanes(parts):
    return parts[0] if len(parts) == 1 else jnp.concatenate(parts, axis=1)


def place_of(u):
    return pl.ds(pl.multiple_of(u * LANES, LANES), LANES)


def loader(refs, step, n_x):
    def load(place):
        rows = refs[0][0, :, place]
        for g in range(1, len(refs)):
            rows = jnp.where(step >= g * n_x, refs[g][0, :, place], rows)
        return rows

    return load


def rounds(unroll, chunks, begin, base_ref, pass_ref, one_pass):
    def some(i, most):
        for u in range(unroll):
            index = begin + i * unroll + u
            most = jnp.maximum(most, pass_ref[index])
            one_pass(place_of(i * unroll + u), base_ref[index], False)
        return most

    most = lax.fori_loop(0, chunks // unroll, some, jnp.int32(1))

    @pl.when(most > 1)
    def _():
        def one(u, carry):
            def more(p, carry):
                one_pass(place_of(u), base_ref[begin + u] + p * PLANES, True)
                return carry

            return lax.fori_loop(1, pass_ref[begin + u], more, carry)

        lax.fori_loop(0, chunks, one, 0)


def factors(rows, tab):
    plus, minus = rotation(tab, rows[2:3])
    middle = wide(rows[5:6] - 0.5, ROWS)
    square = middle * middle
    charge = wide(rows[6:7], ROWS)
    z = along_z(tab, plus, minus, middle, square) * charge
    return z, slope_along_z(tab, plus, minus, middle, square) * charge


def spread(unroll, chunks, step, base_ref, pass_ref, tab_ref, load, out_ref, kept):
    tab = [tab_ref[m] for m in range(TABLES)]
    cubic = coefficients(SPLINE)
    empty = jnp.zeros((LANES - LINES, 2 * LANES), BF16)

    def one_pass(place, start, again):
        rows = load(place)
        z, z_slope = factors(rows, tab)
        if kept is not None and not again:
            kept[:ROWS, place] = z
            kept[ROWS:, place] = z_slope
        high, low = along_y(rows[1:2], [poly(cubic, wide(rows[4:5], 8))])
        lines = jnp.concatenate(
            [lanes([high, high]), empty, lanes([low, jnp.zeros_like(low)]), empty], axis=0
        )
        x = pick(poly(cubic, wide(rows[3:4], 8)), x_index(start, rows[0:1]))
        pieces = [split(wide(x[m : m + 1], ROWS) * z) for m in range(PLANES)]
        left = lanes([jnp.concatenate([p[k] for p in pieces], axis=0) for k in range(2)])
        both = lax.dot_general(left, lines, NT, preferred_element_type=F32)
        total = both[:, :LANES] + both[:, LANES:]
        out_ref[pl.ds(start, PLANES)] += total.reshape(PLANES, ROWS, LANES)

    rounds(unroll, chunks, step * chunks, base_ref, pass_ref, one_pass)


def add_rows(terms):
    a, c, b, d = terms
    place = lax.broadcasted_iota(jnp.int32, (8, LANES), 0)
    low, even = place < 4, place & 2 == 0
    p = jnp.where(low, a, b) + pltpu.roll(jnp.where(low, b, a), 4, 0)
    q = jnp.where(low, c, d) + pltpu.roll(jnp.where(low, d, c), 4, 0)
    r = jnp.where(even, p, q) + jnp.where(even, pltpu.roll(p, 6, 0), pltpu.roll(q, 2, 0))
    r = r + pltpu.roll(r, 7, 0)
    return jnp.concatenate([r[i : i + 1] for i in (0, 2, 4, 6)], axis=0)


def sample(unroll, chunks, step, base_ref, pass_ref, tab_ref, load, field_ref, out_ref, kept):
    tab = [tab_ref[m] for m in range(TABLES)]
    cubic, quadratic = coefficients(SPLINE), coefficients(SLOPES)

    def one_pass(place, start, again):
        rows = load(place)
        if kept is None:
            z, z_slope = factors(rows, tab)
        else:
            z, z_slope = kept[:ROWS, place], kept[ROWS:, place]
        part = wide(rows[4:5], 8)
        high, low, s_high, s_low = along_y(rows[1:2], [poly(cubic, part), poly(quadratic, part)])
        lines = lanes([stack_lines(high, low), stack_lines(s_high, s_low)])
        field = field_ref[pl.ds(start, PLANES)].reshape(PLANES * ROWS, N)
        sampled = jnp.dot(field, lines, preferred_element_type=F32)
        part = wide(rows[3:4], 8)
        index = x_index(start, rows[0:1])
        x = pick(poly(cubic, part), index)
        x_slope = pick(poly(quadratic, part), index)
        both, by_x, by_y = [jnp.zeros((ROWS, LANES), F32) for _ in range(3)]
        for m in range(PLANES):
            v = sampled[m * ROWS : (m + 1) * ROWS, :LANES]
            g = sampled[m * ROWS : (m + 1) * ROWS, LANES:]
            wx = wide(x[m : m + 1], ROWS)
            both += v * wx
            by_x += v * wide(x_slope[m : m + 1], ROWS)
            by_y += g * wx
        terms = [both * z, by_x * z, by_y * z, both * z_slope]
        total = add_rows([t[:8] + t[8:] for t in terms])
        if again:
            total += out_ref[:, place]
        out_ref[:, place] = total

    rounds(unroll, chunks, step * chunks, base_ref, pass_ref, one_pass)


MORE = LANES - LINES


def stack_lines(high, low):
    zero = jnp.zeros((2 * LANES - 3 * LINES, LANES), BF16)
    return jnp.concatenate([high, low[MORE:], zero, high, low[:MORE]], axis=0)


def pack(field, out_ref):
    field[0:ROWS, :] = field[N * ROWS : (N + 1) * ROWS, :]
    field[(N + 1) * ROWS : (N + PAD) * ROWS, :] = field[ROWS : PAD * ROWS, :]
    size = (N + PAD) * ROWS // 4
    lane = lax.broadcasted_iota(jnp.int32, (size, LANES), 1)

    def part(i, carry):
        where = pl.ds(pl.multiple_of(i * size, size), size)
        value = field[where, :]
        high = value.astype(BF16).astype(F32)
        first = jnp.where(lane < LINES, high, pltpu.roll(high, LANES - MORE + LINES - LANES, 1))
        second = jnp.where(lane < LINES, value - high, pltpu.roll(high, LINES, 1))
        out_ref[where, :LANES] = first.astype(BF16)
        out_ref[where, LANES:] = second.astype(BF16)
        return carry

    lax.fori_loop(0, (N + PAD) * ROWS // size, part, 0)


def wrap(mesh_ref):
    mesh_ref[N] += mesh_ref[0]
    mesh_ref[1:3] += mesh_ref[N + 1 : N + 3]


def deliver(step, n_x, sums, out_refs):
    for g, out_ref in enumerate(out_refs):

        @pl.when(step // n_x == g)
        def _():
            out_ref[0] = sums[...]


def near_kernel(unroll, chunks, n_x, base_ref, pass_ref, tab_ref, *refs):
    in_refs, out_ref, kept = refs[:-2], refs[-2], refs[-1]
    step = pl.program_id(0)

    @pl.when(step % n_x == 0)
    def _():
        out_ref[...] = jnp.zeros_like(out_ref)

    load = loader(in_refs, step, n_x)
    spread(unroll, chunks, step, base_ref, pass_ref, tab_ref, load, out_ref.at[0], kept.at[0])

    @pl.when(step % n_x == n_x - 1)
    def _():
        wrap(out_ref.at[0])


def far_kernel(longer, unroll, chunks, n_x, turns, base_ref, pass_ref, at_ref, tab_ref, *refs):
    groups = (len(refs) - 11) // 2
    in_refs = refs[:groups]
    near_ref, table_ref, lines_ref, back_ref, green_ref = refs[groups : groups + 5]
    field_ref, out_refs = refs[groups + 5], refs[groups + 6 : -5]
    mesh, far_field, sums, kept, arrived = refs[-5:]
    keep = kept.shape[0] == groups * n_x
    step = pl.program_id(0)
    spreads = groups * n_x
    packs = spreads + turns
    samples = packs + 2 * groups
    slots = [at_ref[0] ^ s for s in range(2 * groups)]
    copies = [
        pltpu.make_async_copy(near_ref.at[g], mesh.at[slots[g]], arrived.at[g]) for g in range(groups)
    ]

    @pl.when(step == 0)
    def _():
        for copy in copies:
            copy.start()
        for slot in slots[groups:]:
            mesh[slot] = jnp.zeros(mesh.shape[1:], F32)

    @pl.when(step < spreads)
    def _():
        load = loader(in_refs, step, n_x)
        to = mesh.at[at_ref[0] ^ (groups + step // n_x)]
        at_kept = kept.at[step] if keep else None
        spread(longer, chunks, step, base_ref, pass_ref, tab_ref, load, to, at_kept)

    @pl.when(step == spreads)
    def _():
        for copy in copies:
            copy.wait()
        for slot in slots[groups:]:
            wrap(mesh.at[slot])

    flat = mesh.reshape(2 * groups, (N + PAD) * ROWS, LANES)

    @pl.when((step >= spreads) & (step < packs))
    def _():
        def right(value, matrix_ref):
            high, low = split(value)
            return jnp.dot(lanes([high, low, high]), matrix_ref[...], preferred_element_type=F32)

        def left(value):
            high, low = split(value)
            both = jnp.concatenate([high, high, low], axis=0)
            return jnp.dot(table_ref[...], both, preferred_element_type=F32)

        at_once = green_ref.shape[0]
        begin = ROWS + (step - spreads) * at_once
        owns = [pl.ds(begin + u, N, ROWS) for u in range(at_once)]
        values = [lanes([flat.at[s][own, :] for s in range(2 * groups)]) for own in owns]
        values = [right(v, lines_ref) for v in values]
        values = [left(v) * green_ref[u] for u, v in enumerate(values)]
        values = [left(v) for v in values]
        values = [right(v, back_ref) for v in values]
        for own, value in zip(owns, values):
            for s in range(2 * groups):
                flat.at[s][own, :] = value[:, s * LANES : (s + 1) * LANES]

    far_flat = far_field.reshape(groups, (N + PAD) * ROWS, N)

    @pl.when((step >= packs) & (step < packs + groups))
    def _():
        pack(flat.at[at_ref[0] ^ (groups + step - packs)], far_flat.at[step - packs])

    @pl.when((step >= packs + groups) & (step < samples))
    def _():
        pack(flat.at[at_ref[0] ^ (step - packs - groups)], field_ref.at[0])

    @pl.when(step >= samples)
    def _():
        now = step - samples
        load = loader(in_refs, now, n_x)
        at_field = far_field.at[now // n_x]
        at_kept = kept.at[now] if keep else None
        sample(unroll, chunks, now, base_ref, pass_ref, tab_ref, load, at_field, sums, at_kept)
        deliver(now, n_x, sums, out_refs)


def last_kernel(unroll, chunks, n_x, base_ref, pass_ref, tab_ref, *refs):
    groups = (len(refs) - 3) // 2
    in_refs, (kept, field_ref) = refs[:groups], refs[groups : groups + 2]
    out_refs, sums = refs[groups + 2 : -1], refs[-1]
    step = pl.program_id(0)
    load = loader(in_refs, step, n_x)
    sample(
        unroll, chunks, step, base_ref, pass_ref, tab_ref, load, field_ref.at[0], sums, kept.at[0]
    )
    deliver(step, n_x, sums, out_refs)


def tables(n_y, planes_y):
    def halves(value):
        value = value.astype(np.float32)
        high = value.astype(BF16)
        return high, (value - high.astype(np.float32)).astype(BF16)

    full = np.arange(N)
    reach = np.arange(LANES)
    line = np.concatenate([b * planes_y + reach - 1 for b in range(n_y)]) % N
    used = np.tile(reach < planes_y + 3, n_y)

    def table(rows, columns):
        angle = (rows[:, None] * columns[None, :] % N) * (2.0 * np.pi / N)
        return np.cos(angle) + np.sin(angle)

    high, low = halves(table(full, full))
    left = np.concatenate([high, low, high], axis=1)
    high, low = halves(table(line, full) * used[:, None])
    lines = np.concatenate([high, high, low], axis=0)
    high, low = halves(table(full, line) * used[None, :])
    return left, lines, np.concatenate([high, high, low], axis=0)


def symbol(index, size):
    sines = 2.0 * jnp.sin(jnp.pi * index.astype(F32) / size)
    return sines * sines


def green_of(freq_a, freq_b, freq_c, grid_size):
    total = (
        symbol(freq_a, grid_size)[:, None, None]
        + symbol(freq_b, grid_size)[None, :, None]
        + symbol(freq_c, grid_size)[None, None, :]
    )
    safe = jnp.where(total > 0, total, F32(1.0))
    return jnp.where(total > 0, jnp.exp(-0.5 * total) / safe, F32(0.0)) / float(
        grid_size * grid_size * grid_size
    )


def exchange(value, axis, distance, flip):
    size = lax.axis_size(axis)
    pairs = [(i, i ^ distance if flip else (i + distance) % size) for i in range(size)]
    return lax.ppermute(value, axis, pairs)


def gather_x(value):
    size = lax.axis_size("gx")
    if size > 8:
        return lax.all_gather(value, "gx")
    me = lax.axis_index("gx")
    parts = jnp.stack([value] + [exchange(value, "gx", s, False) for s in range(1, size)])
    return parts[(me - jnp.arange(size)) % size] if size > 1 else parts


def scatter_x(value):
    size = lax.axis_size("gx")
    if size > 8:
        return jnp.sum(lax.all_to_all(value, "gx", split_axis=0, concat_axis=0, tiled=True), axis=0)
    me = lax.axis_index("gx")
    total = lax.dynamic_index_in_dim(value, me, 0, keepdims=False)
    for s in range(1, size):
        part = lax.dynamic_index_in_dim(value, (me + s) % size, 0, keepdims=False)
        total = total + exchange(part, "gx", s, False)
    return total


def shards(cell_x, cell_y, cell_z, fraction, charge):
    count = charge.shape[0]
    n_x, n_y = lax.axis_size("gx"), lax.axis_size("gy")
    at_x, at_y = lax.axis_index("gx"), lax.axis_index("gy")
    planes_x, planes_y = N // n_x, N // n_y
    own = N // (n_x * n_y)
    chunks = count // LANES
    place = jnp.arange(count, dtype=jnp.int32)

    key, cy, cz, fx, fy, fz, q, order = lax.sort(
        (cell_x, cell_y, cell_z, fraction[0], fraction[1], fraction[2], charge, place),
        num_keys=1,
        is_stable=False,
    )
    plane = (key + at_x * planes_x).astype(F32)
    ends = plane.reshape(chunks, LANES)
    ends = jnp.concatenate([ends[:, 0], ends[:, -1], jnp.zeros((count - 2 * chunks,), F32)])
    packed = jnp.stack([plane, cy.astype(F32), cz.astype(F32), fx, fy, fz, q, ends])

    freq = (at_x * n_y + at_y) * own + jnp.arange(ROWS, dtype=jnp.int32)
    angle = freq.astype(F32) * F32(np.pi / N)
    far_cos, near_cos = jnp.cos(3 * angle), jnp.cos(angle)
    far_sin, near_sin = jnp.sin(3 * angle), jnp.sin(angle)
    tab = [
        freq.astype(F32) * F32(1 / N),
        (far_cos + 23 * near_cos) * F32(1 / 24),
        (far_cos - near_cos) * F32(1 / 2),
        (far_sin + 5 * near_sin) * F32(1 / 4),
        far_sin * F32(1 / 3) - near_sin,
        far_cos - near_cos,
        far_sin - 3 * near_sin,
    ]
    tab = jnp.stack(tab)
    tab = jnp.where((jnp.arange(ROWS) < own)[None], tab, F32(0.0))
    tab = jnp.broadcast_to(tab[:, :, None], (TABLES, ROWS, LANES))
    full = jnp.arange(N, dtype=jnp.int32)
    green = green_of(freq[:own], full, full, N)

    half = n_y // 2
    arrived, green, tab = lax.optimization_barrier((gather_x(packed), green, tab))
    groups = [arrived]
    for s in range(1, half + 1):
        step = s & -s
        groups.append(exchange(groups[s ^ step], "gy", step, True))

    unroll = 8 if chunks % 8 == 0 else 1
    longer = 32 if chunks % 32 == 0 else unroll
    size = N + PAD
    steps = half * n_x
    at_once = 4 if own % 4 == 0 else 1
    turns = own // at_once
    params = pltpu.CompilerParams(vmem_limit_bytes=56 * 1024 * 1024)

    def bounds(some):
        ends = jnp.concatenate([g[:, 7, : 2 * chunks] for g in some]).astype(jnp.int32)
        first, last = ends[:, :chunks].reshape(-1), ends[:, chunks:].reshape(-1)
        return first, (last - first + (3 + PLANES)) // PLANES

    def clamp(step, top):
        return jnp.minimum(jnp.maximum(step, 0), top)

    def charges(begins):
        def spec(g):
            def place(t, *_):
                at = 0
                for begin in begins:
                    at = jnp.where(t >= begin, clamp(t - begin - g * n_x, n_x - 1), at)
                return (at, 0, 0)

            return pl.BlockSpec((1, 8, count), place)

        return [spec(g) for g in range(half)]

    def whole(*shape):
        return pl.BlockSpec(shape, lambda *_: (0,) * len(shape))

    def results(begin):
        def spec(g):
            return pl.BlockSpec(
                (1, 4, count), lambda t, *_: (clamp(t - begin - g * n_x, n_x - 1), 0, 0)
            )

        return [spec(g) for g in range(half)]

    def estimate(passes):
        return pl.CostEstimate(
            flops=passes * steps * count * 600000,
            bytes_accessed=passes * steps * count * 160,
            transcendentals=0,
        )

    tab_spec = whole(TABLES, ROWS, LANES)
    mesh_shape = (half, size, ROWS, LANES)
    sums_shape = [jax.ShapeDtypeStruct((n_x, 4, count), F32)] * half
    sums_scratch = pltpu.VMEM((4, count), F32)
    near = groups[:half]
    near_bounds = bounds(near)

    kept_spec = pl.BlockSpec((1, 2 * ROWS, count), lambda t, *_: (t, 0, 0))
    kept_shape = jax.ShapeDtypeStruct((steps, 2 * ROWS, count), F32)
    near_mesh, near_kept = pl.pallas_call(
        functools.partial(near_kernel, longer, chunks, n_x),
        grid_spec=pltpu.PrefetchScalarGridSpec(
            num_scalar_prefetch=2,
            grid=(steps,),
            in_specs=[tab_spec] + charges([0]),
            out_specs=[
                pl.BlockSpec((1, size, ROWS, LANES), lambda t, *_: (t // n_x, 0, 0, 0)),
                kept_spec,
            ],
        ),
        out_shape=[jax.ShapeDtypeStruct(mesh_shape, F32), kept_shape],
        compiler_params=params,
        cost_estimate=estimate(1),
        name="near_spread",
    )(*near_bounds, tab, *near)

    near_mesh, arrived = lax.optimization_barrier((near_mesh, groups[half]))
    far = [arrived]
    for s in range(1, half):
        step = s & -s
        far.append(exchange(far[s ^ step], "gy", step, True))
    far_bounds = bounds(far)

    packs = steps + turns
    samples = packs + 2 * half
    near_field, *far_sums = pl.pallas_call(
        functools.partial(far_kernel, longer, unroll, chunks, n_x, turns),
        grid_spec=pltpu.PrefetchScalarGridSpec(
            num_scalar_prefetch=3,
            grid=(samples + steps,),
            in_specs=[tab_spec]
            + charges([0, samples])
            + [
                pl.BlockSpec(memory_space=pl.ANY),
                whole(N, 3 * N),
                whole(3 * n_y * LANES, N),
                whole(3 * N, n_y * LANES),
                pl.BlockSpec((at_once, N, N), lambda t, *_: (clamp(t - steps, turns - 1), 0, 0)),
            ],
            out_specs=[
                pl.BlockSpec(
                    (1, size * ROWS, N), lambda t, *_: (clamp(t - packs - half, half - 1), 0, 0)
                ),
            ]
            + results(samples),
            scratch_shapes=[
                pltpu.VMEM((n_y, size, ROWS, LANES), F32),
                pltpu.VMEM((half, size, ROWS, N), BF16),
                sums_scratch,
                pltpu.VMEM((steps if steps <= 8 else 1, 2 * ROWS, count), F32),
                pltpu.SemaphoreType.DMA((half,)),
            ],
        ),
        out_shape=[jax.ShapeDtypeStruct((half, size * ROWS, N), BF16)] + sums_shape,
        compiler_params=params,
        cost_estimate=estimate(3),
        name="far_spread_filter_sample",
    )(
        *far_bounds,
        at_y[None],
        tab,
        *far,
        near_mesh,
        *tables(n_y, planes_y),
        green,
    )

    *far_sums, near_field = lax.optimization_barrier((*far_sums, near_field))
    far_sums = [exchange(v, "gy", half, True) for v in far_sums]
    near_sums = pl.pallas_call(
        functools.partial(last_kernel, unroll, chunks, n_x),
        grid_spec=pltpu.PrefetchScalarGridSpec(
            num_scalar_prefetch=2,
            grid=(steps,),
            in_specs=[tab_spec]
            + charges([0])
            + [kept_spec, pl.BlockSpec((1, size, ROWS, N), lambda t, *_: (t // n_x, 0, 0, 0))],
            out_specs=results(0),
            scratch_shapes=[sums_scratch],
        ),
        out_shape=sums_shape,
        compiler_params=params,
        cost_estimate=estimate(1),
        name="near_sample",
    )(*near_bounds, tab, *near, near_kept, near_field.reshape(half, size, ROWS, N))

    sums = [near_sums[s] + far_sums[s] for s in range(half)]
    for s in range(half - 1, 0, -1):
        step = s & -s
        sums[s ^ step] = sums[s ^ step] + exchange(sums[s], "gy", step, True)
    total = scatter_x(sums[0])
    _, value, grad_x, grad_y, grad_z = lax.sort(
        (order, total[0], total[1], total[2], total[3]), num_keys=1, is_stable=False
    )
    return (value, -jnp.stack([grad_x, grad_y, grad_z], axis=0))


def solution(mesh):
    placed = P(("parts", "gx", "gy"))
    return jax.shard_map(
        shards,
        mesh=mesh,
        in_specs=(placed, placed, placed, P(None, ("parts", "gx", "gy")), placed),
        out_specs=(placed, P(None, ("parts", "gx", "gy"))),
        check_vma=False,
    )
```

```python
import functools

import jax
import jax.numpy as jnp
import numpy as np
from jax import lax
from jax.experimental import pallas as pl
from jax.experimental.pallas import tpu as pltpu
from jax.sharding import PartitionSpec as P

N = 256
LANES = 128
ROWS = 16
PLANES = 7
AHEAD = 1
TABLES = 9
PAD = 16
LINES = 80
F32 = jnp.float32
BF16 = jnp.bfloat16
NT = (((1,), (1,)), ((), ()))

def poly(coefficients, x):
    result = coefficients[-1]
    for value in coefficients[-2::-1]:
        result = result * x + value
    return result


SPLINE = (
    (1 / 6, 4 / 6, 1 / 6, 0.0),
    (-1 / 2, 0.0, 1 / 2, 0.0),
    (1 / 2, -1.0, 1 / 2, 0.0),
    (-1 / 6, 1 / 2, -1 / 2, 1 / 6),
)
SLOPES = ((-1 / 2, 0.0, 1 / 2, 0.0), (1.0, -2.0, 1.0, 0.0), (-1 / 2, 3 / 2, -3 / 2, 1 / 2))


def coefficients(table):
    place = iota(8)
    results = []
    for values in table:
        result = jnp.zeros((8, LANES), F32)
        for i, value in enumerate(values):
            result = jnp.where(place == i, F32(value), result)
        results.append(result)
    return results


def split(value):
    high = value.astype(BF16)
    return high, (value - high.astype(F32)).astype(BF16)


def wide(row, rows):
    return jnp.broadcast_to(row, (rows, row.shape[1]))


def iota(rows):
    return lax.broadcasted_iota(jnp.int32, (rows, LANES), 0)


def pick(options, index):
    return jnp.take_along_axis(options, index, axis=0)


def x_index(start, row_x):
    offset = iota(8) + (start - wide(row_x, 8).astype(jnp.int32))
    return jnp.minimum(offset & 0x7FFFFFFF, 7)


def rotation(tab, row_z):
    cell = wide(row_z, 8).astype(jnp.int32) & (LANES - 1)

    def look(table):
        tiles = [table[i : i + 8] for i in range(0, ROWS, 8)]
        return jnp.concatenate([jnp.take_along_axis(t, cell, axis=1) for t in tiles], axis=0)

    return look(tab[0]), look(tab[7])


def along_z(tab, plus, minus, middle, square):
    return (tab[1] + tab[2] * square) * plus + middle * (tab[3] + tab[4] * square) * minus


def slope_along_z(tab, plus, minus, middle, square):
    return (tab[5] * middle) * plus + (tab[3] + tab[6] * square) * minus


def along_y(row_y, options_list):
    cell = wide(row_y, 8).astype(jnp.int32)
    places = [iota(8), iota(8) + 8]
    index = [jnp.minimum((p - cell) & 15, 7) for p in places]
    tile = jnp.concatenate([(cell + (15 - p)) >> 4 for p in places], axis=0)
    tile = tile.astype(F32).astype(BF16)
    pieces = []
    for options in options_list:
        pieces += split(jnp.concatenate([pick(options, i) for i in index], axis=0))
    zero = jnp.zeros((16, LANES), BF16)
    results = [[] for _ in pieces]
    for t in range(LINES // 16):
        here = tile == BF16(t)
        for result, piece in zip(results, pieces):
            result.append(jnp.where(here, piece, zero))
    return [jnp.concatenate(r, axis=0) for r in results]


def lanes(parts):
    return parts[0] if len(parts) == 1 else jnp.concatenate(parts, axis=1)


def place_of(u):
    return pl.ds(pl.multiple_of(u * LANES, LANES), LANES)


def loader(refs, step, n_x):
    def load(place):
        rows = refs[0][0, :, place]
        for g in range(1, len(refs)):
            rows = jnp.where(step >= g * n_x, refs[g][0, :, place], rows)
        return rows

    return load


def rounds(unroll, chunks, begin, base_ref, pass_ref, prepare, finish):
    def some(i, most):
        waiting = []
        for u in range(unroll):
            index = begin + i * unroll + u
            most = jnp.maximum(most, pass_ref[index])
            place, start = place_of(i * unroll + u), base_ref[index]
            waiting.append((place, start, prepare(place, start, False)))
            if len(waiting) > AHEAD:
                finish(*waiting.pop(0), False)
        for item in waiting:
            finish(*item, False)
        return most

    most = lax.fori_loop(0, chunks // unroll, some, jnp.int32(1))

    @pl.when(most > 1)
    def _():
        def one(u, carry):
            def more(p, carry):
                place, start = place_of(u), base_ref[begin + u] + p * PLANES
                finish(place, start, prepare(place, start, True), True)
                return carry

            return lax.fori_loop(1, pass_ref[begin + u], more, carry)

        lax.fori_loop(0, chunks, one, 0)


def factors(rows, tab):
    plus, minus = rotation(tab, rows[2:3])
    middle = wide(rows[5:6] - 0.5, ROWS)
    square = middle * middle
    turned = tab[8] * (wide(rows[2:3], ROWS) >= F32(N // 2)).astype(F32)
    charge = wide(rows[6:7], ROWS) * (1.0 - 2.0 * turned)
    z = along_z(tab, plus, minus, middle, square) * charge
    return z, slope_along_z(tab, plus, minus, middle, square) * charge


def spread(unroll, chunks, step, base_ref, pass_ref, tab_ref, load, out_ref, kept):
    tab = [tab_ref[m] for m in range(TABLES)]
    cubic = coefficients(SPLINE)
    empty = jnp.zeros((LANES - LINES, LANES), BF16)

    def prepare(place, start, again):
        rows = load(place)
        z, z_slope = factors(rows, tab)
        if kept is not None and not again:
            kept[:ROWS, place] = z
            kept[ROWS:, place] = z_slope
        high, low = along_y(rows[1:2], [poly(cubic, wide(rows[4:5], 8))])
        high, low = [jnp.concatenate([v, empty], axis=0) for v in (high, low)]
        lines = lanes([high, high, low])
        x = pick(poly(cubic, wide(rows[3:4], 8)), x_index(start, rows[0:1]))
        pieces = [split(wide(x[m : m + 1], ROWS) * z) for m in range(PLANES)]
        left = lanes([jnp.concatenate([p[k] for p in pieces], axis=0) for k in (0, 1, 0)])
        return lax.dot_general(left, lines, NT, preferred_element_type=F32)

    def finish(place, start, total, again):
        out_ref[pl.ds(start, PLANES)] += total.reshape(PLANES, ROWS, LANES)

    rounds(unroll, chunks, step * chunks, base_ref, pass_ref, prepare, finish)


def add_rows(terms):
    a, c, b, d = terms
    place = lax.broadcasted_iota(jnp.int32, (8, LANES), 0)
    low, even = place < 4, place & 2 == 0
    p = jnp.where(low, a, b) + pltpu.roll(jnp.where(low, b, a), 4, 0)
    q = jnp.where(low, c, d) + pltpu.roll(jnp.where(low, d, c), 4, 0)
    r = jnp.where(even, p, q) + jnp.where(even, pltpu.roll(p, 6, 0), pltpu.roll(q, 2, 0))
    r = r + pltpu.roll(r, 7, 0)
    return jnp.concatenate([r[i : i + 1] for i in (0, 2, 4, 6)], axis=0)


def sample(unroll, chunks, step, base_ref, pass_ref, tab_ref, load, field_ref, out_ref, kept):
    tab = [tab_ref[m] for m in range(TABLES)]
    cubic, quadratic = coefficients(SPLINE), coefficients(SLOPES)

    def prepare(place, start, again):
        rows = load(place)
        part = wide(rows[4:5], 8)
        high, low, s_high, s_low = along_y(rows[1:2], [poly(cubic, part), poly(quadratic, part)])
        lines = lanes([stack_lines(high, low), stack_lines(s_high, s_low)])
        field = field_ref[pl.ds(start, PLANES)].reshape(PLANES * ROWS, N)
        return rows, jnp.dot(field, lines, preferred_element_type=F32)

    def finish(place, start, prepared, again):
        rows, sampled = prepared
        if kept is None:
            z, z_slope = factors(rows, tab)
        else:
            z, z_slope = kept[:ROWS, place], kept[ROWS:, place]
        part = wide(rows[3:4], 8)
        index = x_index(start, rows[0:1])
        x = pick(poly(cubic, part), index)
        x_slope = pick(poly(quadratic, part), index)
        both, by_x, by_y = [jnp.zeros((ROWS, LANES), F32) for _ in range(3)]
        for m in range(PLANES):
            v = sampled[m * ROWS : (m + 1) * ROWS, :LANES]
            g = sampled[m * ROWS : (m + 1) * ROWS, LANES:]
            wx = wide(x[m : m + 1], ROWS)
            both += v * wx
            by_x += v * wide(x_slope[m : m + 1], ROWS)
            by_y += g * wx
        terms = [both * z, by_x * z, by_y * z, both * z_slope]
        total = add_rows([t[:8] + t[8:] for t in terms])
        if again:
            total += out_ref[:, place]
        out_ref[:, place] = total

    rounds(unroll, chunks, step * chunks, base_ref, pass_ref, prepare, finish)


MORE = LANES - LINES


def stack_lines(high, low):
    zero = jnp.zeros((2 * LANES - 3 * LINES, LANES), BF16)
    return jnp.concatenate([high, low[MORE:], zero, high, low[:MORE]], axis=0)


def pack(field, out_ref):
    field[0:ROWS, :] = field[N * ROWS : (N + 1) * ROWS, :]
    field[(N + 1) * ROWS : (N + PAD) * ROWS, :] = field[ROWS : PAD * ROWS, :]
    size = (N + PAD) * ROWS // 4
    lane = lax.broadcasted_iota(jnp.int32, (size, LANES), 1)

    def part(i, carry):
        where = pl.ds(pl.multiple_of(i * size, size), size)
        value = field[where, :]
        high = value.astype(BF16).astype(F32)
        first = jnp.where(lane < LINES, high, pltpu.roll(high, LANES - MORE + LINES - LANES, 1))
        second = jnp.where(lane < LINES, value - high, pltpu.roll(high, LINES, 1))
        out_ref[where, :LANES] = first.astype(BF16)
        out_ref[where, LANES:] = second.astype(BF16)
        return carry

    lax.fori_loop(0, (N + PAD) * ROWS // size, part, 0)


def wrap(mesh_ref):
    mesh_ref[N] += mesh_ref[0]
    mesh_ref[1:3] += mesh_ref[N + 1 : N + 3]


def deliver(step, n_x, sums, out_refs):
    for g, out_ref in enumerate(out_refs):

        @pl.when(step // n_x == g)
        def _():
            out_ref[0] = sums[...]


def near_kernel(unroll, chunks, n_x, base_ref, pass_ref, tab_ref, *refs):
    in_refs, out_ref, kept = refs[:-2], refs[-2], refs[-1]
    step = pl.program_id(0)

    @pl.when(step % n_x == 0)
    def _():
        out_ref[...] = jnp.zeros_like(out_ref)

    load = loader(in_refs, step, n_x)
    spread(unroll, chunks, step, base_ref, pass_ref, tab_ref, load, out_ref.at[0], kept.at[0])

    @pl.when(step % n_x == n_x - 1)
    def _():
        wrap(out_ref.at[0])


def far_kernel(longer, unroll, chunks, n_x, turns, base_ref, pass_ref, at_ref, tab_ref, *refs):
    groups = (len(refs) - 11) // 2
    in_refs = refs[:groups]
    near_ref, table_ref, lines_ref, back_ref, green_ref = refs[groups : groups + 5]
    field_ref, out_refs = refs[groups + 5], refs[groups + 6 : -5]
    mesh, far_field, sums, kept, arrived = refs[-5:]
    keep = kept.shape[0] == groups * n_x
    step = pl.program_id(0)
    spreads = groups * n_x
    packs = spreads + turns
    samples = packs + 2 * groups
    slots = [at_ref[0] ^ s for s in range(2 * groups)]
    copies = [
        pltpu.make_async_copy(near_ref.at[g], mesh.at[slots[g]], arrived.at[g]) for g in range(groups)
    ]

    @pl.when(step == 0)
    def _():
        for copy in copies:
            copy.start()
        for slot in slots[groups:]:
            mesh[slot] = jnp.zeros(mesh.shape[1:], F32)

    @pl.when(step < spreads)
    def _():
        load = loader(in_refs, step, n_x)
        to = mesh.at[at_ref[0] ^ (groups + step // n_x)]
        at_kept = kept.at[step] if keep else None
        spread(longer, chunks, step, base_ref, pass_ref, tab_ref, load, to, at_kept)

    @pl.when(step == spreads)
    def _():
        for copy in copies:
            copy.wait()
        for slot in slots[groups:]:
            wrap(mesh.at[slot])

    flat = mesh.reshape(2 * groups, (N + PAD) * ROWS, LANES)

    @pl.when((step >= spreads) & (step < packs))
    def _():
        def right(value, matrix_ref):
            high, low = split(value)
            return jnp.dot(lanes([high, low, high]), matrix_ref[...], preferred_element_type=F32)

        def left(value):
            high, low = split(value)
            both = jnp.concatenate([high, high, low], axis=0)
            return jnp.dot(table_ref[...], both, preferred_element_type=F32)

        at_once = green_ref.shape[0]
        begin = ROWS + (step - spreads) * at_once
        owns = [pl.ds(begin + u, N, ROWS) for u in range(at_once)]
        values = [lanes([flat.at[s][own, :] for s in range(2 * groups)]) for own in owns]
        values = [right(v, lines_ref) for v in values]
        values = [left(v) * green_ref[u] for u, v in enumerate(values)]
        values = [left(v) for v in values]
        values = [right(v, back_ref) for v in values]
        for own, value in zip(owns, values):
            for s in range(2 * groups):
                flat.at[s][own, :] = value[:, s * LANES : (s + 1) * LANES]

    far_flat = far_field.reshape(groups, (N + PAD) * ROWS, N)

    @pl.when((step >= packs) & (step < packs + groups))
    def _():
        pack(flat.at[at_ref[0] ^ (groups + step - packs)], far_flat.at[step - packs])

    @pl.when((step >= packs + groups) & (step < samples))
    def _():
        pack(flat.at[at_ref[0] ^ (step - packs - groups)], field_ref.at[0])

    @pl.when(step >= samples)
    def _():
        now = step - samples
        load = loader(in_refs, now, n_x)
        at_field = far_field.at[now // n_x]
        at_kept = kept.at[now] if keep else None
        sample(unroll, chunks, now, base_ref, pass_ref, tab_ref, load, at_field, sums, at_kept)
        deliver(now, n_x, sums, out_refs)


def last_kernel(unroll, chunks, n_x, base_ref, pass_ref, tab_ref, *refs):
    groups = (len(refs) - 3) // 2
    in_refs, (kept, field_ref) = refs[:groups], refs[groups : groups + 2]
    out_refs, sums = refs[groups + 2 : -1], refs[-1]
    step = pl.program_id(0)
    load = loader(in_refs, step, n_x)
    sample(
        unroll, chunks, step, base_ref, pass_ref, tab_ref, load, field_ref.at[0], sums, kept.at[0]
    )
    deliver(step, n_x, sums, out_refs)


def tables(n_y, planes_y):
    def halves(value):
        value = value.astype(np.float32)
        high = value.astype(BF16)
        return high, (value - high.astype(np.float32)).astype(BF16)

    full = np.arange(N)
    reach = np.arange(LANES)
    line = np.concatenate([b * planes_y + reach - 1 for b in range(n_y)]) % N
    used = np.tile(reach < planes_y + 3, n_y)

    def table(rows, columns):
        angle = (rows[:, None] * columns[None, :] % N) * (2.0 * np.pi / N)
        return np.cos(angle) + np.sin(angle)

    high, low = halves(table(full, full))
    left = np.concatenate([high, low, high], axis=1)
    high, low = halves(table(line, full) * used[:, None])
    lines = np.concatenate([high, high, low], axis=0)
    high, low = halves(table(full, line) * used[None, :])
    return left, lines, np.concatenate([high, high, low], axis=0)


def symbol(index, size):
    sines = 2.0 * jnp.sin(jnp.pi * index.astype(F32) / size)
    return sines * sines


def green_of(freq_a, freq_b, freq_c, grid_size):
    total = (
        symbol(freq_a, grid_size)[:, None, None]
        + symbol(freq_b, grid_size)[None, :, None]
        + symbol(freq_c, grid_size)[None, None, :]
    )
    safe = jnp.where(total > 0, total, F32(1.0))
    return jnp.where(total > 0, jnp.exp(-0.5 * total) / safe, F32(0.0)) / float(
        grid_size * grid_size * grid_size
    )


def exchange(value, axis, distance, flip):
    size = lax.axis_size(axis)
    pairs = [(i, i ^ distance if flip else (i + distance) % size) for i in range(size)]
    return lax.ppermute(value, axis, pairs)


def gather_x(value):
    size = lax.axis_size("gx")
    if size > 8:
        return lax.all_gather(value, "gx")
    me = lax.axis_index("gx")
    parts = jnp.stack([value] + [exchange(value, "gx", s, False) for s in range(1, size)])
    return parts[(me - jnp.arange(size)) % size] if size > 1 else parts


def scatter_x(value):
    size = lax.axis_size("gx")
    if size > 8:
        return jnp.sum(lax.all_to_all(value, "gx", split_axis=0, concat_axis=0, tiled=True), axis=0)
    me = lax.axis_index("gx")
    total = lax.dynamic_index_in_dim(value, me, 0, keepdims=False)
    for s in range(1, size):
        part = lax.dynamic_index_in_dim(value, (me + s) % size, 0, keepdims=False)
        total = total + exchange(part, "gx", s, False)
    return total


def shards(cell_x, cell_y, cell_z, fraction, charge):
    count = charge.shape[0]
    n_x, n_y = lax.axis_size("gx"), lax.axis_size("gy")
    at_x, at_y = lax.axis_index("gx"), lax.axis_index("gy")
    planes_x, planes_y = N // n_x, N // n_y
    own = N // (n_x * n_y)
    chunks = count // LANES
    place = jnp.arange(count, dtype=jnp.int32)

    key, cy, cz, fx, fy, fz, q, order = lax.sort(
        (cell_x, cell_y, cell_z, fraction[0], fraction[1], fraction[2], charge, place),
        num_keys=1,
        is_stable=False,
    )
    plane = (key + at_x * planes_x).astype(F32)
    ends = plane.reshape(chunks, LANES)
    ends = jnp.concatenate([ends[:, 0], ends[:, -1], jnp.zeros((count - 2 * chunks,), F32)])
    packed = jnp.stack([plane, cy.astype(F32), cz.astype(F32), fx, fy, fz, q, ends])

    freq = (at_x * n_y + at_y) * own + jnp.arange(ROWS, dtype=jnp.int32)
    angle = freq.astype(F32) * F32(np.pi / N)
    far_cos, near_cos = jnp.cos(3 * angle), jnp.cos(angle)
    far_sin, near_sin = jnp.sin(3 * angle), jnp.sin(angle)
    tab = [
        (far_cos + 23 * near_cos) * F32(1 / 24),
        (far_cos - near_cos) * F32(1 / 2),
        (far_sin + 5 * near_sin) * F32(1 / 4),
        far_sin * F32(1 / 3) - near_sin,
        far_cos - near_cos,
        far_sin - 3 * near_sin,
        (freq % 2).astype(F32),
    ]
    tab = [jnp.broadcast_to(t[:, None], (ROWS, LANES)) for t in tab]
    cells = 2 * jnp.arange(LANES, dtype=jnp.int32) + 1
    turns = (freq[:, None] * cells[None, :] % (2 * N)).astype(F32) * F32(np.pi / N)
    turn_cos, turn_sin = jnp.cos(turns), jnp.sin(turns)
    tab = jnp.stack([turn_cos + turn_sin] + tab[:6] + [turn_cos - turn_sin] + tab[6:])
    tab = jnp.where((jnp.arange(ROWS) < own)[None, :, None], tab, F32(0.0))
    full = jnp.arange(N, dtype=jnp.int32)
    green = green_of(freq[:own], full, full, N)

    half = n_y // 2
    arrived, green, tab = lax.optimization_barrier((gather_x(packed), green, tab))
    groups = [arrived]
    for s in range(1, half + 1):
        step = s & -s
        groups.append(exchange(groups[s ^ step], "gy", step, True))

    unroll = 16 if chunks % 16 == 0 else 1
    longer = 32 if chunks % 32 == 0 else unroll
    size = N + PAD
    steps = half * n_x
    at_once = 4 if own % 4 == 0 else 1
    turns = own // at_once
    params = pltpu.CompilerParams(vmem_limit_bytes=56 * 1024 * 1024)

    def bounds(some):
        ends = jnp.concatenate([g[:, 7, : 2 * chunks] for g in some]).astype(jnp.int32)
        first, last = ends[:, :chunks].reshape(-1), ends[:, chunks:].reshape(-1)
        return first, (last - first + (3 + PLANES)) // PLANES

    def clamp(step, top):
        return jnp.minimum(jnp.maximum(step, 0), top)

    def charges(begins):
        def spec(g):
            def place(t, *_):
                at = 0
                for begin in begins:
                    at = jnp.where(t >= begin, clamp(t - begin - g * n_x, n_x - 1), at)
                return (at, 0, 0)

            return pl.BlockSpec((1, 8, count), place)

        return [spec(g) for g in range(half)]

    def whole(*shape):
        return pl.BlockSpec(shape, lambda *_: (0,) * len(shape))

    def results(begin):
        def spec(g):
            return pl.BlockSpec(
                (1, 4, count), lambda t, *_: (clamp(t - begin - g * n_x, n_x - 1), 0, 0)
            )

        return [spec(g) for g in range(half)]

    def estimate(passes):
        return pl.CostEstimate(
            flops=passes * steps * count * 600000,
            bytes_accessed=passes * steps * count * 160,
            transcendentals=0,
        )

    tab_spec = whole(TABLES, ROWS, LANES)
    mesh_shape = (half, size, ROWS, LANES)
    sums_shape = [jax.ShapeDtypeStruct((n_x, 4, count), F32)] * half
    sums_scratch = pltpu.VMEM((4, count), F32)
    near = groups[:half]
    near_bounds = bounds(near)

    kept_spec = pl.BlockSpec((1, 2 * ROWS, count), lambda t, *_: (t, 0, 0))
    kept_shape = jax.ShapeDtypeStruct((steps, 2 * ROWS, count), F32)
    near_mesh, near_kept = pl.pallas_call(
        functools.partial(near_kernel, longer, chunks, n_x),
        grid_spec=pltpu.PrefetchScalarGridSpec(
            num_scalar_prefetch=2,
            grid=(steps,),
            in_specs=[tab_spec] + charges([0]),
            out_specs=[
                pl.BlockSpec((1, size, ROWS, LANES), lambda t, *_: (t // n_x, 0, 0, 0)),
                kept_spec,
            ],
        ),
        out_shape=[jax.ShapeDtypeStruct(mesh_shape, F32), kept_shape],
        compiler_params=params,
        cost_estimate=estimate(1),
        name="near_spread",
    )(*near_bounds, tab, *near)

    near_mesh, arrived = lax.optimization_barrier((near_mesh, groups[half]))
    far = [arrived]
    for s in range(1, half):
        step = s & -s
        far.append(exchange(far[s ^ step], "gy", step, True))
    far_bounds = bounds(far)

    packs = steps + turns
    samples = packs + 2 * half
    near_field, *far_sums = pl.pallas_call(
        functools.partial(far_kernel, longer, unroll, chunks, n_x, turns),
        grid_spec=pltpu.PrefetchScalarGridSpec(
            num_scalar_prefetch=3,
            grid=(samples + steps,),
            in_specs=[tab_spec]
            + charges([0, samples])
            + [
                pl.BlockSpec(memory_space=pl.ANY),
                whole(N, 3 * N),
                whole(3 * n_y * LANES, N),
                whole(3 * N, n_y * LANES),
                pl.BlockSpec((at_once, N, N), lambda t, *_: (clamp(t - steps, turns - 1), 0, 0)),
            ],
            out_specs=[
                pl.BlockSpec(
                    (1, size * ROWS, N), lambda t, *_: (clamp(t - packs - half, half - 1), 0, 0)
                ),
            ]
            + results(samples),
            scratch_shapes=[
                pltpu.VMEM((n_y, size, ROWS, LANES), F32),
                pltpu.VMEM((half, size, ROWS, N), BF16),
                sums_scratch,
                pltpu.VMEM((steps if steps <= 8 else 1, 2 * ROWS, count), F32),
                pltpu.SemaphoreType.DMA((half,)),
            ],
        ),
        out_shape=[jax.ShapeDtypeStruct((half, size * ROWS, N), BF16)] + sums_shape,
        compiler_params=params,
        cost_estimate=estimate(3),
        name="far_spread_filter_sample",
    )(
        *far_bounds,
        at_y[None],
        tab,
        *far,
        near_mesh,
        *tables(n_y, planes_y),
        green,
    )

    *far_sums, near_field = lax.optimization_barrier((*far_sums, near_field))
    far_sums = [exchange(v, "gy", half, True) for v in far_sums]
    near_sums = pl.pallas_call(
        functools.partial(last_kernel, unroll, chunks, n_x),
        grid_spec=pltpu.PrefetchScalarGridSpec(
            num_scalar_prefetch=2,
            grid=(steps,),
            in_specs=[tab_spec]
            + charges([0])
            + [kept_spec, pl.BlockSpec((1, size, ROWS, N), lambda t, *_: (t // n_x, 0, 0, 0))],
            out_specs=results(0),
            scratch_shapes=[sums_scratch],
        ),
        out_shape=sums_shape,
        compiler_params=params,
        cost_estimate=estimate(1),
        name="near_sample",
    )(*near_bounds, tab, *near, near_kept, near_field.reshape(half, size, ROWS, N))

    sums = [near_sums[s] + far_sums[s] for s in range(half)]
    for s in range(half - 1, 0, -1):
        step = s & -s
        sums[s ^ step] = sums[s ^ step] + exchange(sums[s], "gy", step, True)
    total = scatter_x(sums[0])
    _, value, grad_x, grad_y, grad_z = lax.sort(
        (order, total[0], total[1], total[2], total[3]), num_keys=1, is_stable=False
    )
    return (value, -jnp.stack([grad_x, grad_y, grad_z], axis=0))


def solution(mesh):
    placed = P(("parts", "gx", "gy"))
    return jax.shard_map(
        shards,
        mesh=mesh,
        in_specs=(placed, placed, placed, P(None, ("parts", "gx", "gy")), placed),
        out_specs=(placed, P(None, ("parts", "gx", "gy"))),
        check_vma=False,
    )
```

```python
import functools

import jax
import jax.numpy as jnp
import numpy as np
from jax import lax
from jax.experimental import pallas as pl
from jax.experimental.pallas import tpu as pltpu
from jax.sharding import PartitionSpec as P

N = 256
LANES = 128
ROWS = 16
PLANES = 7
AHEAD = 1
FIELDS = 7
KEPT = 2 * ROWS + 8
TABLES = 9
PAD = 16
LINES = 80
F32 = jnp.float32
BF16 = jnp.bfloat16
NT = (((1,), (1,)), ((), ()))

def poly(coefficients, x):
    result = coefficients[-1]
    for value in coefficients[-2::-1]:
        result = result * x + value
    return result


SPLINE = (
    (1 / 6, 4 / 6, 1 / 6, 0.0),
    (-1 / 2, 0.0, 1 / 2, 0.0),
    (1 / 2, -1.0, 1 / 2, 0.0),
    (-1 / 6, 1 / 2, -1 / 2, 1 / 6),
)
SLOPES = ((-1 / 2, 0.0, 1 / 2, 0.0), (1.0, -2.0, 1.0, 0.0), (-1 / 2, 3 / 2, -3 / 2, 1 / 2))


def coefficients(table):
    place = iota(8)
    results = []
    for values in table:
        result = jnp.zeros((8, LANES), F32)
        for i, value in enumerate(values):
            result = jnp.where(place == i, F32(value), result)
        results.append(result)
    return results


def split(value):
    high = value.astype(BF16)
    return high, (value - high.astype(F32)).astype(BF16)


def wide(row, rows):
    return jnp.broadcast_to(row, (rows, row.shape[1]))


def iota(rows):
    return lax.broadcasted_iota(jnp.int32, (rows, LANES), 0)


def pick(options, index):
    return jnp.take_along_axis(options, index, axis=0)


def x_index(start, row_x):
    offset = iota(8) + (start - wide(row_x, 8).astype(jnp.int32))
    return jnp.minimum(offset & 0x7FFFFFFF, 7)


def rotation(tab, row_z):
    cell = wide(row_z, 8).astype(jnp.int32) & (LANES - 1)

    def look(table):
        tiles = [table[i : i + 8] for i in range(0, ROWS, 8)]
        return jnp.concatenate([jnp.take_along_axis(t, cell, axis=1) for t in tiles], axis=0)

    return look(tab[0]), look(tab[7])


def along_z(tab, plus, minus, middle, square):
    return (tab[1] + tab[2] * square) * plus + middle * (tab[3] + tab[4] * square) * minus


def slope_along_z(tab, plus, minus, middle, square):
    return (tab[5] * middle) * plus + (tab[3] + tab[6] * square) * minus


def along_y(row_y, options_list):
    cell = wide(row_y, 8).astype(jnp.int32)
    places = [iota(8), iota(8) + 8]
    index = [jnp.minimum((p - cell) & 15, 7) for p in places]
    tile = jnp.concatenate([(cell + (15 - p)) >> 4 for p in places], axis=0)
    tile = tile.astype(F32).astype(BF16)
    pieces = []
    for options in options_list:
        pieces += split(jnp.concatenate([pick(options, i) for i in index], axis=0))
    zero = jnp.zeros((16, LANES), BF16)
    results = [[] for _ in pieces]
    for t in range(LINES // 16):
        here = tile == BF16(t)
        for result, piece in zip(results, pieces):
            result.append(jnp.where(here, piece, zero))
    return [jnp.concatenate(r, axis=0) for r in results]


def lanes(parts):
    return parts[0] if len(parts) == 1 else jnp.concatenate(parts, axis=1)


def place_of(u):
    return pl.ds(pl.multiple_of(u * LANES, LANES), LANES)


def loader(refs, step, n_x):
    def load(u):
        chunks = refs[0].shape[1] // FIELDS
        where = pl.ds(u, FIELDS, chunks)
        rows = refs[0].at[0][where, :]
        for g in range(1, len(refs)):
            rows = jnp.where(step >= g * n_x, refs[g].at[0][where, :], rows)
        return rows

    return load


def rounds(unroll, chunks, begin, base_ref, pass_ref, prepare, finish):
    def some(i, most):
        waiting = []
        for u in range(unroll):
            index = begin + i * unroll + u
            most = jnp.maximum(most, pass_ref[index])
            chunk, start = i * unroll + u, base_ref[index]
            waiting.append((chunk, start, prepare(chunk, start, False)))
            if len(waiting) > AHEAD:
                finish(*waiting.pop(0), False)
        for item in waiting:
            finish(*item, False)
        return most

    most = lax.fori_loop(0, chunks // unroll, some, jnp.int32(1))

    @pl.when(most > 1)
    def _():
        def one(u, carry):
            def more(p, carry):
                start = base_ref[begin + u] + p * PLANES
                finish(u, start, prepare(u, start, True), True)
                return carry

            return lax.fori_loop(1, pass_ref[begin + u], more, carry)

        lax.fori_loop(0, chunks, one, 0)


def factors(rows, tab):
    plus, minus = rotation(tab, rows[2:3])
    middle = wide(rows[5:6] - 0.5, ROWS)
    square = middle * middle
    turned = tab[8] * (wide(rows[2:3], ROWS) >= F32(N // 2)).astype(F32)
    charge = wide(rows[6:7], ROWS) * (1.0 - 2.0 * turned)
    z = along_z(tab, plus, minus, middle, square) * charge
    return z, slope_along_z(tab, plus, minus, middle, square) * charge


def spread(unroll, chunks, step, base_ref, pass_ref, tab_ref, load, out_ref, kept):
    tab = [tab_ref[m] for m in range(TABLES)]
    cubic = coefficients(SPLINE)
    empty = jnp.zeros((LANES - LINES, LANES), BF16)

    def prepare(chunk, start, again):
        rows, place = load(chunk), place_of(chunk)
        z, z_slope = factors(rows, tab)
        if kept is not None and not again:
            kept[:ROWS, place] = z
            kept[ROWS : 2 * ROWS, place] = z_slope
            kept[2 * ROWS : 2 * ROWS + FIELDS, place] = rows
        high, low = along_y(rows[1:2], [poly(cubic, wide(rows[4:5], 8))])
        high, low = [jnp.concatenate([v, empty], axis=0) for v in (high, low)]
        lines = lanes([high, high, low])
        x = pick(poly(cubic, wide(rows[3:4], 8)), x_index(start, rows[0:1]))
        pieces = [split(wide(x[m : m + 1], ROWS) * z) for m in range(PLANES)]
        left = lanes([jnp.concatenate([p[k] for p in pieces], axis=0) for k in (0, 1, 0)])
        return lax.dot_general(left, lines, NT, preferred_element_type=F32)

    def finish(chunk, start, total, again):
        out_ref[pl.ds(start, PLANES)] += total.reshape(PLANES, ROWS, LANES)

    rounds(unroll, chunks, step * chunks, base_ref, pass_ref, prepare, finish)


def add_rows(terms):
    a, c, b, d = terms
    place = lax.broadcasted_iota(jnp.int32, (8, LANES), 0)
    low, even = place < 4, place & 2 == 0
    p = jnp.where(low, a, b) + pltpu.roll(jnp.where(low, b, a), 4, 0)
    q = jnp.where(low, c, d) + pltpu.roll(jnp.where(low, d, c), 4, 0)
    r = jnp.where(even, p, q) + jnp.where(even, pltpu.roll(p, 6, 0), pltpu.roll(q, 2, 0))
    r = r + pltpu.roll(r, 7, 0)
    return jnp.concatenate([r[i : i + 1] for i in (0, 2, 4, 6)], axis=0)


def sample(unroll, chunks, step, base_ref, pass_ref, tab_ref, load, field_ref, out_ref, kept):
    tab = None if tab_ref is None else [tab_ref[m] for m in range(TABLES)]
    cubic, quadratic = coefficients(SPLINE), coefficients(SLOPES)

    def prepare(chunk, start, again):
        rows = load(chunk) if kept is None else kept[2 * ROWS :, place_of(chunk)]
        part = wide(rows[4:5], 8)
        high, low, s_high, s_low = along_y(rows[1:2], [poly(cubic, part), poly(quadratic, part)])
        lines = lanes([stack_lines(high, low), stack_lines(s_high, s_low)])
        field = field_ref[pl.ds(start, PLANES)].reshape(PLANES * ROWS, N)
        return rows, jnp.dot(field, lines, preferred_element_type=F32)

    def finish(chunk, start, prepared, again):
        rows, sampled = prepared
        place = place_of(chunk)
        if kept is None:
            z, z_slope = factors(rows, tab)
        else:
            z, z_slope = kept[:ROWS, place], kept[ROWS : 2 * ROWS, place]
        part = wide(rows[3:4], 8)
        index = x_index(start, rows[0:1])
        x = pick(poly(cubic, part), index)
        x_slope = pick(poly(quadratic, part), index)
        both, by_x, by_y = [jnp.zeros((ROWS, LANES), F32) for _ in range(3)]
        for m in range(PLANES):
            v = sampled[m * ROWS : (m + 1) * ROWS, :LANES]
            g = sampled[m * ROWS : (m + 1) * ROWS, LANES:]
            wx = wide(x[m : m + 1], ROWS)
            both += v * wx
            by_x += v * wide(x_slope[m : m + 1], ROWS)
            by_y += g * wx
        terms = [both * z, by_x * z, by_y * z, both * z_slope]
        total = add_rows([t[:8] + t[8:] for t in terms])
        if again:
            total += out_ref[:, place]
        out_ref[:, place] = total

    rounds(unroll, chunks, step * chunks, base_ref, pass_ref, prepare, finish)


MORE = LANES - LINES


def stack_lines(high, low):
    zero = jnp.zeros((2 * LANES - 3 * LINES, LANES), BF16)
    return jnp.concatenate([high, low[MORE:], zero, high, low[:MORE]], axis=0)


def pack(field, out_ref):
    field[0:ROWS, :] = field[N * ROWS : (N + 1) * ROWS, :]
    field[(N + 1) * ROWS : (N + PAD) * ROWS, :] = field[ROWS : PAD * ROWS, :]
    size = (N + PAD) * ROWS // 4
    lane = lax.broadcasted_iota(jnp.int32, (size, LANES), 1)

    def part(i, carry):
        where = pl.ds(pl.multiple_of(i * size, size), size)
        value = field[where, :]
        high = value.astype(BF16).astype(F32)
        first = jnp.where(lane < LINES, high, pltpu.roll(high, LANES - MORE + LINES - LANES, 1))
        second = jnp.where(lane < LINES, value - high, pltpu.roll(high, LINES, 1))
        out_ref[where, :LANES] = first.astype(BF16)
        out_ref[where, LANES:] = second.astype(BF16)
        return carry

    lax.fori_loop(0, (N + PAD) * ROWS // size, part, 0)


def wrap(mesh_ref):
    mesh_ref[N] += mesh_ref[0]
    mesh_ref[1:3] += mesh_ref[N + 1 : N + 3]


def deliver(step, n_x, sums, out_refs):
    for g, out_ref in enumerate(out_refs):

        @pl.when(step // n_x == g)
        def _():
            out_ref[0] = sums[...]


def near_kernel(unroll, chunks, n_x, base_ref, pass_ref, tab_ref, *refs):
    in_refs, out_ref, kept = refs[:-2], refs[-2], refs[-1]
    step = pl.program_id(0)

    @pl.when(step % n_x == 0)
    def _():
        out_ref[...] = jnp.zeros_like(out_ref)

    load = loader(in_refs, step, n_x)
    spread(unroll, chunks, step, base_ref, pass_ref, tab_ref, load, out_ref.at[0], kept.at[0])

    @pl.when(step % n_x == n_x - 1)
    def _():
        wrap(out_ref.at[0])


def far_kernel(longer, unroll, chunks, n_x, turns, base_ref, pass_ref, at_ref, tab_ref, *refs):
    groups = (len(refs) - 11) // 2
    in_refs = refs[:groups]
    near_ref, table_ref, lines_ref, back_ref, green_ref = refs[groups : groups + 5]
    field_ref, out_refs = refs[groups + 5], refs[groups + 6 : -5]
    mesh, far_field, sums, kept, arrived = refs[-5:]
    keep = kept.shape[0] == groups * n_x
    step = pl.program_id(0)
    spreads = groups * n_x
    packs = spreads + turns
    samples = packs + 2 * groups
    slots = [at_ref[0] ^ s for s in range(2 * groups)]
    copies = [
        pltpu.make_async_copy(near_ref.at[g], mesh.at[slots[g]], arrived.at[g]) for g in range(groups)
    ]

    @pl.when(step == 0)
    def _():
        for copy in copies:
            copy.start()
        for slot in slots[groups:]:
            mesh[slot] = jnp.zeros(mesh.shape[1:], F32)

    @pl.when(step < spreads)
    def _():
        load = loader(in_refs, step, n_x)
        to = mesh.at[at_ref[0] ^ (groups + step // n_x)]
        at_kept = kept.at[step] if keep else None
        spread(longer, chunks, step, base_ref, pass_ref, tab_ref, load, to, at_kept)

    @pl.when(step == spreads)
    def _():
        for copy in copies:
            copy.wait()
        for slot in slots[groups:]:
            wrap(mesh.at[slot])

    flat = mesh.reshape(2 * groups, (N + PAD) * ROWS, LANES)

    @pl.when((step >= spreads) & (step < packs))
    def _():
        def right(value, matrix_ref):
            high, low = split(value)
            return jnp.dot(lanes([high, low, high]), matrix_ref[...], preferred_element_type=F32)

        def left(value):
            high, low = split(value)
            both = jnp.concatenate([high, high, low], axis=0)
            return jnp.dot(table_ref[...], both, preferred_element_type=F32)

        first_half = lax.broadcasted_iota(jnp.int32, (N, LANES), 1) < LANES // 2

        def lines_of(own, t):
            before, here, after = [
                flat.at[(2 * t + s) % (2 * groups)][own, :] for s in (-1, 0, 1)
            ]
            return here + pltpu.roll(jnp.where(first_half, after, before), LANES // 2, 1)

        at_once = green_ref.shape[0]
        begin = ROWS + (step - spreads) * at_once
        owns = [pl.ds(begin + u, N, ROWS) for u in range(at_once)]
        values = [lanes([lines_of(own, t) for t in range(groups)]) for own in owns]
        values = [right(v, lines_ref) for v in values]
        values = [left(v) * green_ref[u] for u, v in enumerate(values)]
        values = [left(v) for v in values]
        values = [right(v, back_ref) for v in values]
        for own, value in zip(owns, values):
            tiles = [value[:, t * LANES : (t + 1) * LANES] for t in range(groups)]
            for t in range(groups):
                flat.at[2 * t][own, :] = tiles[t]
                odd = jnp.where(first_half, tiles[(t + 1) % groups], tiles[t])
                flat.at[2 * t + 1][own, :] = pltpu.roll(odd, LANES // 2, 1)

    far_flat = far_field.reshape(groups, (N + PAD) * ROWS, N)

    @pl.when((step >= packs) & (step < packs + groups))
    def _():
        pack(flat.at[at_ref[0] ^ (groups + step - packs)], far_flat.at[step - packs])

    @pl.when((step >= packs + groups) & (step < samples))
    def _():
        pack(flat.at[at_ref[0] ^ (step - packs - groups)], field_ref.at[0])

    @pl.when(step >= samples)
    def _():
        now = step - samples
        load = loader(in_refs, now, n_x)
        at_field = far_field.at[now // n_x]
        at_kept = kept.at[now] if keep else None
        sample(unroll, chunks, now, base_ref, pass_ref, tab_ref, load, at_field, sums, at_kept)
        deliver(now, n_x, sums, out_refs)


def last_kernel(unroll, chunks, n_x, base_ref, pass_ref, kept, field_ref, *refs):
    out_refs, sums = refs[:-1], refs[-1]
    step = pl.program_id(0)
    sample(unroll, chunks, step, base_ref, pass_ref, None, None, field_ref.at[0], sums, kept.at[0])
    deliver(step, n_x, sums, out_refs)


def tables():
    def halves(value):
        value = value.astype(np.float32)
        high = value.astype(BF16)
        return high, (value - high.astype(np.float32)).astype(BF16)

    full = np.arange(N)
    line = (full - 1) % N

    def table(rows, columns):
        angle = (rows[:, None] * columns[None, :] % N) * (2.0 * np.pi / N)
        return np.cos(angle) + np.sin(angle)

    high, low = halves(table(full, full))
    left = np.concatenate([high, low, high], axis=1)
    high, low = halves(table(line, full))
    lines = np.concatenate([high, high, low], axis=0)
    high, low = halves(table(full, line))
    return left, lines, np.concatenate([high, high, low], axis=0)


def symbol(index, size):
    sines = 2.0 * jnp.sin(jnp.pi * index.astype(F32) / size)
    return sines * sines


def green_of(freq_a, freq_b, freq_c, grid_size):
    total = (
        symbol(freq_a, grid_size)[:, None, None]
        + symbol(freq_b, grid_size)[None, :, None]
        + symbol(freq_c, grid_size)[None, None, :]
    )
    safe = jnp.where(total > 0, total, F32(1.0))
    return jnp.where(total > 0, jnp.exp(-0.5 * total) / safe, F32(0.0)) / float(
        grid_size * grid_size * grid_size
    )


def exchange(value, axis, distance, flip):
    size = lax.axis_size(axis)
    pairs = [(i, i ^ distance if flip else (i + distance) % size) for i in range(size)]
    return lax.ppermute(value, axis, pairs)


def gather_x(value):
    size = lax.axis_size("gx")
    if size > 8:
        return lax.all_gather(value, "gx")
    me = lax.axis_index("gx")
    parts = jnp.stack([value] + [exchange(value, "gx", s, False) for s in range(1, size)])
    return parts[(me - jnp.arange(size)) % size] if size > 1 else parts


def scatter_x(value):
    size = lax.axis_size("gx")
    if size > 8:
        return jnp.sum(lax.all_to_all(value, "gx", split_axis=0, concat_axis=0, tiled=True), axis=0)
    me = lax.axis_index("gx")
    total = lax.dynamic_index_in_dim(value, me, 0, keepdims=False)
    for s in range(1, size):
        part = lax.dynamic_index_in_dim(value, (me + s) % size, 0, keepdims=False)
        total = total + exchange(part, "gx", s, False)
    return total


def shards(cell_x, cell_y, cell_z, fraction, charge):
    count = charge.shape[0]
    n_x, n_y = lax.axis_size("gx"), lax.axis_size("gy")
    at_x, at_y = lax.axis_index("gx"), lax.axis_index("gy")
    planes_x = N // n_x
    assert 2 * (N // n_y) == LANES
    own = N // (n_x * n_y)
    chunks = count // LANES
    place = jnp.arange(count, dtype=jnp.int32)

    key, cy, cz, fx, fy, fz, q, order = lax.sort(
        (cell_x, cell_y, cell_z, fraction[0], fraction[1], fraction[2], charge, place),
        num_keys=1,
        is_stable=False,
    )
    plane = (key + at_x * planes_x).astype(F32)
    sent = [plane, cy.astype(F32), cz.astype(F32), fx, fy, fz, q]
    packed = jnp.concatenate([v.reshape(chunks, LANES) for v in sent])

    freq = (at_x * n_y + at_y) * own + jnp.arange(ROWS, dtype=jnp.int32)
    angle = freq.astype(F32) * F32(np.pi / N)
    far_cos, near_cos = jnp.cos(3 * angle), jnp.cos(angle)
    far_sin, near_sin = jnp.sin(3 * angle), jnp.sin(angle)
    tab = [
        (far_cos + 23 * near_cos) * F32(1 / 24),
        (far_cos - near_cos) * F32(1 / 2),
        (far_sin + 5 * near_sin) * F32(1 / 4),
        far_sin * F32(1 / 3) - near_sin,
        far_cos - near_cos,
        far_sin - 3 * near_sin,
        (freq % 2).astype(F32),
    ]
    tab = [jnp.broadcast_to(t[:, None], (ROWS, LANES)) for t in tab]
    cells = 2 * jnp.arange(LANES, dtype=jnp.int32) + 1
    turns = (freq[:, None] * cells[None, :] % (2 * N)).astype(F32) * F32(np.pi / N)
    turn_cos, turn_sin = jnp.cos(turns), jnp.sin(turns)
    tab = jnp.stack([turn_cos + turn_sin] + tab[:6] + [turn_cos - turn_sin] + tab[6:])
    tab = jnp.where((jnp.arange(ROWS) < own)[None, :, None], tab, F32(0.0))
    full = jnp.arange(N, dtype=jnp.int32)
    green = green_of(freq[:own], full, full, N)

    half = n_y // 2
    arrived, green, tab = lax.optimization_barrier((gather_x(packed), green, tab))
    groups = [arrived]
    for s in range(1, half + 1):
        step = s & -s
        groups.append(exchange(groups[s ^ step], "gy", step, True))

    unroll = 16 if chunks % 16 == 0 else 1
    longer = 32 if chunks % 32 == 0 else unroll
    size = N + PAD
    steps = half * n_x
    at_once = 4 if own % 4 == 0 else 1
    turns = own // at_once
    params = pltpu.CompilerParams(vmem_limit_bytes=56 * 1024 * 1024)

    def bounds(some):
        planes = jnp.concatenate([g[:, :chunks] for g in some]).astype(jnp.int32)
        first, last = planes[:, :, 0].reshape(-1), planes[:, :, -1].reshape(-1)
        return first, (last - first + (3 + PLANES)) // PLANES

    def clamp(step, top):
        return jnp.minimum(jnp.maximum(step, 0), top)

    def charges(begins):
        def spec(g):
            def place(t, *_):
                at = 0
                for begin in begins:
                    at = jnp.where(t >= begin, clamp(t - begin - g * n_x, n_x - 1), at)
                return (at, 0, 0)

            return pl.BlockSpec((1, FIELDS * chunks, LANES), place)

        return [spec(g) for g in range(half)]

    def whole(*shape):
        return pl.BlockSpec(shape, lambda *_: (0,) * len(shape))

    def results(begin):
        def spec(g):
            return pl.BlockSpec(
                (1, 4, count), lambda t, *_: (clamp(t - begin - g * n_x, n_x - 1), 0, 0)
            )

        return [spec(g) for g in range(half)]

    def estimate(passes):
        return pl.CostEstimate(
            flops=passes * steps * count * 600000,
            bytes_accessed=passes * steps * count * 160,
            transcendentals=0,
        )

    tab_spec = whole(TABLES, ROWS, LANES)
    mesh_shape = (half, size, ROWS, LANES)
    sums_shape = [jax.ShapeDtypeStruct((n_x, 4, count), F32)] * half
    sums_scratch = pltpu.VMEM((4, count), F32)
    near = groups[:half]
    near_bounds = bounds(near)

    kept_spec = pl.BlockSpec((1, KEPT, count), lambda t, *_: (t, 0, 0))
    kept_shape = jax.ShapeDtypeStruct((steps, KEPT, count), F32)
    near_mesh, near_kept = pl.pallas_call(
        functools.partial(near_kernel, longer, chunks, n_x),
        grid_spec=pltpu.PrefetchScalarGridSpec(
            num_scalar_prefetch=2,
            grid=(steps,),
            in_specs=[tab_spec] + charges([0]),
            out_specs=[
                pl.BlockSpec((1, size, ROWS, LANES), lambda t, *_: (t // n_x, 0, 0, 0)),
                kept_spec,
            ],
        ),
        out_shape=[jax.ShapeDtypeStruct(mesh_shape, F32), kept_shape],
        compiler_params=params,
        cost_estimate=estimate(1),
        name="near_spread",
    )(*near_bounds, tab, *near)

    near_mesh, arrived = lax.optimization_barrier((near_mesh, groups[half]))
    far = [arrived]
    for s in range(1, half):
        step = s & -s
        far.append(exchange(far[s ^ step], "gy", step, True))
    far_bounds = bounds(far)

    packs = steps + turns
    samples = packs + 2 * half
    keep = steps <= 8
    near_field, *far_sums = pl.pallas_call(
        functools.partial(far_kernel, longer, unroll, chunks, n_x, turns),
        grid_spec=pltpu.PrefetchScalarGridSpec(
            num_scalar_prefetch=3,
            grid=(samples + steps,),
            in_specs=[tab_spec]
            + charges([0] if keep else [0, samples])
            + [
                pl.BlockSpec(memory_space=pl.ANY),
                whole(N, 3 * N),
                whole(3 * N, N),
                whole(3 * N, N),
                pl.BlockSpec((at_once, N, N), lambda t, *_: (clamp(t - steps, turns - 1), 0, 0)),
            ],
            out_specs=[
                pl.BlockSpec(
                    (1, size * ROWS, N), lambda t, *_: (clamp(t - packs - half, half - 1), 0, 0)
                ),
            ]
            + results(samples),
            scratch_shapes=[
                pltpu.VMEM((n_y, size, ROWS, LANES), F32),
                pltpu.VMEM((half, size, ROWS, N), BF16),
                sums_scratch,
                pltpu.VMEM((steps if keep else 1, KEPT, count), F32),
                pltpu.SemaphoreType.DMA((half,)),
            ],
        ),
        out_shape=[jax.ShapeDtypeStruct((half, size * ROWS, N), BF16)] + sums_shape,
        compiler_params=params,
        cost_estimate=estimate(3),
        name="far_spread_filter_sample",
    )(
        *far_bounds,
        at_y[None],
        tab,
        *far,
        near_mesh,
        *tables(),
        green,
    )

    *far_sums, near_field = lax.optimization_barrier((*far_sums, near_field))
    far_sums = [exchange(v, "gy", half, True) for v in far_sums]
    near_sums = pl.pallas_call(
        functools.partial(last_kernel, unroll, chunks, n_x),
        grid_spec=pltpu.PrefetchScalarGridSpec(
            num_scalar_prefetch=2,
            grid=(steps,),
            in_specs=[
                kept_spec,
                pl.BlockSpec((1, size, ROWS, N), lambda t, *_: (t // n_x, 0, 0, 0)),
            ],
            out_specs=results(0),
            scratch_shapes=[sums_scratch],
        ),
        out_shape=sums_shape,
        compiler_params=params,
        cost_estimate=estimate(1),
        name="near_sample",
    )(*near_bounds, near_kept, near_field.reshape(half, size, ROWS, N))

    sums = [near_sums[s] + far_sums[s] for s in range(half)]
    for s in range(half - 1, 0, -1):
        step = s & -s
        sums[s ^ step] = sums[s ^ step] + exchange(sums[s], "gy", step, True)
    total = scatter_x(sums[0])
    _, value, grad_x, grad_y, grad_z = lax.sort(
        (order, total[0], total[1], total[2], total[3]), num_keys=1, is_stable=False
    )
    return (value, -jnp.stack([grad_x, grad_y, grad_z], axis=0))


def solution(mesh):
    placed = P(("parts", "gx", "gy"))
    return jax.shard_map(
        shards,
        mesh=mesh,
        in_specs=(placed, placed, placed, P(None, ("parts", "gx", "gy")), placed),
        out_specs=(placed, P(None, ("parts", "gx", "gy"))),
        check_vma=False,
    )
```

```python
import functools

import jax
import jax.numpy as jnp
import numpy as np
from jax import lax
from jax.experimental import pallas as pl
from jax.experimental.pallas import tpu as pltpu
from jax.sharding import PartitionSpec as P

N = 256
LANES = 128
ROWS = 16
PLANES = 7
AHEAD = 1
FIELDS = 7
KEPT = 2 * ROWS + 8
TABLES = 9
PAD = 16
LINES = 80
F32 = jnp.float32
BF16 = jnp.bfloat16
NT = (((1,), (1,)), ((), ()))

def poly(coefficients, x):
    result = coefficients[-1]
    for value in coefficients[-2::-1]:
        result = result * x + value
    return result


SPLINE = (
    (1 / 6, 4 / 6, 1 / 6, 0.0),
    (-1 / 2, 0.0, 1 / 2, 0.0),
    (1 / 2, -1.0, 1 / 2, 0.0),
    (-1 / 6, 1 / 2, -1 / 2, 1 / 6),
)
SLOPES = ((-1 / 2, 0.0, 1 / 2, 0.0), (1.0, -2.0, 1.0, 0.0), (-1 / 2, 3 / 2, -3 / 2, 1 / 2))


def coefficients(table):
    place = iota(8)
    results = []
    for values in table:
        result = jnp.zeros((8, LANES), F32)
        for i, value in enumerate(values):
            result = jnp.where(place == i, F32(value), result)
        results.append(result)
    return results


def split(value):
    high = value.astype(BF16)
    return high, (value - high.astype(F32)).astype(BF16)


def wide(row, rows):
    return jnp.broadcast_to(row, (rows, row.shape[1]))


def iota(rows):
    return lax.broadcasted_iota(jnp.int32, (rows, LANES), 0)


def pick(options, index):
    return jnp.take_along_axis(options, index, axis=0)


def x_index(start, row_x):
    offset = iota(8) + (start - wide(row_x, 8).astype(jnp.int32))
    return jnp.minimum(offset & 0x7FFFFFFF, 7)


def rotation(tab, row_z):
    cell = wide(row_z, 8).astype(jnp.int32) & (LANES - 1)

    def look(table):
        tiles = [table[i : i + 8] for i in range(0, ROWS, 8)]
        return jnp.concatenate([jnp.take_along_axis(t, cell, axis=1) for t in tiles], axis=0)

    return look(tab[0]), look(tab[7])


def along_z(tab, plus, minus, middle, square):
    return (tab[1] + tab[2] * square) * plus + middle * (tab[3] + tab[4] * square) * minus


def slope_along_z(tab, plus, minus, middle, square):
    return (tab[5] * middle) * plus + (tab[3] + tab[6] * square) * minus


def along_y(row_y, options_list):
    cell = wide(row_y, 8).astype(jnp.int32)
    places = [iota(8), iota(8) + 8]
    index = [jnp.minimum((p - cell) & 15, 7) for p in places]
    tile = jnp.concatenate([(cell + (15 - p)) >> 4 for p in places], axis=0)
    tile = tile.astype(F32).astype(BF16)
    pieces = []
    for options in options_list:
        pieces += split(jnp.concatenate([pick(options, i) for i in index], axis=0))
    zero = jnp.zeros((16, LANES), BF16)
    results = [[] for _ in pieces]
    for t in range(LINES // 16):
        here = tile == BF16(t)
        for result, piece in zip(results, pieces):
            result.append(jnp.where(here, piece, zero))
    return [jnp.concatenate(r, axis=0) for r in results]


def lanes(parts):
    return parts[0] if len(parts) == 1 else jnp.concatenate(parts, axis=1)


def place_of(u):
    return pl.ds(pl.multiple_of(u * LANES, LANES), LANES)


def loader(refs, step, n_x):
    def load(u):
        chunks = refs[0].shape[1] // FIELDS
        where = pl.ds(u, FIELDS, chunks)
        rows = refs[0].at[0][where, :]
        for g in range(1, len(refs)):
            rows = jnp.where(step >= g * n_x, refs[g].at[0][where, :], rows)
        return rows

    return load


def rounds(unroll, chunks, step, base_ref, last_ref, prepare, finish):
    def some(i, most):
        waiting = []
        for u in range(unroll):
            chunk = i * unroll + u
            start = base_ref[step, chunk]
            most = jnp.maximum(most, last_ref[step, chunk] - start)
            waiting.append((chunk, start, prepare(chunk, start, False)))
            if len(waiting) > AHEAD:
                finish(*waiting.pop(0), False)
        for item in waiting:
            finish(*item, False)
        return most

    most = lax.fori_loop(0, chunks // unroll, some, jnp.int32(0))

    @pl.when(most + 4 > PLANES)
    def _():
        def one(u, carry):
            def more(p, carry):
                start = base_ref[step, u] + p * PLANES
                finish(u, start, prepare(u, start, True), True)
                return carry

            span = last_ref[step, u] - base_ref[step, u] + 4
            return lax.fori_loop(1, (span + PLANES - 1) // PLANES, more, carry)

        lax.fori_loop(0, chunks, one, 0)


def factors(rows, tab):
    plus, minus = rotation(tab, rows[2:3])
    middle = wide(rows[5:6] - 0.5, ROWS)
    square = middle * middle
    turned = tab[8] * (wide(rows[2:3], ROWS) >= F32(N // 2)).astype(F32)
    charge = wide(rows[6:7], ROWS) * (1.0 - 2.0 * turned)
    z = along_z(tab, plus, minus, middle, square) * charge
    return z, slope_along_z(tab, plus, minus, middle, square) * charge


def spread(unroll, chunks, step, base_ref, last_ref, tab_ref, load, out_ref, kept):
    tab = [tab_ref[m] for m in range(TABLES)]
    cubic = coefficients(SPLINE)
    empty = jnp.zeros((LANES - LINES, LANES), BF16)

    def prepare(chunk, start, again):
        rows, place = load(chunk), place_of(chunk)
        z, z_slope = factors(rows, tab)
        if kept is not None and not again:
            kept[:ROWS, place] = z
            kept[ROWS : 2 * ROWS, place] = z_slope
            kept[2 * ROWS : 2 * ROWS + FIELDS, place] = rows
        high, low = along_y(rows[1:2], [poly(cubic, wide(rows[4:5], 8))])
        high, low = [jnp.concatenate([v, empty], axis=0) for v in (high, low)]
        lines = lanes([high, high, low])
        x = pick(poly(cubic, wide(rows[3:4], 8)), x_index(start, rows[0:1]))
        pieces = [split(wide(x[m : m + 1], ROWS) * z) for m in range(PLANES)]
        left = lanes([jnp.concatenate([p[k] for p in pieces], axis=0) for k in (0, 1, 0)])
        return lax.dot_general(left, lines, NT, preferred_element_type=F32)

    def finish(chunk, start, total, again):
        out_ref[pl.ds(start, PLANES)] += total.reshape(PLANES, ROWS, LANES)

    rounds(unroll, chunks, step, base_ref, last_ref, prepare, finish)


def add_rows(terms):
    a, c, b, d = terms
    place = lax.broadcasted_iota(jnp.int32, (8, LANES), 0)
    low, even = place < 4, place & 2 == 0
    p = jnp.where(low, a, b) + pltpu.roll(jnp.where(low, b, a), 4, 0)
    q = jnp.where(low, c, d) + pltpu.roll(jnp.where(low, d, c), 4, 0)
    r = jnp.where(even, p, q) + jnp.where(even, pltpu.roll(p, 6, 0), pltpu.roll(q, 2, 0))
    r = r + pltpu.roll(r, 7, 0)
    return jnp.concatenate([r[i : i + 1] for i in (0, 2, 4, 6)], axis=0)


def sample(unroll, chunks, step, base_ref, last_ref, tab_ref, load, field_ref, out_ref, kept):
    tab = None if tab_ref is None else [tab_ref[m] for m in range(TABLES)]
    cubic, quadratic = coefficients(SPLINE), coefficients(SLOPES)

    def prepare(chunk, start, again):
        rows = load(chunk) if kept is None else kept[2 * ROWS :, place_of(chunk)]
        part = wide(rows[4:5], 8)
        high, low, s_high, s_low = along_y(rows[1:2], [poly(cubic, part), poly(quadratic, part)])
        lines = lanes([stack_lines(high, low), stack_lines(s_high, s_low)])
        field = field_ref[pl.ds(start, PLANES)].reshape(PLANES * ROWS, N)
        return rows, jnp.dot(field, lines, preferred_element_type=F32)

    def finish(chunk, start, prepared, again):
        rows, sampled = prepared
        place = place_of(chunk)
        if kept is None:
            z, z_slope = factors(rows, tab)
        else:
            z, z_slope = kept[:ROWS, place], kept[ROWS : 2 * ROWS, place]
        part = wide(rows[3:4], 8)
        index = x_index(start, rows[0:1])
        x = pick(poly(cubic, part), index)
        x_slope = pick(poly(quadratic, part), index)
        both, by_x, by_y = [jnp.zeros((ROWS, LANES), F32) for _ in range(3)]
        for m in range(PLANES):
            v = sampled[m * ROWS : (m + 1) * ROWS, :LANES]
            g = sampled[m * ROWS : (m + 1) * ROWS, LANES:]
            wx = wide(x[m : m + 1], ROWS)
            both += v * wx
            by_x += v * wide(x_slope[m : m + 1], ROWS)
            by_y += g * wx
        terms = [both * z, by_x * z, by_y * z, both * z_slope]
        total = add_rows([t[:8] + t[8:] for t in terms])
        if again:
            total += out_ref[:, place]
        out_ref[:, place] = total

    rounds(unroll, chunks, step, base_ref, last_ref, prepare, finish)


MORE = LANES - LINES


def stack_lines(high, low):
    zero = jnp.zeros((2 * LANES - 3 * LINES, LANES), BF16)
    return jnp.concatenate([high, low[MORE:], zero, high, low[:MORE]], axis=0)


def pack(field, out_ref):
    field[0:ROWS, :] = field[N * ROWS : (N + 1) * ROWS, :]
    field[(N + 1) * ROWS : (N + PAD) * ROWS, :] = field[ROWS : PAD * ROWS, :]
    size = (N + PAD) * ROWS // 4
    lane = lax.broadcasted_iota(jnp.int32, (size, LANES), 1)

    def part(i, carry):
        where = pl.ds(pl.multiple_of(i * size, size), size)
        value = field[where, :]
        high = value.astype(BF16).astype(F32)
        first = jnp.where(lane < LINES, high, pltpu.roll(high, LANES - MORE + LINES - LANES, 1))
        second = jnp.where(lane < LINES, value - high, pltpu.roll(high, LINES, 1))
        out_ref[where, :LANES] = first.astype(BF16)
        out_ref[where, LANES:] = second.astype(BF16)
        return carry

    lax.fori_loop(0, (N + PAD) * ROWS // size, part, 0)


def wrap(mesh_ref):
    mesh_ref[N] += mesh_ref[0]
    mesh_ref[1:3] += mesh_ref[N + 1 : N + 3]


def deliver(step, n_x, sums, out_refs):
    for g, out_ref in enumerate(out_refs):

        @pl.when(step // n_x == g)
        def _():
            out_ref[0] = sums[...]


def near_kernel(unroll, chunks, n_x, base_ref, last_ref, tab_ref, *refs):
    in_refs, out_ref, kept = refs[:-2], refs[-2], refs[-1]
    step = pl.program_id(0)

    @pl.when(step % n_x == 0)
    def _():
        out_ref[...] = jnp.zeros_like(out_ref)

    load = loader(in_refs, step, n_x)
    spread(unroll, chunks, step, base_ref, last_ref, tab_ref, load, out_ref.at[0], kept.at[0])

    @pl.when(step % n_x == n_x - 1)
    def _():
        wrap(out_ref.at[0])


def far_kernel(longer, unroll, chunks, n_x, at_once, turns, base_ref, last_ref, at_ref, tab_ref, *refs):
    groups = (len(refs) - 12) // 2
    in_refs = refs[:groups]
    near_ref, table_ref, lines_ref, back_ref, flat_ref, own_ref = refs[groups : groups + 6]
    field_ref, out_refs = refs[groups + 6], refs[groups + 7 : -5]
    mesh, far_field, sums, kept, arrived = refs[-5:]
    keep = kept.shape[0] == groups * n_x
    step = pl.program_id(0)
    spreads = groups * n_x
    packs = spreads + turns
    samples = packs + 2 * groups
    slots = [at_ref[0] ^ s for s in range(2 * groups)]
    copies = [
        pltpu.make_async_copy(near_ref.at[g], mesh.at[slots[g]], arrived.at[g]) for g in range(groups)
    ]

    @pl.when(step == 0)
    def _():
        for copy in copies:
            copy.start()
        for slot in slots[groups:]:
            mesh[slot] = jnp.zeros(mesh.shape[1:], F32)

    @pl.when(step < spreads)
    def _():
        load = loader(in_refs, step, n_x)
        to = mesh.at[at_ref[0] ^ (groups + step // n_x)]
        at_kept = kept.at[step] if keep else None
        spread(longer, chunks, step, base_ref, last_ref, tab_ref, load, to, at_kept)

    @pl.when(step == spreads)
    def _():
        for copy in copies:
            copy.wait()
        for slot in slots[groups:]:
            wrap(mesh.at[slot])

    flat = mesh.reshape(2 * groups, (N + PAD) * ROWS, LANES)

    @pl.when((step >= spreads) & (step < packs))
    def _():
        def right(value, matrix_ref):
            high, low = split(value)
            return jnp.dot(lanes([high, low, high]), matrix_ref[...], preferred_element_type=F32)

        def left(value):
            high, low = split(value)
            both = jnp.concatenate([high, high, low], axis=0)
            return jnp.dot(table_ref[...], both, preferred_element_type=F32)

        first_half = lax.broadcasted_iota(jnp.int32, (N, LANES), 1) < LANES // 2

        def green(k):
            total = flat_ref[0] + own_ref[0, pl.ds(k, 1), :]
            rest = flat_ref[1] * own_ref[1, pl.ds(k, 1), :]
            return jnp.where(total > 0, rest / jnp.where(total > 0, total, F32(1)), F32(0))

        def lines_of(own, t):
            before, here, after = [
                flat.at[(2 * t + s) % (2 * groups)][own, :] for s in (-1, 0, 1)
            ]
            return here + pltpu.roll(jnp.where(first_half, after, before), LANES // 2, 1)

        begin = (step - spreads) * at_once
        owns = [pl.ds(ROWS + begin + u, N, ROWS) for u in range(at_once)]
        values = [lanes([lines_of(own, t) for t in range(groups)]) for own in owns]
        values = [right(v, lines_ref) for v in values]
        values = [left(v) * green(begin + u) for u, v in enumerate(values)]
        values = [left(v) for v in values]
        values = [right(v, back_ref) for v in values]
        for own, value in zip(owns, values):
            tiles = [value[:, t * LANES : (t + 1) * LANES] for t in range(groups)]
            for t in range(groups):
                flat.at[2 * t][own, :] = tiles[t]
                odd = jnp.where(first_half, tiles[(t + 1) % groups], tiles[t])
                flat.at[2 * t + 1][own, :] = pltpu.roll(odd, LANES // 2, 1)

    far_flat = far_field.reshape(groups, (N + PAD) * ROWS, N)

    @pl.when((step >= packs) & (step < packs + groups))
    def _():
        pack(flat.at[at_ref[0] ^ (groups + step - packs)], far_flat.at[step - packs])

    @pl.when((step >= packs + groups) & (step < samples))
    def _():
        pack(flat.at[at_ref[0] ^ (step - packs - groups)], field_ref.at[0])

    @pl.when(step >= samples)
    def _():
        now = step - samples
        load = loader(in_refs, now, n_x)
        at_field = far_field.at[now // n_x]
        at_kept = kept.at[now] if keep else None
        sample(unroll, chunks, now, base_ref, last_ref, tab_ref, load, at_field, sums, at_kept)
        deliver(now, n_x, sums, out_refs)


def last_kernel(unroll, chunks, n_x, base_ref, last_ref, kept, field_ref, *refs):
    out_refs, sums = refs[:-1], refs[-1]
    step = pl.program_id(0)
    sample(unroll, chunks, step, base_ref, last_ref, None, None, field_ref.at[0], sums, kept.at[0])
    deliver(step, n_x, sums, out_refs)


def order_kernel(rank_ref, *refs):
    parts, (value_ref, force_ref, source) = refs[:-3], refs[-3:]
    chunks = rank_ref.shape[0]
    half = chunks // 2
    for t in range(half):
        pair = [sum(p[:, place * LANES : (place + 1) * LANES] for p in parts) for place in (t, t + half)]
        source[t] = jnp.concatenate(pair, axis=0)

    def one(o):
        rank = wide(rank_ref[pl.ds(o, 1), :], 8)
        lane, tile = rank & (LANES - 1), rank // LANES
        upper = tile >= half
        tile = jnp.where(upper, tile - half, tile)
        found = jnp.zeros((8, LANES), F32)
        for t in range(half):
            found = jnp.where(tile == t, jnp.take_along_axis(source[t], lane, axis=1), found)
        result = jnp.where(upper[:4], found[4:], found[:4])
        value_ref[pl.ds(o, 1), :] = result[:1]
        force_ref[:, place_of(o)] = -result[1:]

    at_once = 4 if chunks % 4 == 0 else 1

    def some(i, carry):
        for u in range(at_once):
            one(i * at_once + u)
        return carry

    lax.fori_loop(0, chunks // at_once, some, 0)


def tables():
    def halves(value):
        value = value.astype(np.float32)
        high = value.astype(BF16)
        return high, (value - high.astype(np.float32)).astype(BF16)

    full = np.arange(N)
    line = (full - 1) % N

    def table(rows, columns):
        angle = (rows[:, None] * columns[None, :] % N) * (2.0 * np.pi / N)
        return np.cos(angle) + np.sin(angle)

    high, low = halves(table(full, full))
    left = np.concatenate([high, low, high], axis=1)
    high, low = halves(table(line, full))
    lines = np.concatenate([high, high, low], axis=0)
    high, low = halves(table(full, line))
    symbols = (2 * np.sin(np.pi * full / N)) ** 2
    total = symbols[:, None] + symbols[None, :]
    shares = np.stack([total, np.exp(-0.5 * total) / float(N * N * N)]).astype(np.float32)
    return left, lines, np.concatenate([high, high, low], axis=0), shares


def symbol(index, size):
    sines = 2.0 * jnp.sin(jnp.pi * index.astype(F32) / size)
    return sines * sines


def exchange(value, axis, distance, flip):
    size = lax.axis_size(axis)
    pairs = [(i, i ^ distance if flip else (i + distance) % size) for i in range(size)]
    return lax.ppermute(value, axis, pairs)


def gather_x(value):
    size = lax.axis_size("gx")
    if size > 8:
        return lax.all_gather(value, "gx")
    me = lax.axis_index("gx")
    parts = jnp.stack([value] + [exchange(value, "gx", s, False) for s in range(1, size)])
    return parts[(me - jnp.arange(size)) % size] if size > 1 else parts


def scatter_x(value):
    size = lax.axis_size("gx")
    if size > 8:
        return [jnp.sum(lax.all_to_all(value, "gx", split_axis=0, concat_axis=0, tiled=True), axis=0)]
    me = lax.axis_index("gx")
    parts = [lax.dynamic_index_in_dim(value, me, 0, keepdims=False)]
    for s in range(1, size):
        part = lax.dynamic_index_in_dim(value, (me + s) % size, 0, keepdims=False)
        parts.append(exchange(part, "gx", s, False))
    return parts


def shards(cell_x, cell_y, cell_z, fraction, charge):
    count = charge.shape[0]
    n_x, n_y = lax.axis_size("gx"), lax.axis_size("gy")
    at_x, at_y = lax.axis_index("gx"), lax.axis_index("gy")
    planes_x = N // n_x
    assert 2 * (N // n_y) == LANES
    own = N // (n_x * n_y)
    chunks = count // LANES
    place = jnp.arange(count, dtype=jnp.int32)

    key, cy, cz, fx, fy, fz, q, order = lax.sort(
        (cell_x, cell_y, cell_z, fraction[0], fraction[1], fraction[2], charge, place),
        num_keys=1,
        is_stable=False,
    )
    plane = (key + at_x * planes_x).astype(F32)
    sent = [plane, cy.astype(F32), cz.astype(F32), fx, fy, fz, q]
    packed = jnp.concatenate([v.reshape(chunks, LANES) for v in sent])

    freq = (at_x * n_y + at_y) * own + jnp.arange(ROWS, dtype=jnp.int32)
    angle = freq.astype(F32) * F32(np.pi / N)
    far_cos, near_cos = jnp.cos(3 * angle), jnp.cos(angle)
    far_sin, near_sin = jnp.sin(3 * angle), jnp.sin(angle)
    tab = [
        (far_cos + 23 * near_cos) * F32(1 / 24),
        (far_cos - near_cos) * F32(1 / 2),
        (far_sin + 5 * near_sin) * F32(1 / 4),
        far_sin * F32(1 / 3) - near_sin,
        far_cos - near_cos,
        far_sin - 3 * near_sin,
        (freq % 2).astype(F32),
    ]
    tab = [jnp.broadcast_to(t[:, None], (ROWS, LANES)) for t in tab]
    cells = 2 * jnp.arange(LANES, dtype=jnp.int32) + 1
    turns = (freq[:, None] * cells[None, :] % (2 * N)).astype(F32) * F32(np.pi / N)
    turn_cos, turn_sin = jnp.cos(turns), jnp.sin(turns)
    tab = jnp.stack([turn_cos + turn_sin] + tab[:6] + [turn_cos - turn_sin] + tab[6:])
    tab = jnp.where((jnp.arange(ROWS) < own)[None, :, None], tab, F32(0.0))
    along_own = symbol(freq, N)
    own_share = jnp.stack([along_own, jnp.exp(-0.5 * along_own)])
    own_share = jnp.broadcast_to(own_share[:, :, None], (2, ROWS, N))

    half = n_y // 2
    _, rank = lax.sort((order, place), num_keys=1, is_stable=False)
    rank = rank.reshape(chunks, LANES)
    ready = (gather_x(packed), own_share, tab, rank)
    arrived, own_share, tab, rank = lax.optimization_barrier(ready)
    groups = [arrived]
    for s in range(1, half + 1):
        step = s & -s
        groups.append(exchange(groups[s ^ step], "gy", step, True))

    unroll = 16 if chunks % 16 == 0 else 1
    longer = 32 if chunks % 32 == 0 else unroll
    size = N + PAD
    steps = half * n_x
    at_once = 4 if own % 4 == 0 else 1
    turns = own // at_once
    params = pltpu.CompilerParams(vmem_limit_bytes=56 * 1024 * 1024)

    def bounds(some):
        planes = jnp.concatenate([g[:, :chunks] for g in some]).astype(jnp.int32)
        return planes[:, :, 0], planes[:, :, -1]

    def clamp(step, top):
        return jnp.minimum(jnp.maximum(step, 0), top)

    def charges(begins):
        def spec(g):
            def place(t, *_):
                at = 0
                for begin in begins:
                    at = jnp.where(t >= begin, clamp(t - begin - g * n_x, n_x - 1), at)
                return (at, 0, 0)

            return pl.BlockSpec((1, FIELDS * chunks, LANES), place)

        return [spec(g) for g in range(half)]

    def whole(*shape):
        return pl.BlockSpec(shape, lambda *_: (0,) * len(shape))

    def results(begin):
        def spec(g):
            return pl.BlockSpec(
                (1, 4, count), lambda t, *_: (clamp(t - begin - g * n_x, n_x - 1), 0, 0)
            )

        return [spec(g) for g in range(half)]

    def estimate(passes):
        return pl.CostEstimate(
            flops=passes * steps * count * 600000,
            bytes_accessed=passes * steps * count * 160,
            transcendentals=0,
        )

    tab_spec = whole(TABLES, ROWS, LANES)
    mesh_shape = (half, size, ROWS, LANES)
    sums_shape = [jax.ShapeDtypeStruct((n_x, 4, count), F32)] * half
    sums_scratch = pltpu.VMEM((4, count), F32)
    near = groups[:half]
    near_bounds = bounds(near)

    kept_spec = pl.BlockSpec((1, KEPT, count), lambda t, *_: (t, 0, 0))
    kept_shape = jax.ShapeDtypeStruct((steps, KEPT, count), F32)
    near_mesh, near_kept = pl.pallas_call(
        functools.partial(near_kernel, longer, chunks, n_x),
        grid_spec=pltpu.PrefetchScalarGridSpec(
            num_scalar_prefetch=2,
            grid=(steps,),
            in_specs=[tab_spec] + charges([0]),
            out_specs=[
                pl.BlockSpec((1, size, ROWS, LANES), lambda t, *_: (t // n_x, 0, 0, 0)),
                kept_spec,
            ],
        ),
        out_shape=[jax.ShapeDtypeStruct(mesh_shape, F32), kept_shape],
        compiler_params=params,
        cost_estimate=estimate(1),
        name="near_spread",
    )(*near_bounds, tab, *near)

    near_mesh, arrived = lax.optimization_barrier((near_mesh, groups[half]))
    far = [arrived]
    for s in range(1, half):
        step = s & -s
        far.append(exchange(far[s ^ step], "gy", step, True))
    far_bounds = bounds(far)

    packs = steps + turns
    samples = packs + 2 * half
    keep = steps <= 8
    near_field, *far_sums = pl.pallas_call(
        functools.partial(far_kernel, longer, unroll, chunks, n_x, at_once, turns),
        grid_spec=pltpu.PrefetchScalarGridSpec(
            num_scalar_prefetch=3,
            grid=(samples + steps,),
            in_specs=[tab_spec]
            + charges([0] if keep else [0, samples])
            + [
                pl.BlockSpec(memory_space=pl.ANY),
                whole(N, 3 * N),
                whole(3 * N, N),
                whole(3 * N, N),
                whole(2, N, N),
                whole(2, ROWS, N),
            ],
            out_specs=[
                pl.BlockSpec(
                    (1, size * ROWS, N), lambda t, *_: (clamp(t - packs - half, half - 1), 0, 0)
                ),
            ]
            + results(samples),
            scratch_shapes=[
                pltpu.VMEM((n_y, size, ROWS, LANES), F32),
                pltpu.VMEM((half, size, ROWS, N), BF16),
                sums_scratch,
                pltpu.VMEM((steps if keep else 1, KEPT, count), F32),
                pltpu.SemaphoreType.DMA((half,)),
            ],
        ),
        out_shape=[jax.ShapeDtypeStruct((half, size * ROWS, N), BF16)] + sums_shape,
        compiler_params=params,
        cost_estimate=estimate(3),
        name="far_spread_filter_sample",
    )(
        *far_bounds,
        at_y[None],
        tab,
        *far,
        near_mesh,
        *tables(),
        own_share,
    )

    *far_sums, near_field = lax.optimization_barrier((*far_sums, near_field))
    far_sums = [exchange(v, "gy", half, True) for v in far_sums]
    near_sums = pl.pallas_call(
        functools.partial(last_kernel, unroll, chunks, n_x),
        grid_spec=pltpu.PrefetchScalarGridSpec(
            num_scalar_prefetch=2,
            grid=(steps,),
            in_specs=[
                kept_spec,
                pl.BlockSpec((1, size, ROWS, N), lambda t, *_: (t // n_x, 0, 0, 0)),
            ],
            out_specs=results(0),
            scratch_shapes=[sums_scratch],
        ),
        out_shape=sums_shape,
        compiler_params=params,
        cost_estimate=estimate(1),
        name="near_sample",
    )(*near_bounds, near_kept, near_field.reshape(half, size, ROWS, N))

    sums = [near_sums[s] + far_sums[s] for s in range(half)]
    for s in range(half - 1, 0, -1):
        step = s & -s
        sums[s ^ step] = sums[s ^ step] + exchange(sums[s], "gy", step, True)
    parts = scatter_x(sums[0])
    value, forces = pl.pallas_call(
        order_kernel,
        out_shape=[
            jax.ShapeDtypeStruct((chunks, LANES), F32),
            jax.ShapeDtypeStruct((3, count), F32),
        ],
        scratch_shapes=[pltpu.VMEM((chunks // 2, 8, LANES), F32)],
        compiler_params=params,
        name="order",
    )(rank, *parts)
    return (value.reshape(count), forces)


def solution(mesh):
    placed = P(("parts", "gx", "gy"))
    return jax.shard_map(
        shards,
        mesh=mesh,
        in_specs=(placed, placed, placed, P(None, ("parts", "gx", "gy")), placed),
        out_specs=(placed, P(None, ("parts", "gx", "gy"))),
        check_vma=False,
    )
```

```python
import functools

import jax
import jax.numpy as jnp
import numpy as np
from jax import lax
from jax.experimental import pallas as pl
from jax.experimental.pallas import tpu as pltpu
from jax.sharding import PartitionSpec as P

N = 256
LANES = 128
ROWS = 16
PLANES = 7
AHEAD = 1
FIELDS = 7
KEPT = 2 * ROWS + 8
TABLES = 11
PAD = 16
LINES = 80
F32 = jnp.float32
BF16 = jnp.bfloat16
NT = (((1,), (1,)), ((), ()))

def poly(coefficients, x):
    result = coefficients[-1]
    for value in coefficients[-2::-1]:
        result = result * x + value
    return result


SPLINE = (
    (1 / 6, 4 / 6, 1 / 6, 0.0),
    (-1 / 2, 0.0, 1 / 2, 0.0),
    (1 / 2, -1.0, 1 / 2, 0.0),
    (-1 / 6, 1 / 2, -1 / 2, 1 / 6),
)
SLOPES = ((-1 / 2, 0.0, 1 / 2, 0.0), (1.0, -2.0, 1.0, 0.0), (-1 / 2, 3 / 2, -3 / 2, 1 / 2))


def coefficients(table):
    place = iota(8)
    results = []
    for values in table:
        result = jnp.zeros((8, LANES), F32)
        for i, value in enumerate(values):
            result = jnp.where(place == i, F32(value), result)
        results.append(result)
    return results


def split(value):
    high = value.astype(BF16)
    return high, (value - high.astype(F32)).astype(BF16)


def wide(row, rows):
    return jnp.broadcast_to(row, (rows, row.shape[1]))


def iota(rows):
    return lax.broadcasted_iota(jnp.int32, (rows, LANES), 0)


def pick(options, index):
    return jnp.take_along_axis(options, index, axis=0)


def x_index(start, row_x):
    offset = iota(8) + (start - wide(row_x, 8).astype(jnp.int32))
    return jnp.minimum(offset & 0x7FFFFFFF, 7)


def rotation(tab, row_z):
    cell = wide(row_z, 8).astype(jnp.int32) & (LANES - 1)

    def look(table):
        tiles = [table[i : i + 8] for i in range(0, ROWS, 8)]
        return jnp.concatenate([jnp.take_along_axis(t, cell, axis=1) for t in tiles], axis=0)

    return look(tab[0]), look(tab[7])


def along_z(tab, plus, minus, middle, square):
    return (tab[1] + tab[2] * square) * plus + middle * (tab[3] + tab[4] * square) * minus


def slope_along_z(tab, plus, minus, middle, square):
    return (tab[5] * middle) * plus + (tab[3] + tab[6] * square) * minus


def along_y(row_y, options_list):
    cell = wide(row_y, 8).astype(jnp.int32)
    places = [iota(8), iota(8) + 8]
    index = [jnp.minimum((p - cell) & 15, 7) for p in places]
    tile = jnp.concatenate([(cell + (15 - p)) >> 4 for p in places], axis=0)
    tile = tile.astype(F32).astype(BF16)
    pieces = []
    for options in options_list:
        pieces += split(jnp.concatenate([pick(options, i) for i in index], axis=0))
    zero = jnp.zeros((16, LANES), BF16)
    results = [[] for _ in pieces]
    for t in range(LINES // 16):
        here = tile == BF16(t)
        for result, piece in zip(results, pieces):
            result.append(jnp.where(here, piece, zero))
    return [jnp.concatenate(r, axis=0) for r in results]


def lanes(parts):
    return parts[0] if len(parts) == 1 else jnp.concatenate(parts, axis=1)


def place_of(u):
    return pl.ds(pl.multiple_of(u * LANES, LANES), LANES)


def loader(refs, step, n_x):
    def load(u):
        chunks = refs[0].shape[1] // FIELDS
        where = pl.ds(u, FIELDS, chunks)
        rows = refs[0].at[0][where, :]
        for g in range(1, len(refs)):
            rows = jnp.where(step >= g * n_x, refs[g].at[0][where, :], rows)
        return rows

    return load


def rounds(unroll, chunks, step, base_ref, last_ref, prepare, finish):
    def some(i, most):
        waiting = []
        for u in range(unroll):
            chunk = i * unroll + u
            start = base_ref[step, chunk]
            most = jnp.maximum(most, last_ref[step, chunk] - start)
            waiting.append((chunk, start, prepare(chunk, start, False)))
            if len(waiting) > AHEAD:
                finish(*waiting.pop(0), False)
        for item in waiting:
            finish(*item, False)
        return most

    most = lax.fori_loop(0, chunks // unroll, some, jnp.int32(0))

    @pl.when(most + 4 > PLANES)
    def _():
        def one(u, carry):
            def more(p, carry):
                start = base_ref[step, u] + p * PLANES
                finish(u, start, prepare(u, start, True), True)
                return carry

            span = last_ref[step, u] - base_ref[step, u] + 4
            return lax.fori_loop(1, (span + PLANES - 1) // PLANES, more, carry)

        lax.fori_loop(0, chunks, one, 0)


def factors(rows, tab):
    plus, minus = rotation(tab, rows[2:3])
    middle = wide(rows[5:6] - 0.5, ROWS)
    square = middle * middle
    turned = tab[8] * (wide(rows[2:3], ROWS) >= F32(N // 2)).astype(F32)
    charge = wide(rows[6:7], ROWS) * (1.0 - 2.0 * turned)
    z = along_z(tab, plus, minus, middle, square) * charge
    return z, slope_along_z(tab, plus, minus, middle, square) * charge


def spread(unroll, chunks, step, base_ref, last_ref, tab_ref, load, out_ref, kept):
    tab = [tab_ref[m] for m in range(TABLES)]
    cubic = coefficients(SPLINE)
    empty = jnp.zeros((LANES - LINES, LANES), BF16)

    def prepare(chunk, start, again):
        rows, place = load(chunk), place_of(chunk)
        z, z_slope = factors(rows, tab)
        if kept is not None and not again:
            kept[:ROWS, place] = z
            kept[ROWS : 2 * ROWS, place] = z_slope
            kept[2 * ROWS : 2 * ROWS + FIELDS, place] = rows
        high, low = along_y(rows[1:2], [poly(cubic, wide(rows[4:5], 8))])
        high, low = [jnp.concatenate([v, empty], axis=0) for v in (high, low)]
        lines = lanes([high, high, low])
        x = pick(poly(cubic, wide(rows[3:4], 8)), x_index(start, rows[0:1]))
        pieces = [split(wide(x[m : m + 1], ROWS) * z) for m in range(PLANES)]
        left = lanes([jnp.concatenate([p[k] for p in pieces], axis=0) for k in (0, 1, 0)])
        return lax.dot_general(left, lines, NT, preferred_element_type=F32)

    def finish(chunk, start, total, again):
        out_ref[pl.ds(start, PLANES)] += total.reshape(PLANES, ROWS, LANES)

    rounds(unroll, chunks, step, base_ref, last_ref, prepare, finish)


def add_rows(terms):
    a, c, b, d = terms
    place = lax.broadcasted_iota(jnp.int32, (8, LANES), 0)
    low, even = place < 4, place & 2 == 0
    p = jnp.where(low, a, b) + pltpu.roll(jnp.where(low, b, a), 4, 0)
    q = jnp.where(low, c, d) + pltpu.roll(jnp.where(low, d, c), 4, 0)
    r = jnp.where(even, p, q) + jnp.where(even, pltpu.roll(p, 6, 0), pltpu.roll(q, 2, 0))
    r = r + pltpu.roll(r, 7, 0)
    return jnp.concatenate([r[i : i + 1] for i in (0, 2, 4, 6)], axis=0)


def sample(unroll, chunks, step, base_ref, last_ref, tab_ref, load, field_ref, out_ref, kept):
    tab = None if tab_ref is None else [tab_ref[m] for m in range(TABLES)]
    cubic, quadratic = coefficients(SPLINE), coefficients(SLOPES)

    def prepare(chunk, start, again):
        rows = load(chunk) if kept is None else kept[2 * ROWS :, place_of(chunk)]
        part = wide(rows[4:5], 8)
        high, low, s_high, s_low = along_y(rows[1:2], [poly(cubic, part), poly(quadratic, part)])
        lines = lanes([stack_lines(high, low), stack_lines(s_high, s_low)])
        field = field_ref[pl.ds(start, PLANES)].reshape(PLANES * ROWS, N)
        return rows, jnp.dot(field, lines, preferred_element_type=F32)

    def finish(chunk, start, prepared, again):
        rows, sampled = prepared
        place = place_of(chunk)
        if kept is None:
            z, z_slope = factors(rows, tab)
        else:
            z, z_slope = kept[:ROWS, place], kept[ROWS : 2 * ROWS, place]
        part = wide(rows[3:4], 8)
        index = x_index(start, rows[0:1])
        x = pick(poly(cubic, part), index)
        x_slope = pick(poly(quadratic, part), index)
        both, by_x, by_y = [jnp.zeros((ROWS, LANES), F32) for _ in range(3)]
        for m in range(PLANES):
            v = sampled[m * ROWS : (m + 1) * ROWS, :LANES]
            g = sampled[m * ROWS : (m + 1) * ROWS, LANES:]
            wx = wide(x[m : m + 1], ROWS)
            both += v * wx
            by_x += v * wide(x_slope[m : m + 1], ROWS)
            by_y += g * wx
        terms = [both * z, by_x * z, by_y * z, both * z_slope]
        total = add_rows([t[:8] + t[8:] for t in terms])
        if again:
            total += out_ref[:, place]
        out_ref[:, place] = total

    rounds(unroll, chunks, step, base_ref, last_ref, prepare, finish)


MORE = LANES - LINES


def stack_lines(high, low):
    zero = jnp.zeros((2 * LANES - 3 * LINES, LANES), BF16)
    return jnp.concatenate([high, low[MORE:], zero, high, low[:MORE]], axis=0)


def pack(field, out_ref):
    field[0:ROWS, :] = field[N * ROWS : (N + 1) * ROWS, :]
    field[(N + 1) * ROWS : (N + PAD) * ROWS, :] = field[ROWS : PAD * ROWS, :]
    size = (N + PAD) * ROWS // 4
    lane = lax.broadcasted_iota(jnp.int32, (size, LANES), 1)

    def part(i, carry):
        where = pl.ds(pl.multiple_of(i * size, size), size)
        value = field[where, :]
        high = value.astype(BF16).astype(F32)
        first = jnp.where(lane < LINES, high, pltpu.roll(high, LANES - MORE + LINES - LANES, 1))
        second = jnp.where(lane < LINES, value - high, pltpu.roll(high, LINES, 1))
        out_ref[where, :LANES] = first.astype(BF16)
        out_ref[where, LANES:] = second.astype(BF16)
        return carry

    lax.fori_loop(0, (N + PAD) * ROWS // size, part, 0)


def wrap(mesh_ref):
    mesh_ref[N] += mesh_ref[0]
    mesh_ref[1:3] += mesh_ref[N + 1 : N + 3]


def deliver(step, n_x, sums, out_refs):
    for g, out_ref in enumerate(out_refs):

        @pl.when(step // n_x == g)
        def _():
            out_ref[0] = sums[...]


def near_kernel(unroll, chunks, n_x, base_ref, last_ref, tab_ref, *refs):
    in_refs, out_ref, kept = refs[:-2], refs[-2], refs[-1]
    step = pl.program_id(0)

    @pl.when(step % n_x == 0)
    def _():
        out_ref[...] = jnp.zeros_like(out_ref)

    load = loader(in_refs, step, n_x)
    spread(unroll, chunks, step, base_ref, last_ref, tab_ref, load, out_ref.at[0], kept.at[0])

    @pl.when(step % n_x == n_x - 1)
    def _():
        wrap(out_ref.at[0])


def far_kernel(longer, unroll, chunks, n_x, at_once, turns, base_ref, last_ref, at_ref, tab_ref, *refs):
    groups = (len(refs) - 11) // 2
    in_refs = refs[:groups]
    near_ref, table_ref, lines_ref, back_ref, flat_ref = refs[groups : groups + 5]
    field_ref, out_refs = refs[groups + 5], refs[groups + 6 : -5]
    mesh, far_field, sums, kept, arrived = refs[-5:]
    keep = kept.shape[0] == groups * n_x
    step = pl.program_id(0)
    spreads = groups * n_x
    packs = spreads + turns
    samples = packs + 2 * groups
    slots = [at_ref[0] ^ s for s in range(2 * groups)]
    copies = [
        pltpu.make_async_copy(near_ref.at[g], mesh.at[slots[g]], arrived.at[g]) for g in range(groups)
    ]

    @pl.when(step == 0)
    def _():
        for copy in copies:
            copy.start()
        for slot in slots[groups:]:
            mesh[slot] = jnp.zeros(mesh.shape[1:], F32)

    @pl.when(step < spreads)
    def _():
        load = loader(in_refs, step, n_x)
        to = mesh.at[at_ref[0] ^ (groups + step // n_x)]
        at_kept = kept.at[step] if keep else None
        spread(longer, chunks, step, base_ref, last_ref, tab_ref, load, to, at_kept)

    @pl.when(step == spreads)
    def _():
        for copy in copies:
            copy.wait()
        for slot in slots[groups:]:
            wrap(mesh.at[slot])

    flat = mesh.reshape(2 * groups, (N + PAD) * ROWS, LANES)

    @pl.when((step >= spreads) & (step < packs))
    def _():
        def right(value, matrix_ref):
            high, low = split(value)
            return jnp.dot(lanes([high, low, high]), matrix_ref[...], preferred_element_type=F32)

        def left(value):
            high, low = split(value)
            both = jnp.concatenate([high, high, low], axis=0)
            return jnp.dot(table_ref[...], both, preferred_element_type=F32)

        first_half = lax.broadcasted_iota(jnp.int32, (N, LANES), 1) < LANES // 2

        def green(k):
            share = [lanes([tab_ref[m, pl.ds(k, 1), :]] * (N // LANES)) for m in (9, 10)]
            total, rest = flat_ref[0] + share[0], flat_ref[1] * share[1]
            return jnp.where(total > 0, rest / jnp.where(total > 0, total, F32(1)), F32(0))

        def lines_of(own, t):
            before, here, after = [
                flat.at[(2 * t + s) % (2 * groups)][own, :] for s in (-1, 0, 1)
            ]
            return here + pltpu.roll(jnp.where(first_half, after, before), LANES // 2, 1)

        begin = (step - spreads) * at_once
        owns = [pl.ds(ROWS + begin + u, N, ROWS) for u in range(at_once)]
        values = [lanes([lines_of(own, t) for t in range(groups)]) for own in owns]
        values = [right(v, lines_ref) for v in values]
        values = [left(v) * green(begin + u) for u, v in enumerate(values)]
        values = [left(v) for v in values]
        values = [right(v, back_ref) for v in values]
        for own, value in zip(owns, values):
            tiles = [value[:, t * LANES : (t + 1) * LANES] for t in range(groups)]
            for t in range(groups):
                flat.at[2 * t][own, :] = tiles[t]
                odd = jnp.where(first_half, tiles[(t + 1) % groups], tiles[t])
                flat.at[2 * t + 1][own, :] = pltpu.roll(odd, LANES // 2, 1)

    far_flat = far_field.reshape(groups, (N + PAD) * ROWS, N)

    @pl.when((step >= packs) & (step < packs + groups))
    def _():
        pack(flat.at[at_ref[0] ^ (groups + step - packs)], far_flat.at[step - packs])

    @pl.when((step >= packs + groups) & (step < samples))
    def _():
        pack(flat.at[at_ref[0] ^ (step - packs - groups)], field_ref.at[0])

    @pl.when(step >= samples)
    def _():
        now = step - samples
        load = loader(in_refs, now, n_x)
        at_field = far_field.at[now // n_x]
        at_kept = kept.at[now] if keep else None
        sample(unroll, chunks, now, base_ref, last_ref, tab_ref, load, at_field, sums, at_kept)
        deliver(now, n_x, sums, out_refs)


def last_kernel(unroll, chunks, n_x, base_ref, last_ref, kept, field_ref, *refs):
    out_refs, sums = refs[:-1], refs[-1]
    step = pl.program_id(0)
    sample(unroll, chunks, step, base_ref, last_ref, None, None, field_ref.at[0], sums, kept.at[0])
    deliver(step, n_x, sums, out_refs)


def order_kernel(rank_ref, *refs):
    parts, (value_ref, force_ref, source) = refs[:-3], refs[-3:]
    chunks = rank_ref.shape[0]
    half = chunks // 2
    for t in range(half):
        pair = [sum(p[:, place * LANES : (place + 1) * LANES] for p in parts) for place in (t, t + half)]
        source[t] = jnp.concatenate(pair, axis=0)

    def one(o):
        rank = wide(rank_ref[pl.ds(o, 1), :], 8)
        lane, tile = rank & (LANES - 1), rank // LANES
        upper = tile >= half
        tile = jnp.where(upper, tile - half, tile)
        found = jnp.zeros((8, LANES), F32)
        for t in range(half):
            found = jnp.where(tile == t, jnp.take_along_axis(source[t], lane, axis=1), found)
        result = jnp.where(upper[:4], found[4:], found[:4])
        value_ref[pl.ds(o, 1), :] = result[:1]
        force_ref[:, place_of(o)] = -result[1:]

    at_once = 4 if chunks % 4 == 0 else 1

    def some(i, carry):
        for u in range(at_once):
            one(i * at_once + u)
        return carry

    lax.fori_loop(0, chunks // at_once, some, 0)


def tables():
    def halves(value):
        value = value.astype(np.float32)
        high = value.astype(BF16)
        return high, (value - high.astype(np.float32)).astype(BF16)

    full = np.arange(N)
    line = (full - 1) % N

    def table(rows, columns):
        angle = (rows[:, None] * columns[None, :] % N) * (2.0 * np.pi / N)
        return np.cos(angle) + np.sin(angle)

    high, low = halves(table(full, full))
    left = np.concatenate([high, low, high], axis=1)
    high, low = halves(table(line, full))
    lines = np.concatenate([high, high, low], axis=0)
    high, low = halves(table(full, line))
    symbols = (2 * np.sin(np.pi * full / N)) ** 2
    total = symbols[:, None] + symbols[None, :]
    shares = np.stack([total, np.exp(-0.5 * total) / float(N * N * N)]).astype(np.float32)
    return left, lines, np.concatenate([high, high, low], axis=0), shares


def symbol(index, size):
    sines = 2.0 * jnp.sin(jnp.pi * index.astype(F32) / size)
    return sines * sines


def exchange(value, axis, distance, flip):
    size = lax.axis_size(axis)
    pairs = [(i, i ^ distance if flip else (i + distance) % size) for i in range(size)]
    return lax.ppermute(value, axis, pairs)


def gather_x(value):
    size = lax.axis_size("gx")
    if size > 8:
        return lax.all_gather(value, "gx")
    me = lax.axis_index("gx")
    parts = jnp.stack([value] + [exchange(value, "gx", s, False) for s in range(1, size)])
    return parts[(me - jnp.arange(size)) % size] if size > 1 else parts


def scatter_x(value):
    size = lax.axis_size("gx")
    if size > 8:
        return [jnp.sum(lax.all_to_all(value, "gx", split_axis=0, concat_axis=0, tiled=True), axis=0)]
    me = lax.axis_index("gx")
    parts = [lax.dynamic_index_in_dim(value, me, 0, keepdims=False)]
    for s in range(1, size):
        part = lax.dynamic_index_in_dim(value, (me + s) % size, 0, keepdims=False)
        parts.append(exchange(part, "gx", s, False))
    return parts


def shards(cell_x, cell_y, cell_z, fraction, charge):
    count = charge.shape[0]
    n_x, n_y = lax.axis_size("gx"), lax.axis_size("gy")
    at_x, at_y = lax.axis_index("gx"), lax.axis_index("gy")
    planes_x = N // n_x
    assert 2 * (N // n_y) == LANES
    own = N // (n_x * n_y)
    chunks = count // LANES
    place = jnp.arange(count, dtype=jnp.int32)

    key, cy, cz, fx, fy, fz, q, order = lax.sort(
        (cell_x, cell_y, cell_z, fraction[0], fraction[1], fraction[2], charge, place),
        num_keys=1,
        is_stable=False,
    )
    plane = (key + at_x * planes_x).astype(F32)
    sent = [plane, cy.astype(F32), cz.astype(F32), fx, fy, fz, q]
    packed = jnp.concatenate([v.reshape(chunks, LANES) for v in sent])

    freq = (at_x * n_y + at_y) * own + jnp.arange(ROWS, dtype=jnp.int32)
    angle = freq.astype(F32) * F32(np.pi / N)
    far_cos, near_cos = jnp.cos(3 * angle), jnp.cos(angle)
    far_sin, near_sin = jnp.sin(3 * angle), jnp.sin(angle)
    along_own = symbol(freq, N)
    tab = [
        (far_cos + 23 * near_cos) * F32(1 / 24),
        (far_cos - near_cos) * F32(1 / 2),
        (far_sin + 5 * near_sin) * F32(1 / 4),
        far_sin * F32(1 / 3) - near_sin,
        far_cos - near_cos,
        far_sin - 3 * near_sin,
        (freq % 2).astype(F32),
        along_own,
        jnp.exp(-0.5 * along_own),
    ]
    tab = [jnp.broadcast_to(t[:, None], (ROWS, LANES)) for t in tab]
    cells = 2 * jnp.arange(LANES, dtype=jnp.int32) + 1
    turns = (freq[:, None] * cells[None, :] % (2 * N)).astype(F32) * F32(np.pi / N)
    turn_cos, turn_sin = jnp.cos(turns), jnp.sin(turns)
    tab = jnp.stack([turn_cos + turn_sin] + tab[:6] + [turn_cos - turn_sin] + tab[6:])
    tab = jnp.where((jnp.arange(ROWS) < own)[None, :, None], tab, F32(0.0))

    half = n_y // 2
    _, rank = lax.sort((order, place), num_keys=1, is_stable=False)
    rank = rank.reshape(chunks, LANES)
    arrived, tab, rank = lax.optimization_barrier((gather_x(packed), tab, rank))
    groups = [arrived]
    for s in range(1, half + 1):
        step = s & -s
        groups.append(exchange(groups[s ^ step], "gy", step, True))

    unroll = 16 if chunks % 16 == 0 else 1
    longer = 32 if chunks % 32 == 0 else unroll
    size = N + PAD
    steps = half * n_x
    at_once = 4 if own % 4 == 0 else 1
    turns = own // at_once
    params = pltpu.CompilerParams(vmem_limit_bytes=56 * 1024 * 1024)

    def bounds(some):
        planes = jnp.concatenate([g[:, :chunks] for g in some]).astype(jnp.int32)
        return planes[:, :, 0], planes[:, :, -1]

    def clamp(step, top):
        return jnp.minimum(jnp.maximum(step, 0), top)

    def charges(begins):
        def spec(g):
            def place(t, *_):
                at = 0
                for begin in begins:
                    at = jnp.where(t >= begin, clamp(t - begin - g * n_x, n_x - 1), at)
                return (at, 0, 0)

            return pl.BlockSpec((1, FIELDS * chunks, LANES), place)

        return [spec(g) for g in range(half)]

    def whole(*shape):
        return pl.BlockSpec(shape, lambda *_: (0,) * len(shape))

    def results(begin):
        def spec(g):
            return pl.BlockSpec(
                (1, 4, count), lambda t, *_: (clamp(t - begin - g * n_x, n_x - 1), 0, 0)
            )

        return [spec(g) for g in range(half)]

    def estimate(passes):
        return pl.CostEstimate(
            flops=passes * steps * count * 600000,
            bytes_accessed=passes * steps * count * 160,
            transcendentals=0,
        )

    tab_spec = whole(TABLES, ROWS, LANES)
    mesh_shape = (half, size, ROWS, LANES)
    sums_shape = [jax.ShapeDtypeStruct((n_x, 4, count), F32)] * half
    sums_scratch = pltpu.VMEM((4, count), F32)
    near = groups[:half]
    near_bounds = bounds(near)

    kept_spec = pl.BlockSpec((1, KEPT, count), lambda t, *_: (t, 0, 0))
    kept_shape = jax.ShapeDtypeStruct((steps, KEPT, count), F32)
    near_mesh, near_kept = pl.pallas_call(
        functools.partial(near_kernel, longer, chunks, n_x),
        grid_spec=pltpu.PrefetchScalarGridSpec(
            num_scalar_prefetch=2,
            grid=(steps,),
            in_specs=[tab_spec] + charges([0]),
            out_specs=[
                pl.BlockSpec((1, size, ROWS, LANES), lambda t, *_: (t // n_x, 0, 0, 0)),
                kept_spec,
            ],
        ),
        out_shape=[jax.ShapeDtypeStruct(mesh_shape, F32), kept_shape],
        compiler_params=params,
        cost_estimate=estimate(1),
        name="near_spread",
    )(*near_bounds, tab, *near)

    near_mesh, arrived = lax.optimization_barrier((near_mesh, groups[half]))
    far = [arrived]
    for s in range(1, half):
        step = s & -s
        far.append(exchange(far[s ^ step], "gy", step, True))
    far_bounds = bounds(far)

    packs = steps + turns
    samples = packs + 2 * half
    keep = steps <= 8
    near_field, *far_sums = pl.pallas_call(
        functools.partial(far_kernel, longer, unroll, chunks, n_x, at_once, turns),
        grid_spec=pltpu.PrefetchScalarGridSpec(
            num_scalar_prefetch=3,
            grid=(samples + steps,),
            in_specs=[tab_spec]
            + charges([0] if keep else [0, samples])
            + [
                pl.BlockSpec(memory_space=pl.ANY),
                whole(N, 3 * N),
                whole(3 * N, N),
                whole(3 * N, N),
                whole(2, N, N),
            ],
            out_specs=[
                pl.BlockSpec(
                    (1, size * ROWS, N), lambda t, *_: (clamp(t - packs - half, half - 1), 0, 0)
                ),
            ]
            + results(samples),
            scratch_shapes=[
                pltpu.VMEM((n_y, size, ROWS, LANES), F32),
                pltpu.VMEM((half, size, ROWS, N), BF16),
                sums_scratch,
                pltpu.VMEM((steps if keep else 1, KEPT, count), F32),
                pltpu.SemaphoreType.DMA((half,)),
            ],
        ),
        out_shape=[jax.ShapeDtypeStruct((half, size * ROWS, N), BF16)] + sums_shape,
        compiler_params=params,
        cost_estimate=estimate(3),
        name="far_spread_filter_sample",
    )(
        *far_bounds,
        at_y[None],
        tab,
        *far,
        near_mesh,
        *tables(),
    )

    *far_sums, near_field = lax.optimization_barrier((*far_sums, near_field))
    far_sums = [exchange(v, "gy", half, True) for v in far_sums]
    near_sums = pl.pallas_call(
        functools.partial(last_kernel, unroll, chunks, n_x),
        grid_spec=pltpu.PrefetchScalarGridSpec(
            num_scalar_prefetch=2,
            grid=(steps,),
            in_specs=[
                kept_spec,
                pl.BlockSpec((1, size, ROWS, N), lambda t, *_: (t // n_x, 0, 0, 0)),
            ],
            out_specs=results(0),
            scratch_shapes=[sums_scratch],
        ),
        out_shape=sums_shape,
        compiler_params=params,
        cost_estimate=estimate(1),
        name="near_sample",
    )(*near_bounds, near_kept, near_field.reshape(half, size, ROWS, N))

    sums = [near_sums[s] + far_sums[s] for s in range(half)]
    for s in range(half - 1, 0, -1):
        step = s & -s
        sums[s ^ step] = sums[s ^ step] + exchange(sums[s], "gy", step, True)
    parts = scatter_x(sums[0])
    value, forces = pl.pallas_call(
        order_kernel,
        out_shape=[
            jax.ShapeDtypeStruct((chunks, LANES), F32),
            jax.ShapeDtypeStruct((3, count), F32),
        ],
        scratch_shapes=[pltpu.VMEM((chunks // 2, 8, LANES), F32)],
        compiler_params=params,
        name="order",
    )(rank, *parts)
    return (value.reshape(count), forces)


def solution(mesh):
    placed = P(("parts", "gx", "gy"))
    return jax.shard_map(
        shards,
        mesh=mesh,
        in_specs=(placed, placed, placed, P(None, ("parts", "gx", "gy")), placed),
        out_specs=(placed, P(None, ("parts", "gx", "gy"))),
        check_vma=False,
    )
```

```python
import functools

import jax
import jax.numpy as jnp
import numpy as np
from jax import lax
from jax.experimental import pallas as pl
from jax.experimental.pallas import tpu as pltpu
from jax.sharding import PartitionSpec as P

N = 256
LANES = 128
ROWS = 16
PLANES = 7
AHEAD = 1
FIELDS = 7
KEPT = 2 * ROWS + 8
TABLES = 11
PAD = 16
LINES = 80
F32 = jnp.float32
BF16 = jnp.bfloat16
NT = (((1,), (1,)), ((), ()))

def poly(coefficients, x):
    result = coefficients[-1]
    for value in coefficients[-2::-1]:
        result = result * x + value
    return result


SPLINE = (
    (1 / 6, 4 / 6, 1 / 6, 0.0),
    (-1 / 2, 0.0, 1 / 2, 0.0),
    (1 / 2, -1.0, 1 / 2, 0.0),
    (-1 / 6, 1 / 2, -1 / 2, 1 / 6),
)
SLOPES = ((-1 / 2, 0.0, 1 / 2, 0.0), (1.0, -2.0, 1.0, 0.0), (-1 / 2, 3 / 2, -3 / 2, 1 / 2))


def coefficients(table):
    place = iota(8)
    results = []
    for values in table:
        result = jnp.zeros((8, LANES), F32)
        for i, value in enumerate(values):
            result = jnp.where(place == i, F32(value), result)
        results.append(result)
    return results


def split(value):
    high = value.astype(BF16)
    return high, (value - high.astype(F32)).astype(BF16)


def wide(row, rows):
    return jnp.broadcast_to(row, (rows, row.shape[1]))


def iota(rows):
    return lax.broadcasted_iota(jnp.int32, (rows, LANES), 0)


def pick(options, index):
    return jnp.take_along_axis(options, index, axis=0)


def x_index(start, row_x):
    offset = iota(8) + (start - wide(row_x, 8).astype(jnp.int32))
    return jnp.minimum(offset & 0x7FFFFFFF, 7)


def rotation(tab, row_z):
    cell = wide(row_z, 8).astype(jnp.int32) & (LANES - 1)

    def look(table):
        tiles = [table[i : i + 8] for i in range(0, ROWS, 8)]
        return jnp.concatenate([jnp.take_along_axis(t, cell, axis=1) for t in tiles], axis=0)

    return look(tab[0]), look(tab[7])


def along_z(tab, plus, minus, middle, square):
    return (tab[1] + tab[2] * square) * plus + middle * (tab[3] + tab[4] * square) * minus


def slope_along_z(tab, plus, minus, middle, square):
    return (tab[5] * middle) * plus + (tab[3] + tab[6] * square) * minus


def along_y(row_y, options_list):
    cell = wide(row_y, 8).astype(jnp.int32)
    places = [iota(8), iota(8) + 8]
    index = [jnp.minimum((p - cell) & 15, 7) for p in places]
    tile = jnp.concatenate([(cell + (15 - p)) >> 4 for p in places], axis=0)
    tile = tile.astype(F32).astype(BF16)
    pieces = []
    for options in options_list:
        pieces += split(jnp.concatenate([pick(options, i) for i in index], axis=0))
    zero = jnp.zeros((16, LANES), BF16)
    results = [[] for _ in pieces]
    for t in range(LINES // 16):
        here = tile == BF16(t)
        for result, piece in zip(results, pieces):
            result.append(jnp.where(here, piece, zero))
    return [jnp.concatenate(r, axis=0) for r in results]


def lanes(parts):
    return parts[0] if len(parts) == 1 else jnp.concatenate(parts, axis=1)


def place_of(u):
    return pl.ds(pl.multiple_of(u * LANES, LANES), LANES)


def loader(refs, step, n_x):
    def load(u):
        chunks = refs[0].shape[1] // FIELDS
        where = pl.ds(u, FIELDS, chunks)
        rows = refs[0].at[0][where, :]
        for g in range(1, len(refs)):
            rows = jnp.where(step >= g * n_x, refs[g].at[0][where, :], rows)
        return rows

    return load


def rounds(unroll, chunks, step, base_ref, last_ref, prepare, finish):
    def some(i, most):
        waiting = []
        for u in range(unroll):
            chunk = i * unroll + u
            start = base_ref[step, chunk]
            most = jnp.maximum(most, last_ref[step, chunk] - start)
            waiting.append((chunk, start, prepare(chunk, start, False)))
            if len(waiting) > AHEAD:
                finish(*waiting.pop(0), False)
        for item in waiting:
            finish(*item, False)
        return most

    most = lax.fori_loop(0, chunks // unroll, some, jnp.int32(0))

    @pl.when(most + 4 > PLANES)
    def _():
        def one(u, carry):
            def more(p, carry):
                start = base_ref[step, u] + p * PLANES
                finish(u, start, prepare(u, start, True), True)
                return carry

            span = last_ref[step, u] - base_ref[step, u] + 4
            return lax.fori_loop(1, (span + PLANES - 1) // PLANES, more, carry)

        lax.fori_loop(0, chunks, one, 0)


def factors(rows, tab):
    plus, minus = rotation(tab, rows[2:3])
    middle = wide(rows[5:6] - 0.5, ROWS)
    square = middle * middle
    turned = tab[8] * (wide(rows[2:3], ROWS) >= F32(N // 2)).astype(F32)
    charge = wide(rows[6:7], ROWS) * (1.0 - 2.0 * turned)
    z = along_z(tab, plus, minus, middle, square) * charge
    return z, slope_along_z(tab, plus, minus, middle, square) * charge


def spread(unroll, chunks, step, base_ref, last_ref, tab_ref, load, out_ref, kept):
    tab = [tab_ref[m] for m in range(TABLES)]
    cubic = coefficients(SPLINE)
    empty = jnp.zeros((LANES - LINES, LANES), BF16)

    def prepare(chunk, start, again):
        rows, place = load(chunk), place_of(chunk)
        z, z_slope = factors(rows, tab)
        if kept is not None and not again:
            kept[:ROWS, place] = z
            kept[ROWS : 2 * ROWS, place] = z_slope
            kept[2 * ROWS : 2 * ROWS + FIELDS, place] = rows
        high, low = along_y(rows[1:2], [poly(cubic, wide(rows[4:5], 8))])
        high, low = [jnp.concatenate([v, empty], axis=0) for v in (high, low)]
        lines = lanes([high, high, low])
        x = pick(poly(cubic, wide(rows[3:4], 8)), x_index(start, rows[0:1]))
        pieces = [split(wide(x[m : m + 1], ROWS) * z) for m in range(PLANES)]
        left = lanes([jnp.concatenate([p[k] for p in pieces], axis=0) for k in (0, 1, 0)])
        return lax.dot_general(left, lines, NT, preferred_element_type=F32)

    def finish(chunk, start, total, again):
        out_ref[pl.ds(start, PLANES)] += total.reshape(PLANES, ROWS, LANES)

    rounds(unroll, chunks, step, base_ref, last_ref, prepare, finish)


def add_rows(terms):
    a, c, b, d = terms
    place = lax.broadcasted_iota(jnp.int32, (8, LANES), 0)
    low, even = place < 4, place & 2 == 0
    p = jnp.where(low, a, b) + pltpu.roll(jnp.where(low, b, a), 4, 0)
    q = jnp.where(low, c, d) + pltpu.roll(jnp.where(low, d, c), 4, 0)
    r = jnp.where(even, p, q) + jnp.where(even, pltpu.roll(p, 6, 0), pltpu.roll(q, 2, 0))
    r = r + pltpu.roll(r, 7, 0)
    return jnp.concatenate([r[i : i + 1] for i in (0, 2, 4, 6)], axis=0)


def sample(unroll, chunks, step, base_ref, last_ref, tab_ref, load, field_ref, out_ref, kept):
    tab = None if tab_ref is None else [tab_ref[m] for m in range(TABLES)]
    cubic, quadratic = coefficients(SPLINE), coefficients(SLOPES)

    def prepare(chunk, start, again):
        rows = load(chunk) if kept is None else kept[2 * ROWS :, place_of(chunk)]
        part = wide(rows[4:5], 8)
        high, low, s_high, s_low = along_y(rows[1:2], [poly(cubic, part), poly(quadratic, part)])
        lines = lanes([stack_lines(high, low), stack_lines(s_high, s_low)])
        field = field_ref[pl.ds(start, PLANES)].reshape(PLANES * ROWS, N)
        return rows, jnp.dot(field, lines, preferred_element_type=F32)

    def finish(chunk, start, prepared, again):
        rows, sampled = prepared
        place = place_of(chunk)
        if kept is None:
            z, z_slope = factors(rows, tab)
        else:
            z, z_slope = kept[:ROWS, place], kept[ROWS : 2 * ROWS, place]
        part = wide(rows[3:4], 8)
        index = x_index(start, rows[0:1])
        x = pick(poly(cubic, part), index)
        x_slope = pick(poly(quadratic, part), index)
        both, by_x, by_y = [jnp.zeros((ROWS, LANES), F32) for _ in range(3)]
        for m in range(PLANES):
            v = sampled[m * ROWS : (m + 1) * ROWS, :LANES]
            g = sampled[m * ROWS : (m + 1) * ROWS, LANES:]
            wx = wide(x[m : m + 1], ROWS)
            both += v * wx
            by_x += v * wide(x_slope[m : m + 1], ROWS)
            by_y += g * wx
        terms = [both * z, by_x * z, by_y * z, both * z_slope]
        total = add_rows([t[:8] + t[8:] for t in terms])
        if again:
            total += out_ref[:, place]
        out_ref[:, place] = total

    rounds(unroll, chunks, step, base_ref, last_ref, prepare, finish)


MORE = LANES - LINES


def stack_lines(high, low):
    zero = jnp.zeros((2 * LANES - 3 * LINES, LANES), BF16)
    return jnp.concatenate([high, low[MORE:], zero, high, low[:MORE]], axis=0)


def pack(field, out_ref):
    field[0:ROWS, :] = field[N * ROWS : (N + 1) * ROWS, :]
    field[(N + 1) * ROWS : (N + PAD) * ROWS, :] = field[ROWS : PAD * ROWS, :]
    size = (N + PAD) * ROWS // 4
    lane = lax.broadcasted_iota(jnp.int32, (size, LANES), 1)

    def part(i, carry):
        where = pl.ds(pl.multiple_of(i * size, size), size)
        value = field[where, :]
        high = value.astype(BF16).astype(F32)
        first = jnp.where(lane < LINES, high, pltpu.roll(high, LANES - MORE + LINES - LANES, 1))
        second = jnp.where(lane < LINES, value - high, pltpu.roll(high, LINES, 1))
        out_ref[where, :LANES] = first.astype(BF16)
        out_ref[where, LANES:] = second.astype(BF16)
        return carry

    lax.fori_loop(0, (N + PAD) * ROWS // size, part, 0)


def wrap(mesh_ref):
    mesh_ref[N] += mesh_ref[0]
    mesh_ref[1:3] += mesh_ref[N + 1 : N + 3]


def deliver(step, n_x, sums, out_refs):
    for g, out_ref in enumerate(out_refs):

        @pl.when(step // n_x == g)
        def _():
            out_ref[0] = sums[...]


def near_kernel(unroll, chunks, n_x, base_ref, last_ref, tab_ref, *refs):
    in_refs, out_ref, kept = refs[:-2], refs[-2], refs[-1]
    step = pl.program_id(0)

    @pl.when(step % n_x == 0)
    def _():
        out_ref[...] = jnp.zeros_like(out_ref)

    load = loader(in_refs, step, n_x)
    spread(unroll, chunks, step, base_ref, last_ref, tab_ref, load, out_ref.at[0], kept.at[0])

    @pl.when(step % n_x == n_x - 1)
    def _():
        wrap(out_ref.at[0])


def far_kernel(longer, unroll, chunks, n_x, at_once, turns, base_ref, last_ref, at_ref, tab_ref, *refs):
    groups = (len(refs) - 11) // 2
    in_refs = refs[:groups]
    near_ref, table_ref, lines_ref, back_ref, flat_ref = refs[groups : groups + 5]
    field_ref, out_refs = refs[groups + 5], refs[groups + 6 : -5]
    mesh, far_field, sums, kept, arrived = refs[-5:]
    keep = kept.shape[0] == groups * n_x
    step = pl.program_id(0)
    spreads = groups * n_x
    packs = spreads + turns
    samples = packs + 1 + groups
    slots = [at_ref[0] ^ s for s in range(2 * groups)]
    copies = [
        pltpu.make_async_copy(near_ref.at[g], mesh.at[slots[g]], arrived.at[g]) for g in range(groups)
    ]

    @pl.when(step == 0)
    def _():
        for copy in copies:
            copy.start()
        for slot in slots[groups:]:
            mesh[slot] = jnp.zeros(mesh.shape[1:], F32)

    @pl.when(step < spreads)
    def _():
        load = loader(in_refs, step, n_x)
        to = mesh.at[at_ref[0] ^ (groups + step // n_x)]
        at_kept = kept.at[step] if keep else None
        spread(longer, chunks, step, base_ref, last_ref, tab_ref, load, to, at_kept)

    @pl.when(step == spreads)
    def _():
        for copy in copies:
            copy.wait()
        for slot in slots[groups:]:
            wrap(mesh.at[slot])

    flat = mesh.reshape(2 * groups, (N + PAD) * ROWS, LANES)

    @pl.when((step >= spreads) & (step < packs))
    def _():
        def right(value, matrix_ref):
            high, low = split(value)
            return jnp.dot(lanes([high, low, high]), matrix_ref[...], preferred_element_type=F32)

        def left(value):
            high, low = split(value)
            both = jnp.concatenate([high, high, low], axis=0)
            return jnp.dot(table_ref[...], both, preferred_element_type=F32)

        first_half = lax.broadcasted_iota(jnp.int32, (N, LANES), 1) < LANES // 2

        def green(k):
            share = [lanes([tab_ref[m, pl.ds(k, 1), :]] * (N // LANES)) for m in (9, 10)]
            total, rest = flat_ref[0] + share[0], flat_ref[1] * share[1]
            return jnp.where(total > 0, rest / jnp.where(total > 0, total, F32(1)), F32(0))

        def lines_of(own, t):
            before, here, after = [
                flat.at[(2 * t + s) % (2 * groups)][own, :] for s in (-1, 0, 1)
            ]
            return here + pltpu.roll(jnp.where(first_half, after, before), LANES // 2, 1)

        begin = (step - spreads) * at_once
        owns = [pl.ds(ROWS + begin + u, N, ROWS) for u in range(at_once)]
        values = [lanes([lines_of(own, t) for t in range(groups)]) for own in owns]
        values = [right(v, lines_ref) for v in values]
        values = [left(v) * green(begin + u) for u, v in enumerate(values)]
        values = [left(v) for v in values]
        values = [right(v, back_ref) for v in values]
        for own, value in zip(owns, values):
            tiles = [value[:, t * LANES : (t + 1) * LANES] for t in range(groups)]
            for t in range(groups):
                flat.at[2 * t][own, :] = tiles[t]
                odd = jnp.where(first_half, tiles[(t + 1) % groups], tiles[t])
                flat.at[2 * t + 1][own, :] = pltpu.roll(odd, LANES // 2, 1)

    far_flat = far_field.reshape(groups, (N + PAD) * ROWS, N)

    @pl.when(step == packs)
    def _():
        for g in range(groups):
            pack(flat.at[slots[groups + g]], far_flat.at[g])

    @pl.when((step > packs) & (step < samples))
    def _():
        pack(flat.at[at_ref[0] ^ (step - packs - 1)], field_ref.at[0])

    @pl.when(step >= samples)
    def _():
        now = step - samples
        load = loader(in_refs, now, n_x)
        at_field = far_field.at[now // n_x]
        at_kept = kept.at[now] if keep else None
        sample(unroll, chunks, now, base_ref, last_ref, tab_ref, load, at_field, sums, at_kept)
        deliver(now, n_x, sums, out_refs)


def last_kernel(unroll, chunks, n_x, base_ref, last_ref, kept, field_ref, *refs):
    out_refs, sums = refs[:-1], refs[-1]
    step = pl.program_id(0)
    sample(unroll, chunks, step, base_ref, last_ref, None, None, field_ref.at[0], sums, kept.at[0])
    deliver(step, n_x, sums, out_refs)


def order_kernel(rank_ref, *refs):
    parts, (value_ref, force_ref, source) = refs[:-3], refs[-3:]
    chunks = rank_ref.shape[0]
    half = chunks // 2
    for t in range(half):
        pair = [sum(p[:, place * LANES : (place + 1) * LANES] for p in parts) for place in (t, t + half)]
        source[t] = jnp.concatenate(pair, axis=0)

    def one(o):
        rank = wide(rank_ref[pl.ds(o, 1), :], 8)
        lane, tile = rank & (LANES - 1), rank // LANES
        upper = tile >= half
        tile = jnp.where(upper, tile - half, tile)
        found = jnp.zeros((8, LANES), F32)
        for t in range(half):
            found = jnp.where(tile == t, jnp.take_along_axis(source[t], lane, axis=1), found)
        result = jnp.where(upper[:4], found[4:], found[:4])
        value_ref[pl.ds(o, 1), :] = result[:1]
        force_ref[:, place_of(o)] = -result[1:]

    at_once = 8 if chunks % 8 == 0 else 1

    def some(i, carry):
        for u in range(at_once):
            one(i * at_once + u)
        return carry

    lax.fori_loop(0, chunks // at_once, some, 0)


def tables():
    def halves(value):
        value = value.astype(np.float32)
        high = value.astype(BF16)
        return high, (value - high.astype(np.float32)).astype(BF16)

    full = np.arange(N)
    line = (full - 1) % N

    def table(rows, columns):
        angle = (rows[:, None] * columns[None, :] % N) * (2.0 * np.pi / N)
        return np.cos(angle) + np.sin(angle)

    high, low = halves(table(full, full))
    left = np.concatenate([high, low, high], axis=1)
    high, low = halves(table(line, full))
    lines = np.concatenate([high, high, low], axis=0)
    high, low = halves(table(full, line))
    symbols = (2 * np.sin(np.pi * full / N)) ** 2
    total = symbols[:, None] + symbols[None, :]
    shares = np.stack([total, np.exp(-0.5 * total) / float(N * N * N)]).astype(np.float32)
    return left, lines, np.concatenate([high, high, low], axis=0), shares


def symbol(index, size):
    sines = 2.0 * jnp.sin(jnp.pi * index.astype(F32) / size)
    return sines * sines


def exchange(value, axis, distance, flip):
    size = lax.axis_size(axis)
    pairs = [(i, i ^ distance if flip else (i + distance) % size) for i in range(size)]
    return lax.ppermute(value, axis, pairs)


def gather_x(value):
    size = lax.axis_size("gx")
    if size > 8:
        return lax.all_gather(value, "gx")
    me = lax.axis_index("gx")
    parts = jnp.stack([value] + [exchange(value, "gx", s, False) for s in range(1, size)])
    return parts[(me - jnp.arange(size)) % size] if size > 1 else parts


def scatter_x(value):
    size = lax.axis_size("gx")
    if size > 8:
        return [jnp.sum(lax.all_to_all(value, "gx", split_axis=0, concat_axis=0, tiled=True), axis=0)]
    me = lax.axis_index("gx")
    parts = [lax.dynamic_index_in_dim(value, me, 0, keepdims=False)]
    for s in range(1, size):
        part = lax.dynamic_index_in_dim(value, (me + s) % size, 0, keepdims=False)
        parts.append(exchange(part, "gx", s, False))
    return parts


def shards(cell_x, cell_y, cell_z, fraction, charge):
    count = charge.shape[0]
    n_x, n_y = lax.axis_size("gx"), lax.axis_size("gy")
    at_x, at_y = lax.axis_index("gx"), lax.axis_index("gy")
    planes_x = N // n_x
    assert 2 * (N // n_y) == LANES
    own = N // (n_x * n_y)
    chunks = count // LANES
    place = jnp.arange(count, dtype=jnp.int32)

    key, cy, cz, fx, fy, fz, q, order = lax.sort(
        (cell_x, cell_y, cell_z, fraction[0], fraction[1], fraction[2], charge, place),
        num_keys=1,
        is_stable=False,
    )
    plane = (key + at_x * planes_x).astype(F32)
    sent = [plane, cy.astype(F32), cz.astype(F32), fx, fy, fz, q]
    packed = jnp.concatenate([v.reshape(chunks, LANES) for v in sent])

    freq = (at_x * n_y + at_y) * own + jnp.arange(ROWS, dtype=jnp.int32)
    angle = freq.astype(F32) * F32(np.pi / N)
    far_cos, near_cos = jnp.cos(3 * angle), jnp.cos(angle)
    far_sin, near_sin = jnp.sin(3 * angle), jnp.sin(angle)
    along_own = symbol(freq, N)
    tab = [
        (far_cos + 23 * near_cos) * F32(1 / 24),
        (far_cos - near_cos) * F32(1 / 2),
        (far_sin + 5 * near_sin) * F32(1 / 4),
        far_sin * F32(1 / 3) - near_sin,
        far_cos - near_cos,
        far_sin - 3 * near_sin,
        (freq % 2).astype(F32),
        along_own,
        jnp.exp(-0.5 * along_own),
    ]
    tab = [jnp.broadcast_to(t[:, None], (ROWS, LANES)) for t in tab]
    cells = 2 * jnp.arange(LANES, dtype=jnp.int32) + 1
    turns = (freq[:, None] * cells[None, :] % (2 * N)).astype(F32) * F32(np.pi / N)
    turn_cos, turn_sin = jnp.cos(turns), jnp.sin(turns)
    tab = jnp.stack([turn_cos + turn_sin] + tab[:6] + [turn_cos - turn_sin] + tab[6:])
    tab = jnp.where((jnp.arange(ROWS) < own)[None, :, None], tab, F32(0.0))

    half = n_y // 2
    _, rank = lax.sort((order, place), num_keys=1, is_stable=False)
    rank = rank.reshape(chunks, LANES)
    arrived, tab, rank = lax.optimization_barrier((gather_x(packed), tab, rank))
    groups = [arrived]
    for s in range(1, half + 1):
        step = s & -s
        groups.append(exchange(groups[s ^ step], "gy", step, True))

    unroll = 16 if chunks % 16 == 0 else 1
    longer = 32 if chunks % 32 == 0 else unroll
    size = N + PAD
    steps = half * n_x
    at_once = 8 if own % 8 == 0 else 1
    turns = own // at_once
    params = pltpu.CompilerParams(vmem_limit_bytes=56 * 1024 * 1024)

    def bounds(some):
        planes = jnp.concatenate([g[:, :chunks] for g in some]).astype(jnp.int32)
        return planes[:, :, 0], planes[:, :, -1]

    def clamp(step, top):
        return jnp.minimum(jnp.maximum(step, 0), top)

    def charges(begins):
        def spec(g):
            def place(t, *_):
                at = 0
                for begin in begins:
                    at = jnp.where(t >= begin, clamp(t - begin - g * n_x, n_x - 1), at)
                return (at, 0, 0)

            return pl.BlockSpec((1, FIELDS * chunks, LANES), place)

        return [spec(g) for g in range(half)]

    def whole(*shape):
        return pl.BlockSpec(shape, lambda *_: (0,) * len(shape))

    def results(begin):
        def spec(g):
            return pl.BlockSpec(
                (1, 4, count), lambda t, *_: (clamp(t - begin - g * n_x, n_x - 1), 0, 0)
            )

        return [spec(g) for g in range(half)]

    def estimate(passes):
        return pl.CostEstimate(
            flops=passes * steps * count * 600000,
            bytes_accessed=passes * steps * count * 160,
            transcendentals=0,
        )

    tab_spec = whole(TABLES, ROWS, LANES)
    mesh_shape = (half, size, ROWS, LANES)
    sums_shape = [jax.ShapeDtypeStruct((n_x, 4, count), F32)] * half
    sums_scratch = pltpu.VMEM((4, count), F32)
    near = groups[:half]
    near_bounds = bounds(near)

    kept_spec = pl.BlockSpec((1, KEPT, count), lambda t, *_: (t, 0, 0))
    kept_shape = jax.ShapeDtypeStruct((steps, KEPT, count), F32)
    near_mesh, near_kept = pl.pallas_call(
        functools.partial(near_kernel, longer, chunks, n_x),
        grid_spec=pltpu.PrefetchScalarGridSpec(
            num_scalar_prefetch=2,
            grid=(steps,),
            in_specs=[tab_spec] + charges([0]),
            out_specs=[
                pl.BlockSpec((1, size, ROWS, LANES), lambda t, *_: (t // n_x, 0, 0, 0)),
                kept_spec,
            ],
        ),
        out_shape=[jax.ShapeDtypeStruct(mesh_shape, F32), kept_shape],
        compiler_params=params,
        cost_estimate=estimate(1),
        name="near_spread",
    )(*near_bounds, tab, *near)

    near_mesh, arrived = lax.optimization_barrier((near_mesh, groups[half]))
    far = [arrived]
    for s in range(1, half):
        step = s & -s
        far.append(exchange(far[s ^ step], "gy", step, True))
    far_bounds = bounds(far)

    packs = steps + turns
    samples = packs + 1 + half
    keep = steps <= 8
    near_field, *far_sums = pl.pallas_call(
        functools.partial(far_kernel, longer, unroll, chunks, n_x, at_once, turns),
        grid_spec=pltpu.PrefetchScalarGridSpec(
            num_scalar_prefetch=3,
            grid=(samples + steps,),
            in_specs=[tab_spec]
            + charges([0] if keep else [0, samples])
            + [
                pl.BlockSpec(memory_space=pl.ANY),
                whole(N, 3 * N),
                whole(3 * N, N),
                whole(3 * N, N),
                whole(2, N, N),
            ],
            out_specs=[
                pl.BlockSpec(
                    (1, size * ROWS, N), lambda t, *_: (clamp(t - packs - 1, half - 1), 0, 0)
                ),
            ]
            + results(samples),
            scratch_shapes=[
                pltpu.VMEM((n_y, size, ROWS, LANES), F32),
                pltpu.VMEM((half, size, ROWS, N), BF16),
                sums_scratch,
                pltpu.VMEM((steps if keep else 1, KEPT, count), F32),
                pltpu.SemaphoreType.DMA((half,)),
            ],
        ),
        out_shape=[jax.ShapeDtypeStruct((half, size * ROWS, N), BF16)] + sums_shape,
        compiler_params=params,
        cost_estimate=estimate(3),
        name="far_spread_filter_sample",
    )(
        *far_bounds,
        at_y[None],
        tab,
        *far,
        near_mesh,
        *tables(),
    )

    *far_sums, near_field = lax.optimization_barrier((*far_sums, near_field))
    far_sums = [exchange(v, "gy", half, True) for v in far_sums]
    near_sums = pl.pallas_call(
        functools.partial(last_kernel, unroll, chunks, n_x),
        grid_spec=pltpu.PrefetchScalarGridSpec(
            num_scalar_prefetch=2,
            grid=(steps,),
            in_specs=[
                kept_spec,
                pl.BlockSpec((1, size, ROWS, N), lambda t, *_: (t // n_x, 0, 0, 0)),
            ],
            out_specs=results(0),
            scratch_shapes=[sums_scratch],
        ),
        out_shape=sums_shape,
        compiler_params=params,
        cost_estimate=estimate(1),
        name="near_sample",
    )(*near_bounds, near_kept, near_field.reshape(half, size, ROWS, N))

    sums = [near_sums[s] + far_sums[s] for s in range(half)]
    for s in range(half - 1, 0, -1):
        step = s & -s
        sums[s ^ step] = sums[s ^ step] + exchange(sums[s], "gy", step, True)
    parts = scatter_x(sums[0])
    value, forces = pl.pallas_call(
        order_kernel,
        out_shape=[
            jax.ShapeDtypeStruct((chunks, LANES), F32),
            jax.ShapeDtypeStruct((3, count), F32),
        ],
        scratch_shapes=[pltpu.VMEM((chunks // 2, 8, LANES), F32)],
        compiler_params=params,
        name="order",
    )(rank, *parts)
    return (value.reshape(count), forces)


def solution(mesh):
    placed = P(("parts", "gx", "gy"))
    return jax.shard_map(
        shards,
        mesh=mesh,
        in_specs=(placed, placed, placed, P(None, ("parts", "gx", "gy")), placed),
        out_specs=(placed, P(None, ("parts", "gx", "gy"))),
        check_vma=False,
    )
```
